256 devices in a mesh: region: 8 (over x, core), dev: 32 (over y, z).
Axes of the slice: x: 4, y: 4, z: 8, core: 2. Of those that a mesh axis runs over, the one named last changes fastest.
Arguments:
- inputs: bfloat16 [49152, 128], P(('region', 'dev')), may hold values from -6 to 6
- responses: bfloat16 [49152], P(('region', 'dev')), may hold values from -6 to 6
- point_slot: int32 [49152], P(('region', 'dev')), may hold values from 0 to 191, as said below
- block_home: int32 [512], replicated, may hold values from 0 to 511, as said below
- nbr_ids: int32 [512, 4], P(('region', 'dev')), may hold values from 0 to 511, as said below
- nbr_count: int32 [512], P(('region', 'dev')), may hold values from 0 to 4, as said below
- w_in: bfloat16 [128, 128], replicated, may hold values from -0.5 to 0.5
- b_in: float32 [128], replicated, may hold values from -3 to 3
- w_out: bfloat16 [128, 128], replicated, may hold values from -0.5 to 0.5
- kernel_params: float32 [3], replicated, may hold values from -1.61 to 2.49, as said below
Outputs:
- block_loglik: float32 [512], P(('region', 'dev'))
- feature_grad: float32 [49152, 128], P(('region', 'dev'))
- grad_w_in: float32 [128, 128], replicated
- grad_b_in: float32 [128], replicated
- grad_w_out: float32 [128, 128], replicated
- grad_kernel: float32 [3], replicated
The draws below stay inside these ranges and needn't reach their ends.
Inputs may be any that keep to these rules, and one draw needn't show every extreme that they name: `point_slot`: on each device, a permutation of 0 to 2 * 96 - 1 over that device's points. A permutation: block id b is stored in slot block_home[b], on device block_home[b] // 2 in the order region then dev. `nbr_ids`: the first nbr_count[s] entries of row s are distinct ids of blocks whose slots lie in 2 * (s // 2) - 6 to s - 1; the other entries are 0. `nbr_count`: slot 0 has 0; the last slot has 4. `kernel_params`: entry 0 within log(7) to log(12), entry 1 within log(0.5) to log(2), entry 2 within log(0.2) to log(0.6).
All inputs are finite; a program needn't handle non-finite values.
Results may differ from the reference program's by a relative error of at most 0.0097.
Values may be sent and summed in bfloat16 or wider, within the bound.
A program may use at most 64 MiB of HBM per device.

```python
import math
from functools import partial
import jax
import jax.numpy as jnp
from jax import lax

F_IN = 128
H = 128
BS = 96
BPD = 2
NMAX = 4
WIN = 3
NBLK = 512
POINTS = 49152


def window_tables(key):
    home = jax.random.permutation(jax.random.fold_in(key, 11), NBLK).astype(jnp.int32)
    id_of_slot = jnp.zeros((NBLK,), jnp.int32).at[home].set(jnp.arange(NBLK, dtype=jnp.int32))
    span = WIN * BPD + BPD - 1
    slots = jnp.arange(NBLK, dtype=jnp.int32)
    offsets = jnp.arange(1, span + 1, dtype=jnp.int32)
    avail = jnp.minimum(WIN * BPD + slots % BPD, slots)
    scores = jax.random.randint(jax.random.fold_in(key, 12), (NBLK, span), 0, 1 << 20) * span + (offsets - 1)[None, :]
    scores = jnp.where(offsets[None, :] <= avail[:, None], scores, scores + (1 << 29))
    picked = jnp.argsort(scores, axis=1, stable=True)[:, :NMAX].astype(jnp.int32) + 1
    raw_count = jax.random.randint(jax.random.fold_in(key, 13), (NBLK,), 1, NMAX + 1)
    raw_count = jnp.where(slots == NBLK - 1, NMAX, raw_count)
    count = jnp.minimum(raw_count, avail).astype(jnp.int32)
    source = jnp.clip(slots[:, None] - picked, 0, NBLK - 1)
    live = jnp.arange(NMAX, dtype=jnp.int32)[None, :] < count[:, None]
    ids = jnp.where(live, id_of_slot[source], 0).astype(jnp.int32)
    return (home, ids, count)


def draw_block_home(key, part):
    home, ids, count = window_tables(key)
    return home


def draw_nbr_ids(key, part):
    home, ids, count = window_tables(key)
    return ids


def draw_nbr_count(key, part):
    home, ids, count = window_tables(key)
    return count


def one_perm(sub_key):
    return jax.random.permutation(sub_key, BPD * BS)


def draw_point_slot(key, part):
    key = jax.random.fold_in(key, 21)
    sub_keys = jax.random.split(key, NBLK // BPD)
    return jax.vmap(one_perm)(sub_keys).reshape(-1).astype(jnp.int32)


def draw_kernel_params(key, part):
    key = jax.random.fold_in(key, 31)
    unit = jax.random.uniform(key, (3,), jnp.float32)
    lower = jnp.array([math.log(7.0), math.log(0.5), math.log(0.2)], jnp.float32)
    upper = jnp.array([math.log(12.0), math.log(2.0), math.log(0.6)], jnp.float32)
    return lower + unit * (upper - lower)


def level_of(stream_key, shape, pieces, least, largest):
    def one(dim, blocks):
        heights = jax.random.uniform(jax.random.fold_in(jax.random.fold_in(stream_key, 6), dim), (blocks,), jnp.float32, least / len(pieces), largest / len(pieces))
        return jnp.repeat(jnp.exp(heights), shape[dim] // blocks).reshape((-1,) + (1,) * (len(shape) - dim - 1))

    loudness = one(*pieces[0])
    for cut in pieces[1:]:
        loudness = loudness * one(*cut)
    return loudness


def noise(rng, dims, deviation, most, pieces=(), kind=jnp.bfloat16):
    gain = level_of(rng, dims, pieces, -0.22, 0.18) if pieces else 1.0
    entries = jax.random.normal(rng, dims, jnp.float32) * deviation * gain
    return jnp.minimum(jnp.maximum(entries, -most), most).astype(kind)


def setup_inputs(seed: int = 0) -> dict:
    key_list = jax.random.split(jax.random.key(seed), 11)
    inputs = noise(key_list[0], (POINTS, F_IN), 1.0, 6.0, ((0, 256),))
    responses = noise(key_list[1], (POINTS,), 1.0, 6.0, ((0, 256),))
    point_slot = draw_point_slot(jax.random.fold_in(key_list[10], 71), 0)
    block_home = draw_block_home(jax.random.fold_in(key_list[10], 71), 0)
    nbr_ids = draw_nbr_ids(jax.random.fold_in(key_list[10], 71), 0)
    nbr_count = draw_nbr_count(jax.random.fold_in(key_list[10], 71), 0)
    w_in = noise(key_list[6], (F_IN, H), F_IN ** -0.5, 0.5)
    b_in = noise(key_list[7], (H,), 0.5, 3.0, (), jnp.float32)
    w_out = noise(key_list[8], (H, H), H ** -0.5, 0.5)
    kernel_params = draw_kernel_params(jax.random.fold_in(key_list[10], 71), 0)
    return {"inputs": inputs, "responses": responses, "point_slot": point_slot, "block_home": block_home, "nbr_ids": nbr_ids, "nbr_count": nbr_count, "w_in": w_in, "b_in": b_in, "w_out": w_out, "kernel_params": kernel_params}


SQRT_THREE = math.sqrt(3.0)
LOG_TWO_PI = math.log(2.0 * math.pi)

def block_loglik(resp_joint, valid_rows, joint_rows, params):
    own_rows = joint_rows.shape[0] // (NMAX + 1)
    inv_sq = jnp.exp(-2.0 * params[0])
    variance = jnp.exp(params[1])
    nugget = jnp.exp(params[2])
    sq_norm = lax.optimization_barrier(jnp.sum(joint_rows * joint_rows, axis=1))
    gram = jnp.dot(joint_rows, joint_rows.T, precision=lax.Precision.HIGHEST)
    dist = jnp.maximum(sq_norm[:, None] + sq_norm[None, :] - 2.0 * gram, 0.0)
    radius = jnp.sqrt(dist * inv_sq + 1e-06)
    kern = variance * (1.0 + SQRT_THREE * radius) * jnp.exp(-SQRT_THREE * radius)
    kmat = kern * valid_rows[:, None] * valid_rows[None, :] + jnp.diag(nugget * valid_rows + 1.0 - valid_rows)
    factor = jnp.linalg.cholesky(kmat)
    white = lax.linalg.triangular_solve(factor, (resp_joint * valid_rows)[:, None], left_side=True, lower=True)
    tail = white[-own_rows:, 0]
    diag_tail = jnp.diagonal(factor)[-own_rows:]
    return -0.5 * jnp.sum(tail * tail) - jnp.sum(jnp.log(diag_tail)) - 0.5 * own_rows * LOG_TWO_PI

def reference(inputs, responses, point_slot, block_home, nbr_ids, nbr_count, w_in, b_in, w_out, kernel_params):
    pre = jnp.dot(inputs.astype(jnp.float32), w_in.astype(jnp.float32), preferred_element_type=jnp.float32) + b_in
    hidden = jax.nn.silu(pre).astype(jnp.bfloat16)
    features = jnp.dot(hidden.astype(jnp.float32), w_out.astype(jnp.float32), preferred_element_type=jnp.float32).astype(jnp.bfloat16)
    per_dev = BPD * BS
    position = (jnp.arange(POINTS, dtype=jnp.int32) // per_dev * per_dev + point_slot).astype(jnp.int32)
    feat_blocks = jnp.zeros((POINTS, H), jnp.bfloat16).at[position].set(features).reshape(NBLK, BS, H)
    resp_blocks = jnp.zeros((POINTS,), jnp.bfloat16).at[position].set(responses).reshape(NBLK, BS)

    def step(carry, slot):
        grad_acc, hyper_acc = carry
        valid_nb = jnp.arange(NMAX, dtype=jnp.int32) < nbr_count[slot]
        nb_slots = jnp.where(valid_nb, block_home[nbr_ids[slot]], 0).astype(jnp.int32)
        slots = jnp.concatenate([nb_slots, slot[None].astype(jnp.int32)])
        member_mask = jnp.concatenate([valid_nb, jnp.ones((1,), bool)]).astype(jnp.float32)
        joint_rows = (feat_blocks[slots].astype(jnp.float32) * member_mask[:, None, None]).reshape(-1, H)
        resp_joint = resp_blocks[slots].astype(jnp.float32).reshape(-1)
        valid_rows = jnp.repeat(member_mask, BS)
        loglik, pull = jax.vjp(partial(block_loglik, resp_joint, valid_rows), joint_rows, kernel_params)
        grad_joint, grad_par = pull(jnp.ones((), jnp.float32))
        grad_joint = grad_joint.reshape(NMAX + 1, BS, H) * member_mask[:, None, None]
        return ((grad_acc.at[slots].add(grad_joint), hyper_acc + grad_par), loglik)
    start = (jnp.zeros((NBLK, BS, H), jnp.float32), jnp.zeros((3,), jnp.float32))
    (grad_acc, hyper_acc), logliks = lax.scan(step, start, jnp.arange(NBLK, dtype=jnp.int32))
    feature_grad = grad_acc.reshape(POINTS, H)[position]
    scale = 1.0 / (NBLK * BS)
    grad_w_out = jnp.dot(hidden.astype(jnp.float32).T, feature_grad, precision=lax.Precision.HIGHEST) * scale
    back_hidden = jnp.dot(feature_grad, w_out.astype(jnp.float32).T, precision=lax.Precision.HIGHEST)
    sigma = jax.nn.sigmoid(pre)
    dpre = back_hidden * sigma * (1.0 + pre * (1.0 - sigma))
    grad_w_in = jnp.dot(inputs.astype(jnp.float32).T, dpre, precision=lax.Precision.HIGHEST) * scale
    grad_b_in = lax.optimization_barrier(jnp.sum(dpre, axis=0)) * scale
    return (logliks / BS, feature_grad, grad_w_in, grad_b_in, grad_w_out, hyper_acc * scale)
```

```python
import math

import jax
import jax.numpy as jnp
from jax import lax
from jax.experimental import pallas as pl
from jax.experimental.pallas import tpu as pltpu
from jax.sharding import PartitionSpec as P

H = 128
BS = 96
BPD = 2
NMAX = 4
WIN = 3
ROWS = BPD * BS
B = 128
N = 4 * B
STEPS = 7

SQRT_THREE = math.sqrt(3.0)
LOG_TWO_PI = math.log(2.0 * math.pi)
MESH = pl.DeviceIdType.MESH
F32 = jnp.float32
BF16 = jnp.bfloat16


def dot(a, b, contract=((1,), (0,))):
    return lax.dot_general(a, b, (contract, ((), ())), preferred_element_type=F32)


NT = ((1,), (1,))
TN = ((0,), (0,))


def split2(a):
    hi = a.astype(BF16)
    return hi, (a - hi.astype(F32)).astype(BF16)


def split3(a):
    hi = a.astype(BF16)
    rest = a - hi.astype(F32)
    mid = rest.astype(BF16)
    return hi, mid, (rest - mid.astype(F32)).astype(BF16)


def wide(parts, cols):
    row = jnp.concatenate(parts, axis=1)
    return jnp.concatenate([row, row], axis=0)


def mul2(a, b):
    n = b.shape[1]
    out = dot(jnp.concatenate(split2(a), axis=1), wide(split2(b), n))
    return out[:, :n] + out[:, n:]


def mul3(a, b):
    n = b.shape[1]
    ah, am, al = split3(a)
    bh, bm, bl = split3(b)
    out = dot(jnp.concatenate([ah, am], axis=1), wide((bh, bm), n))
    low = dot(jnp.concatenate([ah, al], axis=1), jnp.concatenate([bl, bh], axis=0))
    return out[:, :n] + (out[:, n:] + low)


def eye_of(n):
    return (
        lax.broadcasted_iota(jnp.int32, (n, n), 0) == lax.broadcasted_iota(jnp.int32, (n, n), 1)
    ).astype(F32)


def inverses(mats, eye, coef, scales):
    res = [eye - coef * a for a in mats]
    inv = [(scales[0] * coef) * (eye + r) for r in res]
    res = [(1.0 - scales[0]) * eye + scales[0] * mul2(r, r) for r in res]
    for j in range(1, STEPS):
        s = scales[j]
        if j < STEPS - 1:
            both = [mul2(jnp.concatenate([x, r], axis=0), r) for x, r in zip(inv, res)]
            inv = [s * (x + b[:B]) for x, b in zip(inv, both)]
            res = [(1.0 - s) * eye + s * b[B:] for b in both]
        else:
            inv = [s * (x + mul2(x, r)) for x, r in zip(inv, res)]
    left = [eye - mul3(a, x) for a, x in zip(mats, inv)]
    return [x + mul2(x, t) for x, t in zip(inv, left)]


def device(index):
    per = lax.axis_size("dev")
    return (index // per, index % per)


def my_index():
    return lax.axis_index("region") * lax.axis_size("dev") + lax.axis_index("dev")


def network(x, w_in, b_in, w_out):
    pre = dot(x, w_in) + b_in
    sig = 1.0 / (1.0 + jnp.exp(-pre))
    hidden = (pre * sig).astype(BF16)
    return pre, sig, hidden


def one_hot(point_slot, rows, first):
    slot = lax.broadcasted_iota(jnp.int32, (rows, ROWS), 0) + first
    return (slot == point_slot).astype(F32).astype(BF16)


def send_kernel(x_ref, resp_ref, ps_ref, w_in_ref, b_ref, w_out_ref, win_ref, send_sem, recv_sem):
    total = lax.axis_size("region") * lax.axis_size("dev")
    me = my_index()
    barrier = pltpu.get_barrier_semaphore()
    for k in range(1, WIN + 1):
        pl.semaphore_signal(
            barrier, inc=1, device_id=device(lax.rem(me + total - k, total)), device_id_type=MESH
        )
    _, _, hidden = network(x_ref[...], w_in_ref[...], b_ref[...], w_out_ref[...])
    feats = dot(hidden, w_out_ref[...]).astype(BF16)
    point_slot = ps_ref[...]
    win_ref[0, :ROWS, :] = dot(one_hot(point_slot, ROWS, 0), feats).astype(BF16)
    resp = jnp.broadcast_to(resp_ref[...].astype(F32), (16, ROWS)).astype(BF16)
    first = dot(resp, one_hot(point_slot, B, 0), NT)
    second = dot(resp, one_hot(point_slot, B, BS), NT)
    half = lax.broadcasted_iota(jnp.int32, (16, B), 0) < 8
    win_ref[0, ROWS:, :] = jnp.where(half, first, second).astype(BF16)
    pl.semaphore_wait(barrier, WIN)
    copies = []
    for k in range(1, WIN + 1):
        copies.append(
            pltpu.make_async_remote_copy(
                src_ref=win_ref.at[0],
                dst_ref=win_ref.at[k],
                send_sem=send_sem.at[k - 1],
                recv_sem=recv_sem.at[k - 1],
                device_id=device(lax.rem(me + k, total)),
                device_id_type=MESH,
            )
        )
        copies[-1].start()
    for c in copies:
        c.wait()


def block_kernel(
    home_ref, ids_ref, cnt_ref, par_ref, win_ref, ll_ref, hyp_ref, gw_ref, z_ref, e_ref, k_ref
):
    me = my_index()

    def const(x):
        return jnp.full((1, 1), x, F32)

    inv_sq = jnp.exp(-2.0 * const(par_ref[0]))
    var = jnp.exp(const(par_ref[1]))
    nug = jnp.exp(const(par_ref[2]))
    eye = eye_of(B)
    lane = lax.broadcasted_iota(jnp.int32, (B, B), 1)
    sub = lax.broadcasted_iota(jnp.int32, (B, B), 0)
    pick = (lane == BS).astype(F32).astype(BF16)

    top = B * var + 1.0
    coef = 2.0 / (top + nug)
    delta = (top - nug) / (top + nug)
    scales = []
    for _ in range(STEPS):
        sq = delta * delta
        scales.append(2.0 / (2.0 - sq))
        delta = sq / (2.0 - sq)

    wins = []
    for s in range(BPD):
        count = cnt_ref[s]
        row_wins = []
        resp_rows = []
        for k in range(NMAX + 1):
            if k < NMAX:
                slot = home_ref[ids_ref[s, k]]
                live = k < count
                w = jnp.where(live, (me - slot // BPD) * BPD + slot % BPD, 0)
                w = jnp.clip(w, 0, (WIN + 1) * BPD - 1)
                flag = jnp.where(live, 1.0, 0.0)
            else:
                w = jnp.int32(s)
                flag = jnp.float32(1.0)
            row_wins.append(w)
            member = win_ref[w // BPD, pl.ds(pl.multiple_of((w % BPD) * BS, BS), BS), :]
            z_ref[s, k * BS : (k + 1) * BS, :] = (member.astype(F32) * flag).astype(BF16)
            tile = win_ref[w // BPD, ROWS : ROWS + 16, :].astype(F32)
            resp = jnp.where(w % BPD == 0, tile[0:1], tile[8:9]) * flag
            resp_rows.append(jnp.where(eye[:BS] > 0.0, resp, 0.0).astype(BF16))
        z_ref[s, (NMAX + 1) * BS :, :] = jnp.zeros((N - (NMAX + 1) * BS, B), BF16)
        resp_rows.append(jnp.zeros((N - (NMAX + 1) * BS, B), BF16))
        wins.append(row_wins)
        resp_col = dot(jnp.concatenate(resp_rows, axis=0), pick)

        z = z_ref[s]
        gram = dot(z, z, NT)
        diag = [jnp.where(eye > 0.0, gram[i * B : (i + 1) * B, i * B : (i + 1) * B], 0.0) for i in range(4)]
        sq_row = jnp.concatenate([jnp.sum(d, axis=0, keepdims=True) for d in diag], axis=1)
        col_id = lax.broadcasted_iota(jnp.int32, (1, N), 1)
        own = (col_id >= NMAX * BS) & (col_id < (NMAX + 1) * BS)
        v_row = jnp.where((col_id < count * BS) | own, 1.0, 0.0)
        for i in range(4):
            rows = slice(i * B, (i + 1) * B)
            row_id = lax.broadcasted_iota(jnp.int32, (B, 1), 0) + i * B
            own_c = (row_id >= NMAX * BS) & (row_id < (NMAX + 1) * BS)
            v_col = jnp.where((row_id < count * BS) | own_c, 1.0, 0.0)
            sq_col = jnp.sum(diag[i], axis=1, keepdims=True)
            for c in range(0, B, 32):
                part = slice(c, c + 32)
                d2 = jnp.maximum(sq_col[part] + sq_row - 2.0 * gram[i * B + c : i * B + c + 32], 0.0)
                r2 = d2 * inv_sq + 1e-06
                rad = SQRT_THREE * (r2 * lax.rsqrt(r2))
                e = jnp.exp(-rad) * (v_col[part] * v_row)
                e_ref[s, i * B + c : i * B + c + 32, :] = e
                on = lax.broadcasted_iota(jnp.int32, (32, N), 0) + (i * B + c) == lax.broadcasted_iota(
                    jnp.int32, (32, N), 1
                )
                k = var * (1.0 + rad) * e + jnp.where(on, nug * v_col[part] + 1.0 - v_col[part], 0.0)
                k_ref[s, i * B + c : i * B + c + 32, :] = k
            k_ref[s, rows, 3 * B :] = k_ref[s, rows, 3 * B :] + resp_col[rows]

    both = range(BPD)
    invs = []
    for i in range(3):
        lo = (i + 1) * B
        rows = slice(i * B, lo)
        cur = inverses([k_ref[s, rows, rows] for s in both], eye, coef, scales)
        invs.append(cur)
        for s in both:
            panel = mul3(k_ref[s, lo:, rows], cur[s])
            k_ref[s, lo:, lo:] = k_ref[s, lo:, lo:] - mul3(panel, k_ref[s, rows, lo:])
    real = (lane < BS) & (sub < BS)
    resid = [jnp.where((sub < BS) & (lane == BS), k_ref[s, 3 * B :, 3 * B :], 0.0) for s in both]
    schur = [jnp.where(real, k_ref[s, 3 * B :, 3 * B :], eye) for s in both]
    s_inv = inverses(schur, eye, coef, scales)

    hyper = jnp.zeros((1, B), F32)
    lane1 = lax.broadcasted_iota(jnp.int32, (1, B), 1)
    gw_ref[...] = jnp.zeros_like(gw_ref)
    for s in both:
        x3 = mul3(invs[2][s], k_ref[s, 2 * B : 3 * B, 3 * B :])
        x2 = mul3(invs[1][s], k_ref[s, B : 2 * B, 3 * B :] - mul3(k_ref[s, B : 2 * B, 2 * B : 3 * B], x3))
        t1 = k_ref[s, :B, 3 * B :] - mul3(k_ref[s, :B, B : 2 * B], x2) - mul3(k_ref[s, :B, 2 * B : 3 * B], x3)
        x1 = mul3(invs[0][s], t1)
        beta = mul3(s_inv[s], resid[s])
        beta_t = beta.T
        beta_col = jnp.sum(beta, axis=1, keepdims=True)
        beta_row = jnp.sum(beta_t, axis=0, keepdims=True)
        mid = jnp.where(real, beta_col * beta_row - s_inv[s], 0.0) + beta + beta_t
        quad = jnp.sum(jnp.sum(resid[s] * beta, axis=0, keepdims=True), axis=1, keepdims=True)
        left_n = jnp.concatenate([x1, x2, x3], axis=0) * jnp.where(lane1 < BS, -1.0, 1.0)
        left_o = jnp.where(real, eye, 0.0)
        prod = mul2(jnp.concatenate([left_n, left_o], axis=0), mid)
        trace = jnp.sum(
            jnp.sum(prod[: 3 * B] * left_n, axis=0, keepdims=True)
            + jnp.sum(prod[3 * B :] * left_o, axis=0, keepdims=True),
            axis=1,
            keepdims=True,
        )
        t2 = 0.5 * nug * trace
        t1_ = 0.5 * quad - 0.5 * BS - t2
        ph, plo = split2(prod)
        lh, llo = split2(left_n)
        g_n = dot(
            jnp.concatenate([ph, plo], axis=1), jnp.concatenate([lh, lh], axis=1), NT
        ) + dot(ph, llo, NT)
        for i in range(4):
            rows = slice(i * B, (i + 1) * B)
            k_ref[s, rows, : 3 * B] = g_n[rows] * e_ref[s, rows, : 3 * B]
            k_ref[s, rows, 3 * B :] = jnp.where(lane < BS, prod[rows], 0.0) * e_ref[s, rows, 3 * B :]
        z = z_ref[s]
        rhs = jnp.concatenate([z, jnp.ones_like(z)], axis=1)
        hi, low = split2(k_ref[s])
        pz = dot(hi, rhs) + dot(low, rhs)
        zf = z.astype(F32)
        grad = (3.0 * var * inv_sq) * (pz[:, :B] - pz[:, B:] * zf)
        t0 = -jnp.sum(jnp.sum(grad * zf, axis=0, keepdims=True), axis=1, keepdims=True)
        hyper = hyper + jnp.where(lane1 == 0, t0, 0.0) + jnp.where(lane1 == 1, t1_, 0.0)
        hyper = hyper + jnp.where(lane1 == 2, t2, 0.0)
        for k in range(NMAX + 1):
            w = wins[s][k]
            gw_ref[w] = gw_ref[w] + grad[k * BS : (k + 1) * BS]

        mat = schur[s][:BS]
        logdet = jnp.zeros((1, 1), F32)
        for k in range(BS):
            base = (k // 8) * 8
            row = mat[k - (BS - mat.shape[0]) : k - (BS - mat.shape[0]) + 1]
            pivot = row[:, k : k + 1]
            logdet = logdet + jnp.log(pivot)
            if k < BS - 1:
                if (k + 1) % 8 == 0:
                    col = mat[8:, k : k + 1]
                    mat = mat[8:] - col * (row / pivot)
                else:
                    mat = mat - mat[:, k : k + 1] * (row / pivot)
        ll = (-0.5 * quad - 0.5 * logdet) * (1.0 / BS) - 0.5 * LOG_TWO_PI
        ll_ref[s] = jnp.sum(ll)
    hyp_ref[...] = jnp.broadcast_to(hyper, (8, B))


def reduce_kernel(
    x_ref, ps_ref, w_in_ref, b_ref, w_out_ref, gw_ref, hyp_ref,
    fg_ref, gwin_ref, gwout_ref, small_ref,
    out_buf, in_buf, part, part_in, red, red_in, gath,
    g_send, g_recv, s1, r1, s2, r2, s3, r3,
):
    total = lax.axis_size("region") * lax.axis_size("dev")
    region, dev = lax.axis_index("region"), lax.axis_index("dev")
    me = my_index()
    x, core, y, zz = region // 2, region % 2, dev // 8, dev % 8
    g1 = core * 8 + zz
    g2 = x * 4 + y

    def mate1(k):
        other = lax.rem(g1 + k, 16)
        return other, (x * 2 + other // 8, y * 8 + other % 8)

    def mate2(k):
        other = lax.rem(g2 + k, 16)
        return other, ((other // 4) * 2 + core, (other % 4) * 8 + zz)

    barrier = pltpu.get_barrier_semaphore()
    for k in range(1, WIN + 1):
        pl.semaphore_signal(barrier, inc=1, device_id=device(lax.rem(me + k, total)), device_id_type=MESH)
    for k in range(1, 16):
        pl.semaphore_signal(barrier, inc=1, device_id=mate1(k)[1], device_id_type=MESH)
        pl.semaphore_signal(barrier, inc=1, device_id=mate2(k)[1], device_id_type=MESH)
    for k in range(1, WIN + 1):
        out_buf[k - 1, :BS, :] = gw_ref[2 * k].astype(BF16)
        out_buf[k - 1, BS:, :] = gw_ref[2 * k + 1].astype(BF16)
    pl.semaphore_wait(barrier, WIN + 30)
    copies = []
    for k in range(1, WIN + 1):
        copies.append(
            pltpu.make_async_remote_copy(
                src_ref=out_buf.at[k - 1],
                dst_ref=in_buf.at[k - 1],
                send_sem=g_send.at[k - 1],
                recv_sem=g_recv.at[k - 1],
                device_id=device(lax.rem(me + total - k, total)),
                device_id_type=MESH,
            )
        )
        copies[-1].start()
    xs = x_ref[...]
    pre, sig, hidden = network(xs, w_in_ref[...], b_ref[...], w_out_ref[...])
    perm = one_hot(ps_ref[...], ROWS, 0)
    for c in copies:
        c.wait()
    grad = jnp.concatenate([gw_ref[0], gw_ref[1]], axis=0)
    for k in range(WIN):
        grad = grad + in_buf[k].astype(F32)
    hi, lo = split2(grad)
    both = dot(perm, jnp.concatenate([hi, lo], axis=1), TN)
    fg = both[:, :H] + both[:, H:]
    fg_ref[...] = fg
    hi, lo = split2(fg)
    back = dot(hi, w_out_ref[...], NT) + dot(lo, w_out_ref[...], NT)
    dpre = back * sig * (1.0 + pre * (1.0 - sig))
    w_out_part = dot(hidden, jnp.concatenate([hi, lo], axis=1), TN)
    w_out_part = w_out_part[:, :H] + w_out_part[:, H:]
    dhi, dlo = split2(dpre)
    w_in_part = dot(xs, jnp.concatenate([dhi, dlo], axis=1), TN)
    w_in_part = w_in_part[:, :H] + w_in_part[:, H:]
    row = lax.broadcasted_iota(jnp.int32, (8, H), 0)
    extra = jnp.where(row == 0, jnp.sum(dpre, axis=0, keepdims=True), 0.0)
    extra = jnp.where(row == 1, hyp_ref[...], extra)
    for c in range(16):
        src = w_in_part if c < 8 else w_out_part
        part[c, :16, :] = src[(c % 8) * 16 : (c % 8) * 16 + 16]
        part[c, 16:, :] = extra

    copies = []
    for k in range(1, 16):
        other, place = mate1(k)
        copies.append(
            pltpu.make_async_remote_copy(
                src_ref=part.at[other],
                dst_ref=part_in.at[g1],
                send_sem=s1.at[k],
                recv_sem=r1.at[k],
                device_id=place,
                device_id_type=MESH,
            )
        )
        copies[-1].start()
    part_in[g1] = part[g1]
    for c in copies:
        c.wait()
    acc = part_in[0]
    for c in range(1, 16):
        acc = acc + part_in[c]
    red[...] = acc

    copies = []
    for k in range(1, 16):
        _, place = mate2(k)
        copies.append(
            pltpu.make_async_remote_copy(
                src_ref=red,
                dst_ref=red_in.at[g2],
                send_sem=s2.at[k],
                recv_sem=r2.at[k],
                device_id=place,
                device_id_type=MESH,
            )
        )
        copies[-1].start()
    red_in[g2] = red[...]
    for c in copies:
        c.wait()
    acc = red_in[0]
    for c in range(1, 16):
        acc = acc + red_in[c]
    acc = acc * (1.0 / (total * ROWS))
    small_ref[...] = acc[16:]
    gath[g1] = acc[:16]
    copies = []
    for k in range(1, 16):
        _, place = mate1(k)
        copies.append(
            pltpu.make_async_remote_copy(
                src_ref=gath.at[g1],
                dst_ref=gath.at[g1],
                send_sem=s3.at[k],
                recv_sem=r3.at[k],
                device_id=place,
                device_id_type=MESH,
            )
        )
        copies[-1].start()
    for c in copies:
        c.wait()
    for c in range(8):
        gwin_ref[c * 16 : c * 16 + 16, :] = gath[c]
        gwout_ref[c * 16 : c * 16 + 16, :] = gath[8 + c]


VM = pl.BlockSpec(memory_space=pltpu.VMEM)
SM = pl.BlockSpec(memory_space=pltpu.SMEM)
DMA = pltpu.SemaphoreType.DMA


def shards(
    inputs, responses, point_slot, block_home, nbr_ids, nbr_count, w_in, b_in, w_out, kernel_params
):
    place_row = point_slot.reshape(1, ROWS)
    bias = b_in.reshape(1, H)
    window = pl.pallas_call(
        send_kernel,
        out_shape=jax.ShapeDtypeStruct((WIN + 1, ROWS + 16, H), BF16),
        in_specs=[VM] * 6,
        out_specs=VM,
        scratch_shapes=[DMA((WIN,)), DMA((WIN,))],
        compiler_params=pltpu.CompilerParams(collective_id=0, has_side_effects=True),
        name="send_features",
    )(inputs, responses.reshape(1, ROWS), place_row, w_in, bias, w_out)
    loglik, hyper, grads = pl.pallas_call(
        block_kernel,
        out_shape=(
            jax.ShapeDtypeStruct((BPD,), F32),
            jax.ShapeDtypeStruct((8, B), F32),
            jax.ShapeDtypeStruct(((WIN + 1) * BPD, BS, H), F32),
        ),
        in_specs=[SM] * 4 + [VM],
        out_specs=(SM, VM, VM),
        scratch_shapes=[
            pltpu.VMEM((BPD, N, H), BF16),
            pltpu.VMEM((BPD, N, N), F32),
            pltpu.VMEM((BPD, N, N), F32),
        ],
        compiler_params=pltpu.CompilerParams(vmem_limit_bytes=48 * 1024 * 1024),
        name="block_gradients",
    )(block_home, nbr_ids, nbr_count, kernel_params, window)
    feature_grad, g_in, g_out, small = pl.pallas_call(
        reduce_kernel,
        out_shape=(
            jax.ShapeDtypeStruct((ROWS, H), F32),
            jax.ShapeDtypeStruct((H, H), F32),
            jax.ShapeDtypeStruct((H, H), F32),
            jax.ShapeDtypeStruct((8, H), F32),
        ),
        in_specs=[VM] * 7,
        out_specs=(VM,) * 4,
        scratch_shapes=[
            pltpu.VMEM((WIN, ROWS, H), BF16),
            pltpu.VMEM((WIN, ROWS, H), BF16),
            pltpu.VMEM((16, 24, H), F32),
            pltpu.VMEM((16, 24, H), F32),
            pltpu.VMEM((24, H), F32),
            pltpu.VMEM((16, 24, H), F32),
            pltpu.VMEM((16, 16, H), F32),
            DMA((WIN,)),
            DMA((WIN,)),
        ]
        + [DMA((16,))] * 6,
        compiler_params=pltpu.CompilerParams(collective_id=1, has_side_effects=True),
        name="reduce_gradients",
    )(inputs, place_row, w_in, bias, w_out, grads, hyper)
    return loglik, feature_grad, g_in, small[0], g_out, small[1, :3]


def solution(mesh):
    placed = (
        P(("region", "dev"), None),
        P(("region", "dev")),
        P(("region", "dev")),
        P(),
        P(("region", "dev"), None),
        P(("region", "dev")),
        P(),
        P(),
        P(),
        P(),
    )
    return jax.shard_map(
        shards,
        mesh=mesh,
        in_specs=placed,
        out_specs=(P(("region", "dev")), P(("region", "dev"), None), P(), P(), P(), P()),
        check_vma=False,
    )
```

```python
import math

import jax
import jax.numpy as jnp
from jax import lax
from jax.experimental import pallas as pl
from jax.experimental.pallas import tpu as pltpu
from jax.sharding import PartitionSpec as P

H = 128
BS = 96
BPD = 2
NMAX = 4
WIN = 3
ROWS = BPD * BS
B = 128
N = 4 * B
STEPS = 8
GROUP = 16
CHUNK = 16

SQRT_THREE = math.sqrt(3.0)
LOG_TWO_PI = math.log(2.0 * math.pi)
MESH = pl.DeviceIdType.MESH
F32 = jnp.float32
BF16 = jnp.bfloat16


def dot(a, b, contract=((1,), (0,))):
    return lax.dot_general(a, b, (contract, ((), ())), preferred_element_type=F32)


NT = ((1,), (1,))
TN = ((0,), (0,))


def split2(a):
    hi = a.astype(BF16)
    return hi, (a - hi.astype(F32)).astype(BF16)


def split3(a):
    hi = a.astype(BF16)
    rest = a - hi.astype(F32)
    mid = rest.astype(BF16)
    return hi, mid, (rest - mid.astype(F32)).astype(BF16)


def lanes(*parts):
    return jnp.concatenate(parts, axis=1)


def rows_of(*parts):
    return jnp.concatenate(parts, axis=0)


def mul2(a, b):
    n = b.shape[1]
    pair = lanes(*split2(b))
    out = dot(lanes(*split2(a)), rows_of(pair, pair))
    return out[:, :n] + out[:, n:]


def mul3(a, b):
    ah, am, al = a if isinstance(a, tuple) else split3(a)
    bh, bm, bl = b if isinstance(b, tuple) else split3(b)
    n = bh.shape[1]
    pair = lanes(bh, bm)
    out = dot(lanes(ah, am), rows_of(pair, pair))
    low = dot(lanes(ah, al), rows_of(bl, bh))
    return out[:, :n] + (out[:, n:] + low)


def mul3_nt(a, b):
    ah, am, al = a
    bh, bm, bl = b
    n = bh.shape[0]
    pair = rows_of(bh, bm)
    out = dot(lanes(ah, am), lanes(pair, pair), NT)
    low = dot(lanes(ah, al), lanes(bl, bh), NT)
    return out[:, :n] + (out[:, n:] + low)


def eye_of(n):
    return (
        lax.broadcasted_iota(jnp.int32, (n, n), 0) == lax.broadcasted_iota(jnp.int32, (n, n), 1)
    ).astype(F32)


def inverses(mats, eye, coef, scales):
    res = [eye - coef * a for a in mats]
    inv = [(scales[0] * coef) * (eye + r) for r in res]
    res = [(1.0 - scales[0]) * eye + scales[0] * mul3(r, r) for r in res]
    for j in range(1, STEPS):
        s = scales[j]
        if j < STEPS - 1:
            both = [mul3(rows_of(x, r), r) for x, r in zip(inv, res)]
            inv = [s * (x + b[:B]) for x, b in zip(inv, both)]
            res = [(1.0 - s) * eye + s * b[B:] for b in both]
        else:
            inv = [s * (x + mul3(x, r)) for x, r in zip(inv, res)]
    return inv


def device(index):
    per = lax.axis_size("dev")
    return (index // per, index % per)


def my_index():
    return lax.axis_index("region") * lax.axis_size("dev") + lax.axis_index("dev")


def network(x, w_in, b_in, w_out):
    pre = dot(x, w_in) + b_in
    sig = 1.0 / (1.0 + jnp.exp(-pre))
    hidden = (pre * sig).astype(BF16)
    return pre, sig, hidden


def one_hot(point_slot, rows, first):
    slot = lax.broadcasted_iota(jnp.int32, (rows, ROWS), 0) + first
    return (slot == point_slot).astype(F32).astype(BF16)


def block(ref, s, a, b):
    return ref[s, a * B : (a + 1) * B, b * B : (b + 1) * B]


def member_windows(me, home_ref, ids_ref, cnt_ref, s):
    places = []
    for k in range(NMAX):
        slot = home_ref[ids_ref[s, k]]
        live = k < cnt_ref[s]
        w = jnp.where(live, (me - slot // BPD) * BPD + slot % BPD, 0)
        places.append((jnp.clip(w, 0, (WIN + 1) * BPD - 1), jnp.where(live, 1.0, 0.0)))
    return places


def kernel_matrix(s, count, places, feat_ref, resp_ref, z_ref, e_ref, k_ref, inv_sq, var, nug, eye):
    lane1 = lax.broadcasted_iota(jnp.int32, (1, B), 1)
    y_row = jnp.zeros((1, N), F32)
    for k, (w, flag) in enumerate(places + [(s, None)]):
        member = feat_ref[w]
        resp = jnp.where(lane1 < BS, resp_ref[w][0:1].astype(F32), 0.0)
        if flag is not None:
            member = (member.astype(F32) * flag).astype(BF16)
            resp = resp * flag
        z_ref[s, k * BS : (k + 1) * BS, :] = member
        resp = lanes(resp, jnp.zeros((1, N - B), F32))
        y_row = y_row + (pltpu.roll(resp, k * BS, 1) if k else resp)
    z_ref[s, (NMAX + 1) * BS :, :] = jnp.zeros((N - (NMAX + 1) * BS, H), BF16)
    z = z_ref[s]
    gram = dot(z, z, NT)
    diag = [jnp.where(eye > 0.0, gram[i * B : (i + 1) * B, i * B : (i + 1) * B], 0.0) for i in range(4)]
    sq_row = lanes(*[jnp.sum(d, axis=0, keepdims=True) for d in diag])
    col_id = lax.broadcasted_iota(jnp.int32, (1, N), 1)
    own = (col_id >= NMAX * BS) & (col_id < (NMAX + 1) * BS)
    v_row = jnp.where((col_id < count * BS) | own, 1.0, 0.0)
    for i in range(4):
        row_id = lax.broadcasted_iota(jnp.int32, (B, 1), 0) + i * B
        own = (row_id >= NMAX * BS) & (row_id < (NMAX + 1) * BS)
        v_col = jnp.where((row_id < count * BS) | own, 1.0, 0.0)
        sq_col = jnp.sum(diag[i], axis=1, keepdims=True)
        mine = slice(i * B, (i + 1) * B)
        for c in range(0, B, 32):
            part = slice(c, c + 32)
            out = slice(i * B + c, i * B + c + 32)
            d2 = jnp.maximum(sq_col[part] + sq_row - 2.0 * gram[out], 0.0)
            r2 = d2 * inv_sq + 1e-06
            rad = SQRT_THREE * (r2 * lax.rsqrt(r2))
            e = jnp.exp(-rad) * (v_col[part] * v_row)
            e_ref[s, out, :] = e
            wide = (i + 1) * B
            kern = var * (1.0 + rad[:, :wide]) * e[:, :wide]
            spot = kern[:, i * B :] + eye[part] * (nug * v_col[part] + 1.0 - v_col[part])
            k_ref[s, out, :wide] = lanes(kern[:, : i * B], spot) if i else spot
    k_ref[s, 3 * B + BS : 3 * B + BS + 1, :] = y_row


def eliminate(both, k_ref, eye, coef, scales):
    invs = []
    for i in range(3):
        lo = (i + 1) * B
        cols = slice(i * B, lo)
        cur = inverses([block(k_ref, s, i, i) for s in both], eye, coef, scales)
        invs.append([split3(c) for c in cur])
        below = [split3(k_ref[s, lo:, cols]) for s in both]
        panel = [split3(mul3(below[s], invs[i][s])) for s in both]
        for b in range(i + 1, 4):
            first = (b - i - 1) * B
            for s in both:
                at = slice(b * B, (b + 1) * B)
                k_ref[s, b * B :, at] = k_ref[s, b * B :, at] - mul3_nt(
                    tuple(p[first:] for p in panel[s]), tuple(p[first : first + B] for p in below[s])
                )
    return invs


def joint_gradient(s, invs, s_inv, resid, z_ref, e_ref, k_ref, var, inv_sq, nug, eye, real):
    sub = lax.broadcasted_iota(jnp.int32, (B, B), 0)
    lane = lax.broadcasted_iota(jnp.int32, (B, B), 1)
    x3 = mul3(block(k_ref, s, 3, 2), invs[2][s])
    p3 = split3(x3)
    x2 = mul3(block(k_ref, s, 3, 1) - mul3(p3, block(k_ref, s, 2, 1)), invs[1][s])
    p2 = split3(x2)
    t1 = block(k_ref, s, 3, 0) - mul3(p3, block(k_ref, s, 2, 0)) - mul3(p2, block(k_ref, s, 1, 0))
    x1 = mul3(t1, invs[0][s])
    sign = jnp.where(lax.broadcasted_iota(jnp.int32, (B, 1), 0) < BS, -1.0, 1.0)
    ys = [x1 * sign, x2 * sign, x3 * sign]
    own = jnp.where(real, eye, 0.0)
    beta_m = mul3(resid, s_inv)
    beta_row = beta_m[BS : BS + 1]
    beta_col = jnp.sum(eye * beta_row, axis=1, keepdims=True)
    mid = jnp.where(real, beta_col * beta_row - s_inv, 0.0) + beta_m
    mid = mid + jnp.where((lane == BS) & (sub < BS), beta_col, 0.0)
    quad = jnp.sum(jnp.sum(resid * beta_m, axis=0, keepdims=True), axis=1, keepdims=True)
    y = lanes(*ys, own)
    prod = mul2(mid, y)
    trace = jnp.sum(jnp.sum(prod * y, axis=0, keepdims=True), axis=1, keepdims=True)
    t2 = 0.5 * nug * trace
    t1 = 0.5 * quad - 0.5 * BS - t2
    w = rows_of(*[m.T for m in ys])
    g = mul2(w, prod)
    low = jnp.where(lax.broadcasted_iota(jnp.int32, (B, 1), 0) < BS, prod, 0.0)
    weights = rows_of(
        (g * e_ref[s, : 3 * B, :]).astype(BF16), (low * e_ref[s, 3 * B :, :]).astype(BF16)
    )
    z = z_ref[s]
    pz = dot(weights, lanes(z, jnp.ones_like(z)))
    zf = z.astype(F32)
    grad = (3.0 * var * inv_sq) * (pz[:, :H] - pz[:, H:] * zf)
    t0 = -jnp.sum(jnp.sum(grad * zf, axis=0, keepdims=True), axis=1, keepdims=True)
    lane1 = lax.broadcasted_iota(jnp.int32, (1, B), 1)
    hyper = jnp.where(lane1 == 0, t0, 0.0) + jnp.where(lane1 == 1, t1, 0.0)
    return grad, hyper + jnp.where(lane1 == 2, t2, 0.0), quad


def log_likelihood(mat, quad):
    mat = mat[:BS]
    pivots = []
    for k in range(BS):
        at = k - (BS - mat.shape[0])
        row = mat[at : at + 1]
        pivots.append(row[:, k : k + 1])
        if k < BS - 1:
            if (k + 1) % 8 == 0:
                mat = mat[8:]
                mat = mat - mat[:, k : k + 1] * (row / pivots[-1])
            else:
                mat = mat - mat[:, k : k + 1] * (row / pivots[-1])
    logdet = jnp.zeros((1, 1), F32)
    for p in pivots:
        logdet = logdet + jnp.log(p)
    return (-0.5 * quad - 0.5 * logdet) * (1.0 / BS) - 0.5 * LOG_TWO_PI


def main_kernel(
    x_ref, resp_ref, ps_ref, w_in_ref, b_ref, w_out_ref, home_ref, ids_ref, cnt_ref, par_ref,
    ll_ref, fg_ref, gath, ext_ref,
    win_ref, wresp_ref, feat_ref, hid_ref, dsil_ref, z_ref, e_ref, k_ref, gw_ref,
    out_buf, in_buf, part, part_in, red, red_in,
    f_send, f_recv, y_send, y_recv, g_send, g_recv, s1, r1, s2, r2, s3, r3,
):
    total = lax.axis_size("region") * lax.axis_size("dev")
    region, dev = lax.axis_index("region"), lax.axis_index("dev")
    me = my_index()
    x, core, y, z = region // 2, region % 2, dev // 8, dev % 8
    ga = x * 4 + y
    gb = core * 8 + z

    def mate_a(k):
        other = lax.rem(ga + k, GROUP)
        return other, ((other // 4) * 2 + core, (other % 4) * 8 + z)

    def mate_b(k):
        other = lax.rem(gb + k, GROUP)
        return other, (x * 2 + other // 8, y * 8 + other % 8)

    def send(src, dst, ssem, rsem, place):
        copy = pltpu.make_async_remote_copy(
            src_ref=src, dst_ref=dst, send_sem=ssem, recv_sem=rsem, device_id=place, device_id_type=MESH
        )
        copy.start()
        return copy

    def later(k):
        return device(lax.rem(me + k + total, total))

    barrier = pltpu.get_barrier_semaphore()
    for k in range(1, WIN + 1):
        pl.semaphore_signal(barrier, inc=1, device_id=later(k), device_id_type=MESH)
        pl.semaphore_signal(barrier, inc=1, device_id=later(-k), device_id_type=MESH)
    for k in range(1, GROUP):
        pl.semaphore_signal(barrier, inc=1, device_id=mate_a(k)[1], device_id_type=MESH)
        pl.semaphore_signal(barrier, inc=1, device_id=mate_b(k)[1], device_id_type=MESH)

    point_slot = ps_ref[...]
    win_ref[0] = dot(one_hot(point_slot, ROWS, 0), x_ref[...]).astype(BF16)
    resp = jnp.broadcast_to(resp_ref[...].astype(F32), (16, ROWS)).astype(BF16)
    wresp_ref[0] = dot(resp, one_hot(point_slot, B, 0), NT).astype(BF16)
    wresp_ref[1] = dot(resp, one_hot(point_slot, B, BS), NT).astype(BF16)
    pl.semaphore_wait(barrier, 2 * WIN + 2 * (GROUP - 1))
    copies = []
    for k in range(1, WIN + 1):
        copies.append(send(win_ref.at[0], win_ref.at[k], f_send.at[k], f_recv.at[k], later(k)))
        copies.append(
            send(
                wresp_ref.at[pl.ds(0, 2)], wresp_ref.at[pl.ds(2 * k, 2)], y_send.at[k], y_recv.at[k], later(k)
            )
        )

    def forward(d):
        pre, sig, hidden = network(win_ref[d], w_in_ref[...], b_ref[...], w_out_ref[...])
        hid_ref[d] = hidden
        dsil_ref[d] = sig * (1.0 + pre * (1.0 - sig))
        feats = dot(hidden, w_out_ref[...]).astype(BF16)
        feat_ref[2 * d] = feats[:BS]
        feat_ref[2 * d + 1] = feats[BS:]

    forward(0)

    def const(v):
        return jnp.full((1, 1), v, F32)

    inv_sq = jnp.exp(-2.0 * const(par_ref[0]))
    var = jnp.exp(const(par_ref[1]))
    nug = jnp.exp(const(par_ref[2]))
    eye = eye_of(B)
    lane = lax.broadcasted_iota(jnp.int32, (B, B), 1)
    sub = lax.broadcasted_iota(jnp.int32, (B, B), 0)
    top = B * var + 1.0
    coef = 2.0 / (top + nug)
    delta = (top - nug) / (top + nug)
    scales = []
    for _ in range(STEPS):
        sq = delta * delta
        scales.append(2.0 / (2.0 - sq))
        delta = sq / (2.0 - sq)
    both = range(BPD)
    places = [member_windows(me, home_ref, ids_ref, cnt_ref, s) for s in both]
    for c in copies:
        c.wait()
    for d in range(1, WIN + 1):
        forward(d)

    for s in both:
        kernel_matrix(
            s, cnt_ref[s], places[s], feat_ref, wresp_ref, z_ref, e_ref, k_ref, inv_sq, var, nug, eye
        )
    invs = eliminate(both, k_ref, eye, coef, scales)
    real = (lane < BS) & (sub < BS)
    last = [block(k_ref, s, 3, 3) for s in both]
    resid = [jnp.where((sub == BS) & (lane < BS), m, 0.0) for m in last]
    schur = [jnp.where(real, m, eye) for m in last]
    s_inv = inverses(schur, eye, coef, scales)
    grads, hypers, quads = [], [], []
    for s in both:
        grad, hyper, quad = joint_gradient(
            s, invs, s_inv[s], resid[s], z_ref, e_ref, k_ref, var, inv_sq, nug, eye, real
        )
        grads.append(grad)
        hypers.append(hyper)
        quads.append(quad)
    for w in range((WIN + 1) * BPD):
        acc = grads[w][NMAX * BS : (NMAX + 1) * BS] if w < BPD else jnp.zeros((BS, H), F32)
        for s in both:
            if w == 1 or (w == 0 and s == 0):
                continue
            for k in range(NMAX):
                place, flag = places[s][k]
                acc = acc + jnp.where(place == w, flag, 0.0) * grads[s][k * BS : (k + 1) * BS]
        gw_ref[w] = acc
        if w >= BPD:
            out_buf[w // BPD - 1, (w % BPD) * BS : (w % BPD + 1) * BS, :] = acc.astype(BF16)
    returns = [
        send(out_buf.at[k - 1], in_buf.at[k - 1], g_send.at[k], g_recv.at[k], later(-k))
        for k in range(1, WIN + 1)
    ]

    w_in_part = jnp.zeros((H, 2 * H), F32)
    w_out_part = jnp.zeros((H, 2 * H), F32)
    b_part = jnp.zeros((1, H), F32)
    for d in range(WIN + 1):
        hi, lo = split2(rows_of(gw_ref[2 * d], gw_ref[2 * d + 1]))
        back = dot(hi, w_out_ref[...], NT) + dot(lo, w_out_ref[...], NT)
        dpre = back * dsil_ref[d]
        w_out_part = w_out_part + dot(hid_ref[d], lanes(hi, lo), TN)
        w_in_part = w_in_part + dot(win_ref[d], lanes(*split2(dpre)), TN)
        b_part = b_part + jnp.sum(dpre, axis=0, keepdims=True)
    w_in_part = (w_in_part[:, :H] + w_in_part[:, H:]).astype(BF16)
    w_out_part = (w_out_part[:, :H] + w_out_part[:, H:]).astype(BF16)
    row = lax.broadcasted_iota(jnp.int32, (16, H), 0)

    def pack(bias, hyper):
        tile = jnp.zeros((16, H), F32)
        for i, part_row in enumerate(split2(bias) + split2(hyper)):
            tile = tile + jnp.where(row == i, part_row.astype(F32), 0.0)
        return tile.astype(BF16)

    def unpack(tile):
        return tile[0:1] + tile[1:2], tile[2:3] + tile[3:4]

    small = pack(b_part, hypers[0] + hypers[1])
    for c in range(GROUP):
        src = w_in_part if c < 8 else w_out_part
        part[c, :CHUNK, :] = src[(c % 8) * CHUNK : (c % 8 + 1) * CHUNK]
        part[c, CHUNK:, :] = small
    copies = []
    for k in range(1, GROUP):
        other, place = mate_a(k)
        copies.append(send(part.at[other], part_in.at[ga], s1.at[k], r1.at[k], place))
    part_in[ga] = part[ga]
    ll_ref[0] = jnp.sum(log_likelihood(schur[0], quads[0]))
    for c in copies:
        c.wait()
    acc = part_in[0].astype(F32)
    for c in range(1, GROUP):
        acc = acc + part_in[c].astype(F32)
    red[:CHUNK, :] = acc[:CHUNK].astype(BF16)
    red[CHUNK:, :] = pack(*unpack(acc[CHUNK:]))

    copies = []
    for k in range(1, GROUP):
        copies.append(send(red, red_in.at[gb], s2.at[k], r2.at[k], mate_b(k)[1]))
    red_in[gb] = red[...]
    ll_ref[1] = jnp.sum(log_likelihood(schur[1], quads[1]))
    for c in copies:
        c.wait()
    acc = red_in[0].astype(F32)
    for c in range(1, GROUP):
        acc = acc + red_in[c].astype(F32)
    gath[ga] = acc[:CHUNK].astype(BF16)
    copies = []
    for k in range(1, GROUP):
        copies.append(send(gath.at[ga], gath.at[ga], s3.at[k], r3.at[k], mate_a(k)[1]))
    bias, hyper = unpack(acc[CHUNK:])
    row8 = lax.broadcasted_iota(jnp.int32, (8, H), 0)
    ext_ref[...] = jnp.where(row8 == 0, bias, 0.0) + jnp.where(row8 == 1, hyper, 0.0)
    for c in returns:
        c.wait()
    grad = rows_of(gw_ref[0], gw_ref[1])
    for k in range(WIN):
        grad = grad + in_buf[k].astype(F32)
    fg_ref[...] = grad
    for c in copies:
        c.wait()


def finish_kernel(ps_ref, ll_in, grad_ref, gath_ref, ext_ref, ll_ref, fg_ref, gin_ref, b_ref, gout_ref, hyp_ref):
    scale = 1.0 / (lax.axis_size("region") * lax.axis_size("dev") * ROWS)
    hi, lo = split2(grad_ref[...])
    both = dot(one_hot(ps_ref[...], ROWS, 0), lanes(hi, lo), TN)
    fg_ref[...] = both[:, :H] + both[:, H:]
    for c in range(8):
        gin_ref[c * CHUNK : (c + 1) * CHUNK, :] = gath_ref[c].astype(F32) * scale
        gout_ref[c * CHUNK : (c + 1) * CHUNK, :] = gath_ref[8 + c].astype(F32) * scale
    ext = ext_ref[...] * scale
    b_ref[...] = ext[0:1].reshape(H)
    for i in range(3):
        hyp_ref[i] = jnp.sum(ext[1:2, i : i + 1])
    for s in range(BPD):
        ll_ref[s] = ll_in[s]


VM = pl.BlockSpec(memory_space=pltpu.VMEM)
SM = pl.BlockSpec(memory_space=pltpu.SMEM)
DMA = pltpu.SemaphoreType.DMA


def shards(
    inputs, responses, point_slot, block_home, nbr_ids, nbr_count, w_in, b_in, w_out, kernel_params
):
    place_row = point_slot.reshape(1, ROWS)
    loglik, grad, gath, ext = pl.pallas_call(
        main_kernel,
        out_shape=(
            jax.ShapeDtypeStruct((BPD,), F32),
            jax.ShapeDtypeStruct((ROWS, H), F32),
            jax.ShapeDtypeStruct((GROUP, CHUNK, H), BF16),
            jax.ShapeDtypeStruct((8, H), F32),
        ),
        in_specs=[VM] * 6 + [SM] * 4,
        out_specs=(SM, VM, VM, VM),
        scratch_shapes=[
            pltpu.VMEM((WIN + 1, ROWS, H), BF16),
            pltpu.VMEM(((WIN + 1) * BPD, 16, H), BF16),
            pltpu.VMEM(((WIN + 1) * BPD, BS, H), BF16),
            pltpu.VMEM((WIN + 1, ROWS, H), BF16),
            pltpu.VMEM((WIN + 1, ROWS, H), F32),
            pltpu.VMEM((BPD, N, H), BF16),
            pltpu.VMEM((BPD, N, N), F32),
            pltpu.VMEM((BPD, N, N), F32),
            pltpu.VMEM(((WIN + 1) * BPD, BS, H), F32),
            pltpu.VMEM((WIN, ROWS, H), BF16),
            pltpu.VMEM((WIN, ROWS, H), BF16),
            pltpu.VMEM((GROUP, 2 * CHUNK, H), BF16),
            pltpu.VMEM((GROUP, 2 * CHUNK, H), BF16),
            pltpu.VMEM((2 * CHUNK, H), BF16),
            pltpu.VMEM((GROUP, 2 * CHUNK, H), BF16),
        ]
        + [DMA((WIN + 1,))] * 6
        + [DMA((GROUP,))] * 6,
        compiler_params=pltpu.CompilerParams(
            collective_id=0, has_side_effects=True, vmem_limit_bytes=48 * 1024 * 1024
        ),
        name="vecchia_main",
    )(
        inputs, responses.reshape(1, ROWS), place_row, w_in, b_in.reshape(1, H), w_out,
        block_home, nbr_ids, nbr_count, kernel_params,
    )
    loglik, feature_grad, g_in, g_b, g_out, hyper = pl.pallas_call(
        finish_kernel,
        out_shape=(
            jax.ShapeDtypeStruct((BPD,), F32),
            jax.ShapeDtypeStruct((ROWS, H), F32),
            jax.ShapeDtypeStruct((H, H), F32),
            jax.ShapeDtypeStruct((H,), F32),
            jax.ShapeDtypeStruct((H, H), F32),
            jax.ShapeDtypeStruct((3,), F32),
        ),
        in_specs=[VM, SM, VM, VM, VM],
        out_specs=(SM, VM, VM, VM, VM, SM),
        name="vecchia_finish",
    )(place_row, loglik, grad, gath, ext)
    return loglik, feature_grad, g_in, g_b, g_out, hyper


def solution(mesh):
    placed = (
        P(("region", "dev"), None),
        P(("region", "dev")),
        P(("region", "dev")),
        P(),
        P(("region", "dev"), None),
        P(("region", "dev")),
        P(),
        P(),
        P(),
        P(),
    )
    return jax.shard_map(
        shards,
        mesh=mesh,
        in_specs=placed,
        out_specs=(P(("region", "dev")), P(("region", "dev"), None), P(), P(), P(), P()),
        check_vma=False,
    )
```

```python
import math

import jax
import jax.numpy as jnp
from jax import lax
from jax.experimental import pallas as pl
from jax.experimental.pallas import tpu as pltpu
from jax.sharding import PartitionSpec as P

H = 128
BS = 96
BPD = 2
NMAX = 4
WIN = 3
ROWS = BPD * BS
B = 128
N = 4 * B
STEPS = 8
GROUP = 16
CHUNK = 16
DEPTH = 8

SQRT_THREE = math.sqrt(3.0)
LOG_TWO_PI = math.log(2.0 * math.pi)
MESH = pl.DeviceIdType.MESH
F32 = jnp.float32
BF16 = jnp.bfloat16


def dot(a, b, contract=((1,), (0,))):
    return lax.dot_general(a, b, (contract, ((), ())), preferred_element_type=F32)


NT = ((1,), (1,))
TN = ((0,), (0,))


def split2(a):
    hi = a.astype(BF16)
    return hi, (a - hi.astype(F32)).astype(BF16)


def split3(a):
    hi = a.astype(BF16)
    rest = a - hi.astype(F32)
    mid = rest.astype(BF16)
    return hi, mid, (rest - mid.astype(F32)).astype(BF16)


def lanes(*parts):
    return jnp.concatenate(parts, axis=1)


def rows_of(*parts):
    return jnp.concatenate(parts, axis=0)


def mul2(a, b):
    n = b.shape[1]
    pair = lanes(*split2(b))
    out = dot(lanes(*split2(a)), rows_of(pair, pair))
    return out[:, :n] + out[:, n:]


def mul3(a, b):
    ah, am, al = a if isinstance(a, tuple) else split3(a)
    bh, bm, bl = b if isinstance(b, tuple) else split3(b)
    n = bh.shape[1]
    pair = lanes(bh, bm)
    out = dot(lanes(ah, am), rows_of(pair, pair))
    low = dot(lanes(ah, al), rows_of(bl, bh))
    return out[:, :n] + (out[:, n:] + low)


def mul3_nt(a, b):
    ah, am, al = a
    bh, bm, bl = b
    n = bh.shape[0]
    pair = rows_of(bh, bm)
    out = dot(lanes(ah, am), lanes(pair, pair), NT)
    low = dot(lanes(ah, al), lanes(bl, bh), NT)
    return out[:, :n] + (out[:, n:] + low)


def eye_of(n):
    return (
        lax.broadcasted_iota(jnp.int32, (n, n), 0) == lax.broadcasted_iota(jnp.int32, (n, n), 1)
    ).astype(F32)


def inverses(mats, eye, coef, scales):
    res = [eye - coef * a for a in mats]
    inv = [(scales[0] * coef) * (eye + r) for r in res]
    res = [(1.0 - scales[0]) * eye + scales[0] * mul3(r, r) for r in res]
    for j in range(1, STEPS):
        s = scales[j]
        if j < STEPS - 1:
            both = [mul3(rows_of(x, r), r) for x, r in zip(inv, res)]
            inv = [s * (x + b[:B]) for x, b in zip(inv, both)]
            res = [(1.0 - s) * eye + s * b[B:] for b in both]
        else:
            inv = [s * (x + mul3(x, r)) for x, r in zip(inv, res)]
    return inv


def device(index):
    per = lax.axis_size("dev")
    return (index // per, index % per)


def my_index():
    return lax.axis_index("region") * lax.axis_size("dev") + lax.axis_index("dev")


def network(x, w_in, b_in, w_out):
    pre = dot(x, w_in) + b_in
    sig = 1.0 / (1.0 + jnp.exp(-pre))
    hidden = (pre * sig).astype(BF16)
    return pre, sig, hidden


def one_hot(point_slot, rows, first):
    slot = lax.broadcasted_iota(jnp.int32, (rows, ROWS), 0) + first
    return (slot == point_slot).astype(F32).astype(BF16)


def block(ref, s, a, b):
    return ref[s, a * B : (a + 1) * B, b * B : (b + 1) * B]


def member_windows(me, home_ref, ids_ref, cnt_ref, s):
    places = []
    for k in range(NMAX):
        slot = home_ref[ids_ref[s, k]]
        live = k < cnt_ref[s]
        w = jnp.where(live, (me - slot // BPD) * BPD + slot % BPD, 0)
        places.append((jnp.clip(w, 0, (WIN + 1) * BPD - 1), jnp.where(live, 1.0, 0.0)))
    return places


def kernel_matrix(s, count, places, feat_ref, resp_ref, z_ref, e_ref, k_ref, inv_sq, var, nug, eye):
    lane1 = lax.broadcasted_iota(jnp.int32, (1, B), 1)
    y_row = jnp.zeros((1, N), F32)
    for k, (w, flag) in enumerate(places + [(s, None)]):
        member = feat_ref[w]
        resp = jnp.where(lane1 < BS, resp_ref[w][0:1].astype(F32), 0.0)
        if flag is not None:
            member = (member.astype(F32) * flag).astype(BF16)
            resp = resp * flag
        z_ref[s, k * BS : (k + 1) * BS, :] = member
        resp = lanes(resp, jnp.zeros((1, N - B), F32))
        y_row = y_row + (pltpu.roll(resp, k * BS, 1) if k else resp)
    z_ref[s, (NMAX + 1) * BS :, :] = jnp.zeros((N - (NMAX + 1) * BS, H), BF16)
    z = z_ref[s]
    gram = dot(z, z, NT)
    diag = [jnp.where(eye > 0.0, gram[i * B : (i + 1) * B, i * B : (i + 1) * B], 0.0) for i in range(4)]
    sq_row = lanes(*[jnp.sum(d, axis=0, keepdims=True) for d in diag])
    col_id = lax.broadcasted_iota(jnp.int32, (1, N), 1)
    own = (col_id >= NMAX * BS) & (col_id < (NMAX + 1) * BS)
    v_row = jnp.where((col_id < count * BS) | own, 1.0, 0.0)
    for i in range(4):
        row_id = lax.broadcasted_iota(jnp.int32, (B, 1), 0) + i * B
        own = (row_id >= NMAX * BS) & (row_id < (NMAX + 1) * BS)
        v_col = jnp.where((row_id < count * BS) | own, 1.0, 0.0)
        sq_col = jnp.sum(diag[i], axis=1, keepdims=True)
        mine = slice(i * B, (i + 1) * B)
        for c in range(0, B, 32):
            part = slice(c, c + 32)
            out = slice(i * B + c, i * B + c + 32)
            d2 = jnp.maximum(sq_col[part] + sq_row - 2.0 * gram[out], 0.0)
            r2 = d2 * inv_sq + 1e-06
            rad = SQRT_THREE * (r2 * lax.rsqrt(r2))
            e = jnp.exp(-rad) * (v_col[part] * v_row)
            e_ref[s, out, :] = e
            wide = (i + 1) * B
            kern = var * (1.0 + rad[:, :wide]) * e[:, :wide]
            spot = kern[:, i * B :] + eye[part] * (nug * v_col[part] + 1.0 - v_col[part])
            k_ref[s, out, :wide] = lanes(kern[:, : i * B], spot) if i else spot
    k_ref[s, 3 * B + BS : 3 * B + BS + 1, :] = y_row


def eliminate(both, k_ref, eye, coef, scales):
    invs = []
    for i in range(3):
        lo = (i + 1) * B
        cols = slice(i * B, lo)
        cur = inverses([block(k_ref, s, i, i) for s in both], eye, coef, scales)
        invs.append([split3(c) for c in cur])
        below = [split3(k_ref[s, lo:, cols]) for s in both]
        panel = [split3(mul3(below[s], invs[i][s])) for s in both]
        for b in range(i + 1, 4):
            first = (b - i - 1) * B
            for s in both:
                at = slice(b * B, (b + 1) * B)
                k_ref[s, b * B :, at] = k_ref[s, b * B :, at] - mul3_nt(
                    tuple(p[first:] for p in panel[s]), tuple(p[first : first + B] for p in below[s])
                )
    return invs


def joint_gradient(s, invs, s_inv, resid, z_ref, e_ref, k_ref, var, inv_sq, nug, eye, real):
    sub = lax.broadcasted_iota(jnp.int32, (B, B), 0)
    lane = lax.broadcasted_iota(jnp.int32, (B, B), 1)
    x3 = mul3(block(k_ref, s, 3, 2), invs[2][s])
    p3 = split3(x3)
    x2 = mul3(block(k_ref, s, 3, 1) - mul3(p3, block(k_ref, s, 2, 1)), invs[1][s])
    p2 = split3(x2)
    t1 = block(k_ref, s, 3, 0) - mul3(p3, block(k_ref, s, 2, 0)) - mul3(p2, block(k_ref, s, 1, 0))
    x1 = mul3(t1, invs[0][s])
    sign = jnp.where(lax.broadcasted_iota(jnp.int32, (B, 1), 0) < BS, -1.0, 1.0)
    ys = [x1 * sign, x2 * sign, x3 * sign]
    own = jnp.where(real, eye, 0.0)
    beta_m = mul3(resid, s_inv)
    beta_row = beta_m[BS : BS + 1]
    beta_col = jnp.sum(eye * beta_row, axis=1, keepdims=True)
    mid = jnp.where(real, beta_col * beta_row - s_inv, 0.0) + beta_m
    mid = mid + jnp.where((lane == BS) & (sub < BS), beta_col, 0.0)
    quad = jnp.sum(jnp.sum(resid * beta_m, axis=0, keepdims=True), axis=1, keepdims=True)
    y = lanes(*ys, own)
    prod = mul2(mid, y)
    trace = jnp.sum(jnp.sum(prod * y, axis=0, keepdims=True), axis=1, keepdims=True)
    t2 = 0.5 * nug * trace
    t1 = 0.5 * quad - 0.5 * BS - t2
    w = rows_of(*[m.T for m in ys])
    g = mul2(w, prod)
    low = jnp.where(lax.broadcasted_iota(jnp.int32, (B, 1), 0) < BS, prod, 0.0)
    weights = rows_of(
        (g * e_ref[s, : 3 * B, :]).astype(BF16), (low * e_ref[s, 3 * B :, :]).astype(BF16)
    )
    z = z_ref[s]
    pz = dot(weights, lanes(z, jnp.ones_like(z)))
    zf = z.astype(F32)
    grad = (3.0 * var * inv_sq) * (pz[:, :H] - pz[:, H:] * zf)
    t0 = -jnp.sum(jnp.sum(grad * zf, axis=0, keepdims=True), axis=1, keepdims=True)
    lane1 = lax.broadcasted_iota(jnp.int32, (1, B), 1)
    hyper = jnp.where(lane1 == 0, t0, 0.0) + jnp.where(lane1 == 1, t1, 0.0)
    return grad, hyper + jnp.where(lane1 == 2, t2, 0.0), quad


def pivot_steps(mat_ref, log_ref, first, last):
    mats = [mat_ref[i, first:BS, :] for i in range(BPD)]
    logdets = [log_ref[i, 0:1, 0:1] for i in range(BPD)]
    for k in range(first, last):
        for i, mat in enumerate(mats):
            at = k - (BS - mat.shape[0])
            row = mat[at : at + 1]
            pivot = row[:, k : k + 1]
            logdets[i] = logdets[i] + jnp.log(pivot)
            if k < BS - 1:
                if (k + 1) % 8 == 0:
                    mat = mat[8:]
                mats[i] = mat - mat[:, k : k + 1] * (row / pivot)
    for i in range(BPD):
        log_ref[i, 0:1, :] = jnp.broadcast_to(logdets[i], (1, B))
        if last < BS:
            mat_ref[i, last:BS, :] = mats[i]


def main_kernel(
    x_ref, resp_ref, ps_ref, w_in_ref, b_ref, w_out_ref, home_ref, ids_ref, cnt_ref, par_ref,
    ll_ref, fg_ref, gath, ext_ref,
    win_ref, wresp_ref, feat_ref, hid_ref, dsil_ref, z_ref, e_ref, k_ref, gw_ref,
    out_buf, in_buf, part, part_in, pair, red_in, mat_ref, log_ref,
    f_send, f_recv, y_send, y_recv, g_send, g_recv, s1, r1, s2, r2, s3, r3, c_send, c_recv,
):
    total = lax.axis_size("region") * lax.axis_size("dev")
    region, dev = lax.axis_index("region"), lax.axis_index("dev")
    me = my_index()
    x, core, y, z = region // 2, region % 2, dev // DEPTH, dev % DEPTH
    ga = x * 4 + y

    def mate_a(k):
        other = lax.rem(ga + k, GROUP)
        return other, ((other // 4) * 2 + core, (other % 4) * DEPTH + z)

    def send(src, dst, ssem, rsem, place):
        copy = pltpu.make_async_remote_copy(
            src_ref=src, dst_ref=dst, send_sem=ssem, recv_sem=rsem, device_id=place, device_id_type=MESH
        )
        copy.start()
        return copy

    def later(k):
        return device(lax.rem(me + k + total, total))

    barrier = pltpu.get_barrier_semaphore()
    for k in range(1, WIN + 1):
        pl.semaphore_signal(barrier, inc=1, device_id=later(k), device_id_type=MESH)
        pl.semaphore_signal(barrier, inc=1, device_id=later(-k), device_id_type=MESH)
    for k in range(1, GROUP):
        pl.semaphore_signal(barrier, inc=1, device_id=mate_a(k)[1], device_id_type=MESH)
    for k in range(1, DEPTH):
        place = (region, y * DEPTH + lax.rem(z + k, DEPTH))
        pl.semaphore_signal(barrier, inc=1, device_id=place, device_id_type=MESH)
    pl.semaphore_signal(barrier, inc=1, device_id=(x * 2 + 1 - core, dev), device_id_type=MESH)

    point_slot = ps_ref[...].reshape(1, ROWS)
    win_ref[0] = dot(one_hot(point_slot, ROWS, 0), x_ref[...]).astype(BF16)
    resp = jnp.broadcast_to(resp_ref[...].astype(F32).reshape(1, ROWS), (16, ROWS)).astype(BF16)
    wresp_ref[0] = dot(resp, one_hot(point_slot, B, 0), NT).astype(BF16)
    wresp_ref[1] = dot(resp, one_hot(point_slot, B, BS), NT).astype(BF16)
    pl.semaphore_wait(barrier, 2 * WIN + GROUP + DEPTH - 1)
    copies = []
    for k in range(1, WIN + 1):
        copies.append(send(win_ref.at[0], win_ref.at[k], f_send.at[k], f_recv.at[k], later(k)))
        copies.append(
            send(
                wresp_ref.at[pl.ds(0, 2)], wresp_ref.at[pl.ds(2 * k, 2)], y_send.at[k], y_recv.at[k], later(k)
            )
        )

    def forward(d):
        pre, sig, hidden = network(win_ref[d], w_in_ref[...], b_ref[...].reshape(1, H), w_out_ref[...])
        hid_ref[d] = hidden
        dsil_ref[d] = sig * (1.0 + pre * (1.0 - sig))
        feats = dot(hidden, w_out_ref[...]).astype(BF16)
        feat_ref[2 * d] = feats[:BS]
        feat_ref[2 * d + 1] = feats[BS:]

    forward(0)

    def const(v):
        return jnp.full((1, 1), v, F32)

    inv_sq = jnp.exp(-2.0 * const(par_ref[0]))
    var = jnp.exp(const(par_ref[1]))
    nug = jnp.exp(const(par_ref[2]))
    eye = eye_of(B)
    lane = lax.broadcasted_iota(jnp.int32, (B, B), 1)
    sub = lax.broadcasted_iota(jnp.int32, (B, B), 0)
    top = B * var + 1.0
    coef = 2.0 / (top + nug)
    delta = (top - nug) / (top + nug)
    scales = []
    for _ in range(STEPS):
        sq = delta * delta
        scales.append(2.0 / (2.0 - sq))
        delta = sq / (2.0 - sq)
    both = range(BPD)
    places = [member_windows(me, home_ref, ids_ref, cnt_ref, s) for s in both]
    for c in copies:
        c.wait()
    for d in range(1, WIN + 1):
        forward(d)

    for s in both:
        kernel_matrix(
            s, cnt_ref[s], places[s], feat_ref, wresp_ref, z_ref, e_ref, k_ref, inv_sq, var, nug, eye
        )
    invs = eliminate(both, k_ref, eye, coef, scales)
    real = (lane < BS) & (sub < BS)
    last = [block(k_ref, s, 3, 3) for s in both]
    resid = [jnp.where((sub == BS) & (lane < BS), m, 0.0) for m in last]
    schur = [jnp.where(real, m, eye) for m in last]
    s_inv = inverses(schur, eye, coef, scales)
    for s in both:
        mat_ref[s] = schur[s][:BS]
    grads, hypers, quads = [], [], []
    for s in both:
        grad, hyper, quad = joint_gradient(
            s, invs, s_inv[s], resid[s], z_ref, e_ref, k_ref, var, inv_sq, nug, eye, real
        )
        grads.append(grad)
        hypers.append(hyper)
        quads.append(quad)
    for w in range((WIN + 1) * BPD):
        acc = grads[w][NMAX * BS : (NMAX + 1) * BS] if w < BPD else jnp.zeros((BS, H), F32)
        for s in both:
            if w == 1 or (w == 0 and s == 0):
                continue
            for k in range(NMAX):
                place, flag = places[s][k]
                acc = acc + jnp.where(place == w, flag, 0.0) * grads[s][k * BS : (k + 1) * BS]
        gw_ref[w] = acc
        if w >= BPD:
            out_buf[w // BPD - 1, (w % BPD) * BS : (w % BPD + 1) * BS, :] = acc.astype(BF16)
    returns = [
        send(out_buf.at[k - 1], in_buf.at[k - 1], g_send.at[k], g_recv.at[k], later(-k))
        for k in range(1, WIN + 1)
    ]

    w_in_part = jnp.zeros((H, 2 * H), F32)
    w_out_part = jnp.zeros((H, 2 * H), F32)
    b_part = jnp.zeros((1, H), F32)
    for d in range(WIN + 1):
        hi, lo = split2(rows_of(gw_ref[2 * d], gw_ref[2 * d + 1]))
        back = dot(hi, w_out_ref[...], NT) + dot(lo, w_out_ref[...], NT)
        dpre = back * dsil_ref[d]
        w_out_part = w_out_part + dot(hid_ref[d], lanes(hi, lo), TN)
        w_in_part = w_in_part + dot(win_ref[d], lanes(*split2(dpre)), TN)
        b_part = b_part + jnp.sum(dpre, axis=0, keepdims=True)
    w_in_part = w_in_part[:, :H] + w_in_part[:, H:]
    w_out_part = w_out_part[:, :H] + w_out_part[:, H:]
    row8 = lax.broadcasted_iota(jnp.int32, (8, H), 0)
    for s in both:
        log_ref[s] = jnp.where(row8 == 1, quads[s], 0.0)
    small = jnp.where(row8 == 0, b_part, 0.0) + jnp.where(row8 == 1, hypers[0] + hypers[1], 0.0)
    for c in range(GROUP):
        src = w_in_part if c < 8 else w_out_part
        part[c, :CHUNK, :] = src[(c % 8) * CHUNK : (c % 8 + 1) * CHUNK]
        part[c, CHUNK:, :] = small
    copies = []
    for k in range(1, GROUP):
        other, place = mate_a(k)
        copies.append(send(part.at[other], part_in.at[ga], s1.at[k], r1.at[k], place))
    part_in[ga] = part[ga]

    @pl.when(dev >= 0)
    def _():
        pivot_steps(mat_ref, log_ref, 0, 32)

    for c in copies:
        c.wait()
    acc = part_in[0]
    for c in range(1, GROUP):
        acc = acc + part_in[c]
    pair[core] = acc
    copy = send(pair.at[core], pair.at[core], c_send, c_recv, (x * 2 + 1 - core, dev))
    copy.wait()
    red_in[z] = pair[0] + pair[1]
    copies = []
    for k in range(1, DEPTH):
        place = (region, y * DEPTH + lax.rem(z + k, DEPTH))
        copies.append(send(red_in.at[z], red_in.at[z], s2.at[k], r2.at[k], place))

    @pl.when(dev >= 0)
    def _():
        pivot_steps(mat_ref, log_ref, 32, 64)

    for c in copies:
        c.wait()
    acc = red_in[0]
    for c in range(1, DEPTH):
        acc = acc + red_in[c]
    gath[ga] = acc[:CHUNK].astype(BF16)
    ext_ref[...] = acc[CHUNK:]
    copies = []
    for k in range(1, GROUP):
        copies.append(send(gath.at[ga], gath.at[ga], s3.at[k], r3.at[k], mate_a(k)[1]))

    @pl.when(dev >= 0)
    def _():
        pivot_steps(mat_ref, log_ref, 64, BS)
        for s in both:
            ll = -0.5 * (log_ref[s, 0:1, 0:1] + log_ref[s, 1:2, 0:1]) * (1.0 / BS) - 0.5 * LOG_TWO_PI
            ll_ref[s] = jnp.sum(ll)

    for c in returns:
        c.wait()
    grad = rows_of(gw_ref[0], gw_ref[1])
    for k in range(WIN):
        grad = grad + in_buf[k].astype(F32)
    perm = one_hot(ps_ref[...].reshape(1, ROWS), ROWS, 0)
    pairs = dot(perm, lanes(*split2(grad)), TN)
    fg_ref[...] = pairs[:, :H] + pairs[:, H:]
    for c in copies:
        c.wait()


def finish_kernel(ll_in, grad_ref, gath_ref, ext_ref, ll_ref, fg_ref, gin_ref, b_ref, gout_ref, hyp_ref):
    scale = 1.0 / (lax.axis_size("region") * lax.axis_size("dev") * ROWS)
    fg_ref[...] = grad_ref[...]
    for c in range(8):
        gin_ref[c * CHUNK : (c + 1) * CHUNK, :] = gath_ref[c].astype(F32) * scale
        gout_ref[c * CHUNK : (c + 1) * CHUNK, :] = gath_ref[8 + c].astype(F32) * scale
    ext = ext_ref[...] * scale
    b_ref[...] = ext[0:1].reshape(H)
    for i in range(3):
        hyp_ref[i] = jnp.sum(ext[1:2, i : i + 1])
    for s in range(BPD):
        ll_ref[s] = ll_in[s]


VM = pl.BlockSpec(memory_space=pltpu.VMEM)
SM = pl.BlockSpec(memory_space=pltpu.SMEM)
DMA = pltpu.SemaphoreType.DMA


def shards(
    inputs, responses, point_slot, block_home, nbr_ids, nbr_count, w_in, b_in, w_out, kernel_params
):
    loglik, grad, gath, ext = pl.pallas_call(
        main_kernel,
        out_shape=(
            jax.ShapeDtypeStruct((BPD,), F32),
            jax.ShapeDtypeStruct((ROWS, H), F32),
            jax.ShapeDtypeStruct((GROUP, CHUNK, H), BF16),
            jax.ShapeDtypeStruct((8, H), F32),
        ),
        in_specs=[VM] * 6 + [SM] * 4,
        out_specs=(SM, VM, VM, VM),
        scratch_shapes=[
            pltpu.VMEM((WIN + 1, ROWS, H), BF16),
            pltpu.VMEM(((WIN + 1) * BPD, 16, H), BF16),
            pltpu.VMEM(((WIN + 1) * BPD, BS, H), BF16),
            pltpu.VMEM((WIN + 1, ROWS, H), BF16),
            pltpu.VMEM((WIN + 1, ROWS, H), F32),
            pltpu.VMEM((BPD, N, H), BF16),
            pltpu.VMEM((BPD, N, N), F32),
            pltpu.VMEM((BPD, N, N), F32),
            pltpu.VMEM(((WIN + 1) * BPD, BS, H), F32),
            pltpu.VMEM((WIN, ROWS, H), BF16),
            pltpu.VMEM((WIN, ROWS, H), BF16),
            pltpu.VMEM((GROUP, CHUNK + 8, H), F32),
            pltpu.VMEM((GROUP, CHUNK + 8, H), F32),
            pltpu.VMEM((2, CHUNK + 8, H), F32),
            pltpu.VMEM((DEPTH, CHUNK + 8, H), F32),
            pltpu.VMEM((BPD, BS, B), F32),
            pltpu.VMEM((BPD, 8, B), F32),
        ]
        + [DMA((WIN + 1,))] * 6
        + [DMA((GROUP,))] * 6
        + [DMA, DMA],
        compiler_params=pltpu.CompilerParams(
            collective_id=0, has_side_effects=True, vmem_limit_bytes=60 * 1024 * 1024
        ),
        name="vecchia_main",
    )(
        inputs, responses, point_slot, w_in, b_in, w_out,
        block_home, nbr_ids, nbr_count, kernel_params,
    )
    loglik, feature_grad, g_in, g_b, g_out, hyper = pl.pallas_call(
        finish_kernel,
        out_shape=(
            jax.ShapeDtypeStruct((BPD,), F32),
            jax.ShapeDtypeStruct((ROWS, H), F32),
            jax.ShapeDtypeStruct((H, H), F32),
            jax.ShapeDtypeStruct((H,), F32),
            jax.ShapeDtypeStruct((H, H), F32),
            jax.ShapeDtypeStruct((3,), F32),
        ),
        in_specs=[SM, VM, VM, VM],
        out_specs=(SM, VM, VM, VM, VM, SM),
        name="vecchia_finish",
    )(loglik, grad, gath, ext)
    return loglik, feature_grad, g_in, g_b, g_out, hyper


def solution(mesh):
    placed = (
        P(("region", "dev"), None),
        P(("region", "dev")),
        P(("region", "dev")),
        P(),
        P(("region", "dev"), None),
        P(("region", "dev")),
        P(),
        P(),
        P(),
        P(),
    )
    return jax.shard_map(
        shards,
        mesh=mesh,
        in_specs=placed,
        out_specs=(P(("region", "dev")), P(("region", "dev"), None), P(), P(), P(), P()),
        check_vma=False,
    )
```

```python
import math

import jax
import jax.numpy as jnp
from jax import lax
from jax.experimental import pallas as pl
from jax.experimental.pallas import tpu as pltpu
from jax.sharding import PartitionSpec as P

H = 128
BS = 96
BPD = 2
NMAX = 4
WIN = 3
ROWS = BPD * BS
B = 128
N = 4 * B
STEPS = 8
GROUP = 16
CHUNK = 16
DEPTH = 8

SQRT_THREE = math.sqrt(3.0)
LOG_TWO_PI = math.log(2.0 * math.pi)
MESH = pl.DeviceIdType.MESH
F32 = jnp.float32
BF16 = jnp.bfloat16


def dot(a, b, contract=((1,), (0,))):
    return lax.dot_general(a, b, (contract, ((), ())), preferred_element_type=F32)


NT = ((1,), (1,))
TN = ((0,), (0,))


def split2(a):
    hi = a.astype(BF16)
    return hi, (a - hi.astype(F32)).astype(BF16)


def split3(a):
    hi = a.astype(BF16)
    rest = a - hi.astype(F32)
    mid = rest.astype(BF16)
    return hi, mid, (rest - mid.astype(F32)).astype(BF16)


def lanes(*parts):
    return jnp.concatenate(parts, axis=1)


def rows_of(*parts):
    return jnp.concatenate(parts, axis=0)


def mul2(a, b):
    n = b.shape[1]
    pair = lanes(*split2(b))
    out = dot(lanes(*split2(a)), rows_of(pair, pair))
    return out[:, :n] + out[:, n:]


def mul3(a, b):
    ah, am, al = a if isinstance(a, tuple) else split3(a)
    bh, bm, bl = b if isinstance(b, tuple) else split3(b)
    n = bh.shape[1]
    pair = lanes(bh, bm)
    out = dot(lanes(ah, am), rows_of(pair, pair))
    low = dot(lanes(ah, al), rows_of(bl, bh))
    return out[:, :n] + (out[:, n:] + low)


def mul3_nt(a, b):
    ah, am, al = a
    bh, bm, bl = b
    n = bh.shape[0]
    pair = rows_of(bh, bm)
    out = dot(lanes(ah, am), lanes(pair, pair), NT)
    low = dot(lanes(ah, al), lanes(bl, bh), NT)
    return out[:, :n] + (out[:, n:] + low)


def eye_of(n):
    return (
        lax.broadcasted_iota(jnp.int32, (n, n), 0) == lax.broadcasted_iota(jnp.int32, (n, n), 1)
    ).astype(F32)


def inverses(mats, eye, coef, scales, below=None):
    res = [eye - coef * a for a in mats]
    inv = [(scales[0] * coef) * (eye + r) for r in res]
    res = [(1.0 - scales[0]) * eye + scales[0] * mul3(r, r) for r in res]
    for j in range(1, STEPS - 1):
        s = scales[j]
        both = [mul3(rows_of(r, x), r) for x, r in zip(inv, res)]
        if below is not None and j == STEPS - 2:
            panel = [mul3(b, x) for b, x in zip(below, inv)]
            panel = [s * (p + mul3(p, r)) for p, r in zip(panel, res)]
        inv = [s * (x + b[B:]) for x, b in zip(inv, both)]
        res = [(1.0 - s) * eye + s * b[:B] for b in both]
    s = scales[-1]
    parts = [split3(r) for r in res]
    if below is not None:
        panel = [s * (p + mul3(p, r)) for p, r in zip(panel, parts)]
    inv = [s * (x + mul3(x, r)) for x, r in zip(inv, parts)]
    return inv if below is None else (inv, panel)


def device(index):
    per = lax.axis_size("dev")
    return (index // per, index % per)


def my_index():
    return lax.axis_index("region") * lax.axis_size("dev") + lax.axis_index("dev")


def network(x, w_in, b_in, w_out):
    pre = dot(x, w_in) + b_in
    sig = 1.0 / (1.0 + jnp.exp(-pre))
    hidden = (pre * sig).astype(BF16)
    return pre, sig, hidden


def one_hot(point_slot, rows, first):
    slot = lax.broadcasted_iota(jnp.int32, (rows, ROWS), 0) + first
    return (slot == point_slot).astype(F32).astype(BF16)


def block(ref, s, a, b):
    return ref[s, a * B : (a + 1) * B, b * B : (b + 1) * B]


def member_windows(me, home_ref, ids_ref, cnt_ref, s):
    places = []
    for k in range(NMAX):
        slot = home_ref[ids_ref[s, k]]
        live = k < cnt_ref[s]
        w = jnp.where(live, (me - slot // BPD) * BPD + slot % BPD, 0)
        places.append((jnp.clip(w, 0, (WIN + 1) * BPD - 1), jnp.where(live, 1.0, 0.0)))
    return places


def kernel_matrix(s, count, places, feat_ref, resp_ref, z_ref, e_ref, k_ref, inv_sq, var, nug, eye):
    lane1 = lax.broadcasted_iota(jnp.int32, (1, B), 1)
    y_row = jnp.zeros((1, N), F32)
    for k, (w, flag) in enumerate(places + [(s, None)]):
        member = feat_ref[w]
        resp = jnp.where(lane1 < BS, resp_ref[w][0:1].astype(F32), 0.0)
        if flag is not None:
            member = (member.astype(F32) * flag).astype(BF16)
            resp = resp * flag
        z_ref[s, k * BS : (k + 1) * BS, :] = member
        resp = lanes(resp, jnp.zeros((1, N - B), F32))
        y_row = y_row + (pltpu.roll(resp, k * BS, 1) if k else resp)
    z_ref[s, (NMAX + 1) * BS :, :] = jnp.zeros((N - (NMAX + 1) * BS, H), BF16)
    z = z_ref[s]
    gram = dot(z, z, NT)
    diag = [jnp.where(eye > 0.0, gram[i * B : (i + 1) * B, i * B : (i + 1) * B], 0.0) for i in range(4)]
    sq_row = lanes(*[jnp.sum(d, axis=0, keepdims=True) for d in diag])
    col_id = lax.broadcasted_iota(jnp.int32, (1, N), 1)
    own = (col_id >= NMAX * BS) & (col_id < (NMAX + 1) * BS)
    v_row = jnp.where((col_id < count * BS) | own, 1.0, 0.0)
    for i in range(4):
        row_id = lax.broadcasted_iota(jnp.int32, (B, 1), 0) + i * B
        own = (row_id >= NMAX * BS) & (row_id < (NMAX + 1) * BS)
        v_col = jnp.where((row_id < count * BS) | own, 1.0, 0.0)
        sq_col = jnp.sum(diag[i], axis=1, keepdims=True)
        mine = slice(i * B, (i + 1) * B)
        for c in range(0, B, 32):
            part = slice(c, c + 32)
            out = slice(i * B + c, i * B + c + 32)
            d2 = jnp.maximum(sq_col[part] + sq_row - 2.0 * gram[out], 0.0)
            r2 = d2 * inv_sq + 1e-06
            rad = SQRT_THREE * (r2 * lax.rsqrt(r2))
            e = jnp.exp(-rad) * (v_col[part] * v_row)
            e_ref[s, out, :] = e
            wide = (i + 1) * B
            kern = var * (1.0 + rad[:, :wide]) * e[:, :wide]
            spot = kern[:, i * B :] + eye[part] * (nug * v_col[part] + 1.0 - v_col[part])
            k_ref[s, out, :wide] = lanes(kern[:, : i * B], spot) if i else spot
    k_ref[s, 3 * B + BS : 3 * B + BS + 1, :] = y_row


def eliminate(both, k_ref, eye, coef, scales):
    invs = []
    for i in range(3):
        lo = (i + 1) * B
        cols = slice(i * B, lo)
        below = [split3(k_ref[s, lo:, cols]) for s in both]
        cur, panel = inverses([block(k_ref, s, i, i) for s in both], eye, coef, scales, below)
        invs.append([split3(c) for c in cur])
        panel = [split3(p) for p in panel]
        for b in range(i + 1, 4):
            first = (b - i - 1) * B
            for s in both:
                at = slice(b * B, (b + 1) * B)
                k_ref[s, b * B :, at] = k_ref[s, b * B :, at] - mul3_nt(
                    tuple(p[first:] for p in panel[s]), tuple(p[first : first + B] for p in below[s])
                )
    return invs


def joint_gradient(s, invs, s_inv, resid, z_ref, e_ref, k_ref, var, inv_sq, nug, eye, real):
    sub = lax.broadcasted_iota(jnp.int32, (B, B), 0)
    lane = lax.broadcasted_iota(jnp.int32, (B, B), 1)
    x3 = mul3(block(k_ref, s, 3, 2), invs[2][s])
    p3 = split3(x3)
    x2 = mul3(block(k_ref, s, 3, 1) - mul3(p3, block(k_ref, s, 2, 1)), invs[1][s])
    p2 = split3(x2)
    t1 = block(k_ref, s, 3, 0) - mul3(p3, block(k_ref, s, 2, 0)) - mul3(p2, block(k_ref, s, 1, 0))
    x1 = mul3(t1, invs[0][s])
    sign = jnp.where(lax.broadcasted_iota(jnp.int32, (B, 1), 0) < BS, -1.0, 1.0)
    ys = [x1 * sign, x2 * sign, x3 * sign]
    own = jnp.where(real, eye, 0.0)
    beta_m = mul3(resid, s_inv)
    beta_row = beta_m[BS : BS + 1]
    beta_col = jnp.sum(eye * beta_row, axis=1, keepdims=True)
    mid = jnp.where(real, beta_col * beta_row - s_inv, 0.0) + beta_m
    mid = mid + jnp.where((lane == BS) & (sub < BS), beta_col, 0.0)
    quad = jnp.sum(jnp.sum(resid * beta_m, axis=0, keepdims=True), axis=1, keepdims=True)
    y = lanes(*ys, own)
    prod = mul2(mid, y)
    trace = jnp.sum(jnp.sum(prod * y, axis=0, keepdims=True), axis=1, keepdims=True)
    t2 = 0.5 * nug * trace
    t1 = 0.5 * quad - 0.5 * BS - t2
    w = rows_of(*[m.T for m in ys])
    g = mul2(w, prod)
    low = jnp.where(lax.broadcasted_iota(jnp.int32, (B, 1), 0) < BS, prod, 0.0)
    high, rest = split2(rows_of(g * e_ref[s, : 3 * B, :], low * e_ref[s, 3 * B :, :]))
    z = z_ref[s]
    rhs = lanes(z, jnp.ones_like(z))
    pz = dot(high, rhs) + dot(rest, rhs)
    zf = z.astype(F32)
    grad = (3.0 * var * inv_sq) * (pz[:, :H] - pz[:, H:] * zf)
    t0 = -jnp.sum(jnp.sum(grad * zf, axis=0, keepdims=True), axis=1, keepdims=True)
    lane1 = lax.broadcasted_iota(jnp.int32, (1, B), 1)
    hyper = jnp.where(lane1 == 0, t0, 0.0) + jnp.where(lane1 == 1, t1, 0.0)
    return grad, hyper + jnp.where(lane1 == 2, t2, 0.0), quad


def pivot_steps(mat_ref, log_ref, first, last):
    mats = [mat_ref[i, first:BS, :] for i in range(BPD)]
    logdets = [log_ref[i, 0:1, 0:1] for i in range(BPD)]
    for k in range(first, last):
        for i, mat in enumerate(mats):
            at = k - (BS - mat.shape[0])
            row = mat[at : at + 1]
            pivot = row[:, k : k + 1]
            logdets[i] = logdets[i] + jnp.log(pivot)
            if k < BS - 1:
                if (k + 1) % 8 == 0:
                    mat = mat[8:]
                mats[i] = mat - mat[:, k : k + 1] * (row / pivot)
    for i in range(BPD):
        log_ref[i, 0:1, :] = jnp.broadcast_to(logdets[i], (1, B))
        if last < BS:
            mat_ref[i, last:BS, :] = mats[i]


def main_kernel(
    x_in, resp_in, ps_in, w_in_in, b_in, w_out_in, home_ref, ids_ref, cnt_ref, par_ref,
    ll_ref, fg_out, gath, ext_out,
    x_ref, resp_ref, ps_ref, w_in_ref, b_ref, w_out_ref,
    fg_ref, mine_ref, ext_ref, in_sem, out_sem,
    win_ref, wresp_ref, feat_ref, hid_ref, dsil_ref, z_ref, e_ref, k_ref, gw_ref,
    out_buf, in_buf, part, part_in, pair, red_in, mat_ref, log_ref,
    f_send, f_recv, g_send, g_recv, s1, r1, s2, r2, s3, r3, c_send, c_recv,
):
    total = lax.axis_size("region") * lax.axis_size("dev")
    region, dev = lax.axis_index("region"), lax.axis_index("dev")
    me = my_index()
    x, core, y, z = region // 2, region % 2, dev // DEPTH, dev % DEPTH
    ga = x * 4 + y

    def mate_a(k):
        other = lax.rem(ga + k, GROUP)
        return other, ((other // 4) * 2 + core, (other % 4) * DEPTH + z)

    def send(src, dst, ssem, rsem, place):
        copy = pltpu.make_async_remote_copy(
            src_ref=src, dst_ref=dst, send_sem=ssem, recv_sem=rsem, device_id=place, device_id_type=MESH
        )
        copy.start()
        return copy

    def later(k):
        return device(lax.rem(me + k + total, total))

    ops = (x_in, resp_in, ps_in, w_in_in, b_in, w_out_in)
    refs = (x_ref, resp_ref, ps_ref, w_in_ref, b_ref, w_out_ref)
    loads = [pltpu.make_async_copy(a, b, in_sem.at[i]) for i, (a, b) in enumerate(zip(ops, refs))]
    for c in loads:
        c.start()
    barrier = pltpu.get_barrier_semaphore()
    for k in range(1, WIN + 1):
        pl.semaphore_signal(barrier, inc=1, device_id=later(k), device_id_type=MESH)
        pl.semaphore_signal(barrier, inc=1, device_id=later(-k), device_id_type=MESH)
    for k in range(1, GROUP):
        pl.semaphore_signal(barrier, inc=1, device_id=mate_a(k)[1], device_id_type=MESH)
    for k in range(1, DEPTH):
        place = (region, y * DEPTH + lax.rem(z + k, DEPTH))
        pl.semaphore_signal(barrier, inc=1, device_id=place, device_id_type=MESH)
    pl.semaphore_signal(barrier, inc=1, device_id=(x * 2 + 1 - core, dev), device_id_type=MESH)

    for c in loads:
        c.wait()
    point_slot = ps_ref[...].reshape(1, ROWS)
    win_ref[0, :ROWS, :] = dot(one_hot(point_slot, ROWS, 0), x_ref[...]).astype(BF16)
    resp = jnp.broadcast_to(resp_ref[...].astype(F32).reshape(1, ROWS), (16, ROWS)).astype(BF16)
    win_ref[0, ROWS : ROWS + 16, :] = dot(resp, one_hot(point_slot, B, 0), NT).astype(BF16)
    win_ref[0, ROWS + 16 :, :] = dot(resp, one_hot(point_slot, B, BS), NT).astype(BF16)
    pl.semaphore_wait(barrier, 2 * WIN + GROUP + DEPTH - 1)

    def shift(src, dst, cut, sem, k):
        at = pl.ds(cut.start, cut.stop - cut.start)
        return send(win_ref.at[src, at], win_ref.at[dst, at], f_send.at[sem], f_recv.at[sem], later(k))

    cuts = [slice(0, 64), slice(64, 128), slice(128, ROWS + 32)]
    two = [shift(0, 2, cut, q, 2) for q, cut in enumerate(cuts)]
    one = shift(0, 1, slice(0, ROWS + 32), 3, 1)

    def forward(d):
        pre, sig, hidden = network(win_ref[d, :ROWS, :], w_in_ref[...], b_ref[...].reshape(1, H), w_out_ref[...])
        hid_ref[d] = hidden
        dsil_ref[d] = sig * (1.0 + pre * (1.0 - sig))
        feats = dot(hidden, w_out_ref[...]).astype(BF16)
        feat_ref[2 * d] = feats[:BS]
        feat_ref[2 * d + 1] = feats[BS:]
        for b in range(BPD):
            wresp_ref[2 * d + b] = win_ref[d, ROWS + 16 * b : ROWS + 16 * (b + 1), :]

    forward(0)

    def const(v):
        return jnp.full((1, 1), v, F32)

    inv_sq = jnp.exp(-2.0 * const(par_ref[0]))
    var = jnp.exp(const(par_ref[1]))
    nug = jnp.exp(const(par_ref[2]))
    eye = eye_of(B)
    lane = lax.broadcasted_iota(jnp.int32, (B, B), 1)
    sub = lax.broadcasted_iota(jnp.int32, (B, B), 0)
    top = B * var + 1.0
    coef = 2.0 / (top + nug)
    delta = (top - nug) / (top + nug)
    scales = []
    for _ in range(STEPS):
        sq = delta * delta
        scales.append(2.0 / (2.0 - sq))
        delta = sq / (2.0 - sq)
    both = range(BPD)
    places = [member_windows(me, home_ref, ids_ref, cnt_ref, s) for s in both]
    three = []
    for q, cut in enumerate(cuts):
        two[q].wait()
        three.append(shift(2, 3, cut, 4 + q, 1))
    forward(2)
    one.wait()
    forward(1)
    for c in three:
        c.wait()
    forward(3)

    for s in both:
        kernel_matrix(
            s, cnt_ref[s], places[s], feat_ref, wresp_ref, z_ref, e_ref, k_ref, inv_sq, var, nug, eye
        )
    invs = eliminate(both, k_ref, eye, coef, scales)
    real = (lane < BS) & (sub < BS)
    last = [block(k_ref, s, 3, 3) for s in both]
    resid = [jnp.where((sub == BS) & (lane < BS), m, 0.0) for m in last]
    schur = [jnp.where(real, m, eye) for m in last]
    s_inv = inverses(schur, eye, coef, scales)
    for s in both:
        mat_ref[s] = schur[s][:BS]
    grads, hypers, quads = [], [], []
    for s in both:
        grad, hyper, quad = joint_gradient(
            s, invs, s_inv[s], resid[s], z_ref, e_ref, k_ref, var, inv_sq, nug, eye, real
        )
        grads.append(grad)
        hypers.append(hyper)
        quads.append(quad)
    for w in range((WIN + 1) * BPD):
        acc = grads[w][NMAX * BS : (NMAX + 1) * BS] if w < BPD else jnp.zeros((BS, H), F32)
        for s in both:
            if w == 1 or (w == 0 and s == 0):
                continue
            for k in range(NMAX):
                place, flag = places[s][k]
                acc = acc + jnp.where(place == w, flag, 0.0) * grads[s][k * BS : (k + 1) * BS]
        gw_ref[w] = acc
        if w >= BPD:
            out_buf[w // BPD - 1, (w % BPD) * BS : (w % BPD + 1) * BS, :] = acc.astype(BF16)
    returns = [
        send(out_buf.at[k - 1], in_buf.at[k - 1], g_send.at[k], g_recv.at[k], later(-k))
        for k in range(1, WIN + 1)
    ]

    w_in_part = jnp.zeros((H, 2 * H), F32)
    w_out_part = jnp.zeros((H, 2 * H), F32)
    b_part = jnp.zeros((1, H), F32)
    for d in range(WIN + 1):
        hi, lo = split2(rows_of(gw_ref[2 * d], gw_ref[2 * d + 1]))
        back = dot(hi, w_out_ref[...], NT) + dot(lo, w_out_ref[...], NT)
        dpre = back * dsil_ref[d]
        w_out_part = w_out_part + dot(hid_ref[d], lanes(hi, lo), TN)
        w_in_part = w_in_part + dot(win_ref[d, :ROWS, :], lanes(*split2(dpre)), TN)
        b_part = b_part + jnp.sum(dpre, axis=0, keepdims=True)
    w_in_part = w_in_part[:, :H] + w_in_part[:, H:]
    w_out_part = w_out_part[:, :H] + w_out_part[:, H:]
    row8 = lax.broadcasted_iota(jnp.int32, (8, H), 0)
    for s in both:
        log_ref[s] = jnp.where(row8 == 1, quads[s], 0.0)
    small = jnp.where(row8 == 0, b_part, 0.0) + jnp.where(row8 == 1, hypers[0] + hypers[1], 0.0)
    for c in range(GROUP):
        src = w_in_part if c < 8 else w_out_part
        part[c, :CHUNK, :] = src[(c % 8) * CHUNK : (c % 8 + 1) * CHUNK]
        part[c, CHUNK:, :] = small
    copies = []
    for k in range(1, GROUP):
        other, place = mate_a(k)
        copies.append(send(part.at[other], part_in.at[ga], s1.at[k], r1.at[k], place))
    part_in[ga] = part[ga]

    @pl.when(dev >= 0)
    def _():
        pivot_steps(mat_ref, log_ref, 0, 32)

    for c in copies:
        c.wait()
    acc = part_in[0]
    for c in range(1, GROUP):
        acc = acc + part_in[c]
    pair[core] = acc
    copy = send(pair.at[core], pair.at[core], c_send, c_recv, (x * 2 + 1 - core, dev))
    copy.wait()
    red_in[z] = pair[0] + pair[1]
    copies = []
    for k in range(1, DEPTH):
        place = (region, y * DEPTH + lax.rem(z + k, DEPTH))
        copies.append(send(red_in.at[z], red_in.at[z], s2.at[k], r2.at[k], place))

    @pl.when(dev >= 0)
    def _():
        pivot_steps(mat_ref, log_ref, 32, 64)

    for c in copies:
        c.wait()
    acc = red_in[0]
    for c in range(1, DEPTH):
        acc = acc + red_in[c]
    mine_ref[...] = acc[:CHUNK].astype(BF16)
    ext_ref[...] = acc[CHUNK:]
    copies = []
    for k in range(1, GROUP):
        copies.append(send(mine_ref, gath.at[ga], s3.at[k], r3.at[k], mate_a(k)[1]))
    stores = [
        pltpu.make_async_copy(mine_ref, gath.at[ga], out_sem.at[0]),
        pltpu.make_async_copy(ext_ref, ext_out, out_sem.at[1]),
        pltpu.make_async_copy(fg_ref, fg_out, out_sem.at[2]),
    ]
    stores[0].start()
    stores[1].start()

    @pl.when(dev >= 0)
    def _():
        pivot_steps(mat_ref, log_ref, 64, BS)
        for s in both:
            ll = -0.5 * (log_ref[s, 0:1, 0:1] + log_ref[s, 1:2, 0:1]) * (1.0 / BS) - 0.5 * LOG_TWO_PI
            ll_ref[s] = jnp.sum(ll)

    for c in returns:
        c.wait()
    grad = rows_of(gw_ref[0], gw_ref[1])
    for k in range(WIN):
        grad = grad + in_buf[k].astype(F32)
    perm = one_hot(ps_ref[...].reshape(1, ROWS), ROWS, 0)
    pairs = dot(perm, lanes(*split2(grad)), TN)
    fg_ref[...] = pairs[:, :H] + pairs[:, H:]
    stores[2].start()
    for c in copies + stores:
        c.wait()


def finish_kernel(ll_in, grad_ref, gath_ref, ext_ref, ll_ref, fg_ref, gin_ref, b_ref, gout_ref, hyp_ref):
    scale = 1.0 / (lax.axis_size("region") * lax.axis_size("dev") * ROWS)
    fg_ref[...] = grad_ref[...]
    for c in range(8):
        gin_ref[c * CHUNK : (c + 1) * CHUNK, :] = gath_ref[c].astype(F32) * scale
        gout_ref[c * CHUNK : (c + 1) * CHUNK, :] = gath_ref[8 + c].astype(F32) * scale
    ext = ext_ref[...] * scale
    b_ref[...] = ext[0:1].reshape(H)
    for i in range(3):
        hyp_ref[i] = jnp.sum(ext[1:2, i : i + 1])
    for s in range(BPD):
        ll_ref[s] = ll_in[s]


VM = pl.BlockSpec(memory_space=pltpu.VMEM)
SM = pl.BlockSpec(memory_space=pltpu.SMEM)
ANY = pl.BlockSpec(memory_space=pl.ANY)
DMA = pltpu.SemaphoreType.DMA


def shards(
    inputs, responses, point_slot, block_home, nbr_ids, nbr_count, w_in, b_in, w_out, kernel_params
):
    loglik, grad, gath, ext = pl.pallas_call(
        main_kernel,
        out_shape=(
            jax.ShapeDtypeStruct((BPD,), F32),
            jax.ShapeDtypeStruct((ROWS, H), F32),
            jax.ShapeDtypeStruct((GROUP, CHUNK, H), BF16),
            jax.ShapeDtypeStruct((8, H), F32),
        ),
        in_specs=[ANY] * 6 + [SM] * 4,
        out_specs=(SM, ANY, ANY, ANY),
        scratch_shapes=[
            pltpu.VMEM((ROWS, H), BF16),
            pltpu.VMEM((ROWS,), BF16),
            pltpu.VMEM((ROWS,), jnp.int32),
            pltpu.VMEM((H, H), BF16),
            pltpu.VMEM((H,), F32),
            pltpu.VMEM((H, H), BF16),
            pltpu.VMEM((ROWS, H), F32),
            pltpu.VMEM((CHUNK, H), BF16),
            pltpu.VMEM((8, H), F32),
            DMA((6,)),
            DMA((3,)),
            pltpu.VMEM((WIN + 1, ROWS + 32, H), BF16),
            pltpu.VMEM(((WIN + 1) * BPD, 16, H), BF16),
            pltpu.VMEM(((WIN + 1) * BPD, BS, H), BF16),
            pltpu.VMEM((WIN + 1, ROWS, H), BF16),
            pltpu.VMEM((WIN + 1, ROWS, H), F32),
            pltpu.VMEM((BPD, N, H), BF16),
            pltpu.VMEM((BPD, N, N), F32),
            pltpu.VMEM((BPD, N, N), F32),
            pltpu.VMEM(((WIN + 1) * BPD, BS, H), F32),
            pltpu.VMEM((WIN, ROWS, H), BF16),
            pltpu.VMEM((WIN, ROWS, H), BF16),
            pltpu.VMEM((GROUP, CHUNK + 8, H), F32),
            pltpu.VMEM((GROUP, CHUNK + 8, H), F32),
            pltpu.VMEM((2, CHUNK + 8, H), F32),
            pltpu.VMEM((DEPTH, CHUNK + 8, H), F32),
            pltpu.VMEM((BPD, BS, B), F32),
            pltpu.VMEM((BPD, 8, B), F32),
        ]
        + [DMA((8,))] * 2
        + [DMA((WIN + 1,))] * 2
        + [DMA((GROUP,))] * 6
        + [DMA, DMA],
        compiler_params=pltpu.CompilerParams(
            collective_id=0, has_side_effects=True, vmem_limit_bytes=60 * 1024 * 1024
        ),
        name="vecchia_main",
    )(
        inputs, responses, point_slot, w_in, b_in, w_out,
        block_home, nbr_ids, nbr_count, kernel_params,
    )
    loglik, feature_grad, g_in, g_b, g_out, hyper = pl.pallas_call(
        finish_kernel,
        out_shape=(
            jax.ShapeDtypeStruct((BPD,), F32),
            jax.ShapeDtypeStruct((ROWS, H), F32),
            jax.ShapeDtypeStruct((H, H), F32),
            jax.ShapeDtypeStruct((H,), F32),
            jax.ShapeDtypeStruct((H, H), F32),
            jax.ShapeDtypeStruct((3,), F32),
        ),
        in_specs=[SM, VM, VM, VM],
        out_specs=(SM, VM, VM, VM, VM, SM),
        name="vecchia_finish",
    )(loglik, grad, gath, ext)
    return loglik, feature_grad, g_in, g_b, g_out, hyper


def solution(mesh):
    placed = (
        P(("region", "dev"), None),
        P(("region", "dev")),
        P(("region", "dev")),
        P(),
        P(("region", "dev"), None),
        P(("region", "dev")),
        P(),
        P(),
        P(),
        P(),
    )
    return jax.shard_map(
        shards,
        mesh=mesh,
        in_specs=placed,
        out_specs=(P(("region", "dev")), P(("region", "dev"), None), P(), P(), P(), P()),
        check_vma=False,
    )
```

```python
import math

import jax
import jax.numpy as jnp
from jax import lax
from jax.experimental import pallas as pl
from jax.experimental.pallas import tpu as pltpu
from jax.sharding import PartitionSpec as P

H = 128
BS = 96
BPD = 2
NMAX = 4
WIN = 3
ROWS = BPD * BS
B = 128
N = 4 * B
STEPS = 8
GROUP = 16
CHUNK = 16
DEPTH = 8

SQRT_THREE = math.sqrt(3.0)
LOG_TWO_PI = math.log(2.0 * math.pi)
MESH = pl.DeviceIdType.MESH
F32 = jnp.float32
BF16 = jnp.bfloat16


def dot(a, b, contract=((1,), (0,))):
    return lax.dot_general(a, b, (contract, ((), ())), preferred_element_type=F32)


NT = ((1,), (1,))
TN = ((0,), (0,))


def split2(a):
    hi = a.astype(BF16)
    return hi, (a - hi.astype(F32)).astype(BF16)


def split3(a):
    hi = a.astype(BF16)
    rest = a - hi.astype(F32)
    mid = rest.astype(BF16)
    return hi, mid, (rest - mid.astype(F32)).astype(BF16)


def lanes(*parts):
    return jnp.concatenate(parts, axis=1)


def rows_of(*parts):
    return jnp.concatenate(parts, axis=0)


def mul2(a, b):
    n = (b[0] if isinstance(b, tuple) else b).shape[1]
    pair = lanes(*(b if isinstance(b, tuple) else split2(b)))
    out = dot(lanes(*split2(a)), rows_of(pair, pair))
    return out[:, :n] + out[:, n:]


def mul3(a, b):
    ah, am, al = a if isinstance(a, tuple) else split3(a)
    bh, bm, bl = b if isinstance(b, tuple) else split3(b)
    n = bh.shape[1]
    pair = lanes(bh, bm)
    out = dot(lanes(ah, am), rows_of(pair, pair))
    low = dot(lanes(ah, al), rows_of(bl, bh))
    return out[:, :n] + (out[:, n:] + low)


def mul3_nt(a, b):
    ah, am, al = a
    bh, bm, bl = b
    n = bh.shape[0]
    pair = rows_of(bh, bm)
    out = dot(lanes(ah, am), lanes(pair, pair), NT)
    low = dot(lanes(ah, al), lanes(bl, bh), NT)
    return out[:, :n] + (out[:, n:] + low)


def eye_of(n):
    return (
        lax.broadcasted_iota(jnp.int32, (n, n), 0) == lax.broadcasted_iota(jnp.int32, (n, n), 1)
    ).astype(F32)


def inverses(mats, eye, scan, fill=()):
    coef, scales = scan
    fill = list(fill)
    share = -(-len(fill) // (STEPS - 2)) if fill else 0
    res = [eye - coef * a for a in mats]
    inv = [(scales[0] * coef) * (eye + r) for r in res]
    res = [(1.0 - scales[0]) * eye + scales[0] * mul3(r, r) for r in res]
    for j in range(1, STEPS - 1):
        s = scales[j]
        mul = mul2 if j == STEPS - 2 else mul3
        both = [mul(rows_of(r, x), r) for x, r in zip(inv, res)]
        for work in fill[:share]:
            work()
        fill = fill[share:]
        inv = [s * (x + b[B:]) for x, b in zip(inv, both)]
        res = [(1.0 - s) * eye + s * b[:B] for b in both]
    s = scales[-1]
    return [s * x for x in inv], res


def device(index):
    per = lax.axis_size("dev")
    return (index // per, index % per)


def my_index():
    return lax.axis_index("region") * lax.axis_size("dev") + lax.axis_index("dev")


def network(x, w_in, b_in, w_out):
    pre = dot(x, w_in) + b_in
    sig = 1.0 / (1.0 + jnp.exp(-pre))
    hidden = (pre * sig).astype(BF16)
    return pre, sig, hidden


def one_hot(point_slot, rows, first):
    slot = lax.broadcasted_iota(jnp.int32, (rows, ROWS), 0) + first
    return (slot == point_slot).astype(F32).astype(BF16)


def block(ref, s, a, b):
    return ref[s, a * B : (a + 1) * B, b * B : (b + 1) * B]


def member_windows(me, home_ref, ids_ref, cnt_ref, s):
    places = []
    for k in range(NMAX):
        slot = home_ref[ids_ref[s, k]]
        live = k < cnt_ref[s]
        w = jnp.where(live, (me - slot // BPD) * BPD + slot % BPD, 0)
        places.append((jnp.clip(w, 0, (WIN + 1) * BPD - 1), jnp.where(live, 1.0, 0.0)))
    return places


def kernel_rows(s, count, places, feat_ref, resp_ref, z_ref, e_ref, k_ref, inv_sq, var, nug, eye):
    lane1 = lax.broadcasted_iota(jnp.int32, (1, B), 1)
    y_row = jnp.zeros((1, N), F32)
    for k, (w, flag) in enumerate(places + [(s, None)]):
        member = feat_ref[w]
        resp = jnp.where(lane1 < BS, resp_ref[w][0:1].astype(F32), 0.0)
        if flag is not None:
            member = (member.astype(F32) * flag).astype(BF16)
            resp = resp * flag
        z_ref[s, k * BS : (k + 1) * BS, :] = member
        resp = lanes(resp, jnp.zeros((1, N - B), F32))
        y_row = y_row + (pltpu.roll(resp, k * BS, 1) if k else resp)
    z_ref[s, (NMAX + 1) * BS :, :] = jnp.zeros((N - (NMAX + 1) * BS, H), BF16)
    z = z_ref[s]
    gram = dot(z, z, NT)
    e_ref[s] = gram
    diag = [jnp.where(eye > 0.0, gram[i * B : (i + 1) * B, i * B : (i + 1) * B], 0.0) for i in range(4)]
    sq_row = lanes(*[jnp.sum(d, axis=0, keepdims=True) for d in diag])
    sq_col = [jnp.sum(d, axis=1, keepdims=True) for d in diag]
    col_id = lax.broadcasted_iota(jnp.int32, (1, N), 1)
    own = (col_id >= NMAX * BS) & (col_id < (NMAX + 1) * BS)
    v_row = jnp.where((col_id < count * BS) | own, 1.0, 0.0)

    def piece(i, c):
        part = slice(c, c + 32)
        out = slice(i * B + c, i * B + c + 32)
        row_id = lax.broadcasted_iota(jnp.int32, (32, 1), 0) + (i * B + c)
        own = (row_id >= NMAX * BS) & (row_id < (NMAX + 1) * BS)
        v_col = jnp.where((row_id < count * BS) | own, 1.0, 0.0)
        d2 = jnp.maximum(sq_col[i][part] + sq_row - 2.0 * e_ref[s, out, :], 0.0)
        r2 = d2 * inv_sq + 1e-06
        rad = SQRT_THREE * (r2 * lax.rsqrt(r2))
        e = jnp.exp(-rad) * (v_col * v_row)
        e_ref[s, out, :] = e
        wide = (i + 1) * B
        kern = var * (1.0 + rad[:, :wide]) * e[:, :wide]
        spot = kern[:, i * B :] + eye[part] * (nug * v_col + 1.0 - v_col)
        k_ref[s, out, :wide] = lanes(kern[:, : i * B], spot) if i else spot
        if i == 3 and c == BS:
            k_ref[s, 3 * B + BS : 3 * B + BS + 1, :] = y_row

    return [[lambda i=i, c=c: piece(i, c) for c in range(0, B, 32)] for i in range(4)]


def eliminate(both, k_ref, eye, scan, fill):
    invs = []
    for i in range(3):
        lo = (i + 1) * B
        cols = slice(i * B, lo)
        x, r = inverses([block(k_ref, s, i, i) for s in both], eye, scan, fill)
        fill = []
        below = [split3(k_ref[s, lo:, cols]) for s in both]
        panel = [mul3(below[s], x[s]) for s in both]
        panel = [split3(panel[s] + mul2(panel[s], r[s])) for s in both]
        invs.append([split3(x[s] + mul2(x[s], r[s])) for s in both])
        for b in range(i + 1, 4):
            first = (b - i - 1) * B
            for s in both:
                at = slice(b * B, (b + 1) * B)
                k_ref[s, b * B :, at] = k_ref[s, b * B :, at] - mul3_nt(
                    tuple(p[first:] for p in panel[s]), tuple(p[first : first + B] for p in below[s])
                )
    return invs, [block(k_ref, s, 3, 3) for s in both], []


def joint_gradients(both, invs, schur, resid, scan, fill, z_ref, e_ref, k_ref, var, inv_sq, nug, eye, real):
    sub = lax.broadcasted_iota(jnp.int32, (B, B), 0)
    lane = lax.broadcasted_iota(jnp.int32, (B, B), 1)
    lane1 = lax.broadcasted_iota(jnp.int32, (1, B), 1)
    sign = jnp.where(lax.broadcasted_iota(jnp.int32, (B, 1), 0) < BS, -1.0, 1.0)
    p3, p2, t1, x1, ys, w_pair = {}, {}, {}, {}, {}, {}

    def back(s, step):
        if step == 0:
            p3[s] = split3(mul3(block(k_ref, s, 3, 2), invs[2][s]))
        elif step == 1:
            p2[s] = block(k_ref, s, 3, 1) - mul3(p3[s], block(k_ref, s, 2, 1))
            t1[s] = block(k_ref, s, 3, 0) - mul3(p3[s], block(k_ref, s, 2, 0))
        elif step == 2:
            p2[s] = split3(mul3(p2[s], invs[1][s]))
        elif step == 3:
            t1[s] = t1[s] - mul3(p2[s], block(k_ref, s, 1, 0))
        elif step == 4:
            x1[s] = mul3(t1[s], invs[0][s])
        else:
            x2, x3 = [p[0].astype(F32) + (p[1].astype(F32) + p[2].astype(F32)) for p in (p2[s], p3[s])]
            ys[s] = lanes(x1[s] * sign, x2 * sign, x3 * sign)
            w = rows_of(*[ys[s][:, i * B : (i + 1) * B].T for i in range(3)])
            w_pair[s] = lanes(*split2(w))

    own = jnp.where(real, eye, 0.0)
    steps = [lambda s=s, step=step: back(s, step) for step in range(6) for s in both]
    x, r = inverses(schur, eye, scan, fill + steps)
    beta_m = [mul3(resid[s], x[s]) for s in both]
    beta_m = [beta_m[s] + mul2(beta_m[s], r[s]) for s in both]
    s_inv = [x[s] + mul2(x[s], r[s]) for s in both]
    y_parts = [split2(lanes(ys[s], own)) for s in both]
    beta_row = [m[BS : BS + 1] for m in beta_m]
    beta_col = [jnp.sum(eye * b, axis=1, keepdims=True) for b in beta_row]
    mid = [
        jnp.where(real, beta_col[s] * beta_row[s] - s_inv[s], 0.0)
        + beta_m[s]
        + jnp.where((lane == BS) & (sub < BS), beta_col[s], 0.0)
        for s in both
    ]
    prod = [mul2(mid[s], y_parts[s]) for s in both]
    pairs = [lanes(*split2(p)) for p in prod]
    g = [dot(w_pair[s], rows_of(pairs[s], pairs[s])) for s in both]
    below = lax.broadcasted_iota(jnp.int32, (B, 1), 0) < BS
    low = [jnp.where(below, prod[s], 0.0) for s in both]
    weights = [
        split2(rows_of((g[s][:, :N] + g[s][:, N:]) * e_ref[s, : 3 * B, :], low[s] * e_ref[s, 3 * B :, :]))
        for s in both
    ]
    rhs = [lanes(z_ref[s], jnp.ones((N, H), BF16)) for s in both]
    pz = [dot(weights[s][0], rhs[s]) + dot(weights[s][1], rhs[s]) for s in both]
    out = []
    for s in both:
        quad = jnp.sum(jnp.sum(resid[s] * beta_m[s], axis=0, keepdims=True), axis=1, keepdims=True)
        y = lanes(ys[s], own)
        trace = jnp.sum(jnp.sum(prod[s] * y, axis=0, keepdims=True), axis=1, keepdims=True)
        t2 = 0.5 * nug * trace
        t1 = 0.5 * quad - 0.5 * BS - t2
        zf = z_ref[s].astype(F32)
        grad = (3.0 * var * inv_sq) * (pz[s][:, :H] - pz[s][:, H:] * zf)
        t0 = -jnp.sum(jnp.sum(grad * zf, axis=0, keepdims=True), axis=1, keepdims=True)
        hyper = jnp.where(lane1 == 0, t0, 0.0) + jnp.where(lane1 == 1, t1, 0.0)
        out.append((grad, hyper + jnp.where(lane1 == 2, t2, 0.0), quad))
    return out


def pivot_steps(mat_ref, log_ref, first, last):
    mats = [mat_ref[i, first:BS, :] for i in range(BPD)]
    logdets = [log_ref[i, 0:1, 0:1] for i in range(BPD)]
    for k in range(first, last):
        for i, mat in enumerate(mats):
            at = k - (BS - mat.shape[0])
            row = mat[at : at + 1]
            pivot = row[:, k : k + 1]
            logdets[i] = logdets[i] + jnp.log(pivot)
            if k < BS - 1:
                if (k + 1) % 8 == 0:
                    mat = mat[8:]
                mats[i] = mat - mat[:, k : k + 1] * (row / pivot)
    for i in range(BPD):
        log_ref[i, 0:1, :] = jnp.broadcast_to(logdets[i], (1, B))
        if last < BS:
            mat_ref[i, last:BS, :] = mats[i]


def main_kernel(
    x_in, resp_in, ps_in, w_in_in, b_in, w_out_in, home_in, ids_in, cnt_in, par_in,
    ll_ref, hyp_ref, fg_out, gath, b_out,
    x_ref, resp_ref, ps_ref, w_in_ref, b_ref, w_out_ref, home_ref, ids_ref, cnt_ref, par_ref,
    fg_ref, mine_ref, bsum_ref, in_sem, out_sem,
    win_ref, wresp_ref, feat_ref, hid_ref, dsil_ref, z_ref, e_ref, k_ref, gw_ref,
    out_buf, in_buf, part, part_in, pair, red_in, mat_ref, log_ref,
    f_send, f_recv, g_send, g_recv, s1, r1, s2, r2, s3, r3, c_send, c_recv,
):
    total = lax.axis_size("region") * lax.axis_size("dev")
    region, dev = lax.axis_index("region"), lax.axis_index("dev")
    me = my_index()
    x, core, y, z = region // 2, region % 2, dev // DEPTH, dev % DEPTH
    ga = x * 4 + y

    def mate_a(k):
        other = lax.rem(ga + k, GROUP)
        return other, ((other // 4) * 2 + core, (other % 4) * DEPTH + z)

    def send(src, dst, ssem, rsem, place):
        copy = pltpu.make_async_remote_copy(
            src_ref=src, dst_ref=dst, send_sem=ssem, recv_sem=rsem, device_id=place, device_id_type=MESH
        )
        copy.start()
        return copy

    def later(k):
        return device(lax.rem(me + k + total, total))

    ops = (x_in, resp_in, ps_in, w_in_in, b_in, w_out_in, home_in, ids_in, cnt_in, par_in)
    refs = (x_ref, resp_ref, ps_ref, w_in_ref, b_ref, w_out_ref, home_ref, ids_ref, cnt_ref, par_ref)
    loads = [pltpu.make_async_copy(a, b, in_sem.at[i]) for i, (a, b) in enumerate(zip(ops, refs))]
    for c in loads:
        c.start()
    barrier = pltpu.get_barrier_semaphore()
    for k in range(1, WIN + 1):
        pl.semaphore_signal(barrier, inc=1, device_id=later(k), device_id_type=MESH)
        pl.semaphore_signal(barrier, inc=1, device_id=later(-k), device_id_type=MESH)
    for k in range(1, GROUP):
        pl.semaphore_signal(barrier, inc=1, device_id=mate_a(k)[1], device_id_type=MESH)
    for k in range(1, DEPTH):
        place = (region, y * DEPTH + lax.rem(z + k, DEPTH))
        pl.semaphore_signal(barrier, inc=1, device_id=place, device_id_type=MESH)
    pl.semaphore_signal(barrier, inc=1, device_id=(x * 2 + 1 - core, dev), device_id_type=MESH)

    for c in loads:
        c.wait()
    point_slot = ps_ref[...].reshape(1, ROWS)
    win_ref[0, :ROWS, :] = dot(one_hot(point_slot, ROWS, 0), x_ref[...]).astype(BF16)
    resp = jnp.broadcast_to(resp_ref[...].astype(F32).reshape(1, ROWS), (16, ROWS)).astype(BF16)
    win_ref[0, ROWS : ROWS + 16, :] = dot(resp, one_hot(point_slot, B, 0), NT).astype(BF16)
    win_ref[0, ROWS + 16 :, :] = dot(resp, one_hot(point_slot, B, BS), NT).astype(BF16)
    pl.semaphore_wait(barrier, 2 * WIN + GROUP + DEPTH - 1)

    def shift(src, dst, cut, sem, k):
        at = pl.ds(cut.start, cut.stop - cut.start)
        return send(win_ref.at[src, at], win_ref.at[dst, at], f_send.at[sem], f_recv.at[sem], later(k))

    cuts = [slice(0, 64), slice(64, 128), slice(128, ROWS + 32)]
    two = [shift(0, 2, cut, q, 2) for q, cut in enumerate(cuts)]
    one = shift(0, 1, slice(0, ROWS + 32), 3, 1)

    def forward(d):
        pre, sig, hidden = network(win_ref[d, :ROWS, :], w_in_ref[...], b_ref[...].reshape(1, H), w_out_ref[...])
        hid_ref[d] = hidden
        dsil_ref[d] = sig * (1.0 + pre * (1.0 - sig))
        feats = dot(hidden, w_out_ref[...]).astype(BF16)
        feat_ref[2 * d] = feats[:BS]
        feat_ref[2 * d + 1] = feats[BS:]
        for b in range(BPD):
            wresp_ref[2 * d + b] = win_ref[d, ROWS + 16 * b : ROWS + 16 * (b + 1), :]

    forward(0)

    def const(v):
        return jnp.full((1, 1), v, F32)

    inv_sq = jnp.exp(-2.0 * const(par_ref[0]))
    var = jnp.exp(const(par_ref[1]))
    nug = jnp.exp(const(par_ref[2]))
    eye = eye_of(B)
    lane = lax.broadcasted_iota(jnp.int32, (B, B), 1)
    sub = lax.broadcasted_iota(jnp.int32, (B, B), 0)
    top = B * var + 1.0
    coef = 2.0 / (top + nug)
    delta = (top - nug) / (top + nug)
    scales = []
    for _ in range(STEPS):
        sq = delta * delta
        scales.append(2.0 / (2.0 - sq))
        delta = sq / (2.0 - sq)
    both = range(BPD)
    places = [member_windows(me, home_ref, ids_ref, cnt_ref, s) for s in both]
    three = []
    for q, cut in enumerate(cuts):
        two[q].wait()
        three.append(shift(2, 3, cut, 4 + q, 1))
    forward(2)
    one.wait()
    forward(1)
    for c in three:
        c.wait()
    forward(3)

    rows = [
        kernel_rows(
            s, cnt_ref[s], places[s], feat_ref, wresp_ref, z_ref, e_ref, k_ref, inv_sq, var, nug, eye
        )
        for s in both
    ]
    for s in both:
        for work in rows[s][0]:
            work()
    fill = [work for i in range(1, 4) for s in both for work in rows[s][i]]
    scan = (coef, scales)
    invs, last, fill = eliminate(both, k_ref, eye, scan, fill)
    real = (lane < BS) & (sub < BS)
    resid = [jnp.where((sub == BS) & (lane < BS), m, 0.0) for m in last]
    schur = [jnp.where(real, m, eye) for m in last]
    for s in both:
        mat_ref[s] = schur[s][:BS]
    found = joint_gradients(
        both, invs, schur, resid, scan, fill, z_ref, e_ref, k_ref, var, inv_sq, nug, eye, real
    )
    grads, hypers, quads = [list(part) for part in zip(*found)]
    for w in range((WIN + 1) * BPD):
        acc = grads[w][NMAX * BS : (NMAX + 1) * BS] if w < BPD else jnp.zeros((BS, H), F32)
        for s in both:
            if w == 1 or (w == 0 and s == 0):
                continue
            for k in range(NMAX):
                place, flag = places[s][k]
                acc = acc + jnp.where(place == w, flag, 0.0) * grads[s][k * BS : (k + 1) * BS]
        gw_ref[w] = acc
        if w >= BPD:
            out_buf[w // BPD - 1, (w % BPD) * BS : (w % BPD + 1) * BS, :] = acc.astype(BF16)
    returns = [
        send(out_buf.at[k - 1], in_buf.at[k - 1], g_send.at[k], g_recv.at[k], later(-k))
        for k in range(1, WIN + 1)
    ]

    w_in_part = jnp.zeros((H, 2 * H), F32)
    w_out_part = jnp.zeros((H, 2 * H), F32)
    b_part = jnp.zeros((1, H), F32)
    for d in range(WIN + 1):
        hi, lo = split2(rows_of(gw_ref[2 * d], gw_ref[2 * d + 1]))
        back = dot(hi, w_out_ref[...], NT) + dot(lo, w_out_ref[...], NT)
        dpre = back * dsil_ref[d]
        w_out_part = w_out_part + dot(hid_ref[d], lanes(hi, lo), TN)
        w_in_part = w_in_part + dot(win_ref[d, :ROWS, :], lanes(*split2(dpre)), TN)
        b_part = b_part + jnp.sum(dpre, axis=0, keepdims=True)
    w_in_part = w_in_part[:, :H] + w_in_part[:, H:]
    w_out_part = w_out_part[:, :H] + w_out_part[:, H:]
    row8 = lax.broadcasted_iota(jnp.int32, (8, H), 0)
    for s in both:
        log_ref[s] = jnp.where(row8 == 1, quads[s], 0.0)
    small = jnp.where(row8 == 0, b_part, 0.0) + jnp.where(row8 == 1, hypers[0] + hypers[1], 0.0)
    for c in range(GROUP):
        src = w_in_part if c < 8 else w_out_part
        part[c, :CHUNK, :] = src[(c % 8) * CHUNK : (c % 8 + 1) * CHUNK]
        part[c, CHUNK:, :] = small
    copies = []
    for k in range(1, GROUP):
        other, place = mate_a(k)
        copies.append(send(part.at[other], part_in.at[ga], s1.at[k], r1.at[k], place))
    part_in[ga] = part[ga]

    @pl.when(dev >= 0)
    def _():
        pivot_steps(mat_ref, log_ref, 0, 32)

    for c in copies:
        c.wait()
    acc = part_in[0]
    for c in range(1, GROUP):
        acc = acc + part_in[c]
    pair[core] = acc
    copy = send(pair.at[core], pair.at[core], c_send, c_recv, (x * 2 + 1 - core, dev))
    copy.wait()
    red_in[z] = pair[0] + pair[1]
    copies = []
    for k in range(1, DEPTH):
        place = (region, y * DEPTH + lax.rem(z + k, DEPTH))
        copies.append(send(red_in.at[z], red_in.at[z], s2.at[k], r2.at[k], place))

    @pl.when(dev >= 0)
    def _():
        pivot_steps(mat_ref, log_ref, 32, 64)

    for c in copies:
        c.wait()
    acc = red_in[0]
    for c in range(1, DEPTH):
        acc = acc + red_in[c]
    acc = acc * (1.0 / (total * ROWS))
    mine_ref[...] = acc[:CHUNK]
    bsum_ref[...] = acc[CHUNK : CHUNK + 1].reshape(H)
    place = pl.ds(pl.multiple_of(ga * CHUNK, CHUNK), CHUNK)
    copies = []
    for k in range(1, GROUP):
        copies.append(send(mine_ref, gath.at[place], s3.at[k], r3.at[k], mate_a(k)[1]))
    stores = [
        pltpu.make_async_copy(mine_ref, gath.at[place], out_sem.at[0]),
        pltpu.make_async_copy(bsum_ref, b_out, out_sem.at[1]),
        pltpu.make_async_copy(fg_ref, fg_out, out_sem.at[2]),
    ]
    stores[0].start()
    stores[1].start()

    @pl.when(dev >= 0)
    def _():
        pivot_steps(mat_ref, log_ref, 64, BS)
        for s in both:
            ll = -0.5 * (log_ref[s, 0:1, 0:1] + log_ref[s, 1:2, 0:1]) * (1.0 / BS) - 0.5 * LOG_TWO_PI
            ll_ref[s] = jnp.sum(ll)
        for i in range(3):
            hyp_ref[i] = jnp.sum(acc[CHUNK + 1 : CHUNK + 2, i : i + 1])

    for c in returns:
        c.wait()
    grad = rows_of(gw_ref[0], gw_ref[1])
    for k in range(WIN):
        grad = grad + in_buf[k].astype(F32)
    perm = one_hot(ps_ref[...].reshape(1, ROWS), ROWS, 0)
    pairs = dot(perm, lanes(*split2(grad)), TN)
    fg_ref[...] = pairs[:, :H] + pairs[:, H:]
    stores[2].start()
    for c in copies + stores:
        c.wait()


def finish_kernel(ll_in, hyp_in, grad_in, weights_in, b_in, ll_out, fg_out, gin_out, b_out, gout_out, hyp_out):
    fg_out[...] = grad_in[...]
    gin_out[...] = weights_in[:H, :]
    gout_out[...] = weights_in[H:, :]
    b_out[...] = b_in[...]
    for s in range(BPD):
        ll_out[s] = ll_in[s]
    for i in range(3):
        hyp_out[i] = hyp_in[i]


VM = pl.BlockSpec(memory_space=pltpu.VMEM)
SM = pl.BlockSpec(memory_space=pltpu.SMEM)
ANY = pl.BlockSpec(memory_space=pl.ANY)
DMA = pltpu.SemaphoreType.DMA


def shards(
    inputs, responses, point_slot, block_home, nbr_ids, nbr_count, w_in, b_in, w_out, kernel_params
):
    loglik, hyper, grad, weights, bias = pl.pallas_call(
        main_kernel,
        out_shape=(
            jax.ShapeDtypeStruct((BPD,), F32),
            jax.ShapeDtypeStruct((3,), F32),
            jax.ShapeDtypeStruct((ROWS, H), F32),
            jax.ShapeDtypeStruct((GROUP * CHUNK, H), F32),
            jax.ShapeDtypeStruct((H,), F32),
        ),
        in_specs=[ANY] * 10,
        out_specs=(SM, SM, ANY, ANY, ANY),
        scratch_shapes=[
            pltpu.VMEM((ROWS, H), BF16),
            pltpu.VMEM((ROWS,), BF16),
            pltpu.VMEM((ROWS,), jnp.int32),
            pltpu.VMEM((H, H), BF16),
            pltpu.VMEM((H,), F32),
            pltpu.VMEM((H, H), BF16),
            pltpu.SMEM(block_home.shape, jnp.int32),
            pltpu.SMEM((BPD, NMAX), jnp.int32),
            pltpu.SMEM((BPD,), jnp.int32),
            pltpu.SMEM((3,), F32),
            pltpu.VMEM((ROWS, H), F32),
            pltpu.VMEM((CHUNK, H), F32),
            pltpu.VMEM((H,), F32),
            DMA((10,)),
            DMA((3,)),
            pltpu.VMEM((WIN + 1, ROWS + 32, H), BF16),
            pltpu.VMEM(((WIN + 1) * BPD, 16, H), BF16),
            pltpu.VMEM(((WIN + 1) * BPD, BS, H), BF16),
            pltpu.VMEM((WIN + 1, ROWS, H), BF16),
            pltpu.VMEM((WIN + 1, ROWS, H), F32),
            pltpu.VMEM((BPD, N, H), BF16),
            pltpu.VMEM((BPD, N, N), F32),
            pltpu.VMEM((BPD, N, N), F32),
            pltpu.VMEM(((WIN + 1) * BPD, BS, H), F32),
            pltpu.VMEM((WIN, ROWS, H), BF16),
            pltpu.VMEM((WIN, ROWS, H), BF16),
            pltpu.VMEM((GROUP, CHUNK + 8, H), F32),
            pltpu.VMEM((GROUP, CHUNK + 8, H), F32),
            pltpu.VMEM((2, CHUNK + 8, H), F32),
            pltpu.VMEM((DEPTH, CHUNK + 8, H), F32),
            pltpu.VMEM((BPD, BS, B), F32),
            pltpu.VMEM((BPD, 8, B), F32),
        ]
        + [DMA((8,))] * 2
        + [DMA((WIN + 1,))] * 2
        + [DMA((GROUP,))] * 6
        + [DMA, DMA],
        compiler_params=pltpu.CompilerParams(
            collective_id=0, has_side_effects=True, vmem_limit_bytes=60 * 1024 * 1024
        ),
        name="vecchia_main",
    )(
        inputs, responses, point_slot, w_in, b_in, w_out,
        block_home, nbr_ids, nbr_count, kernel_params,
    )
    loglik, feature_grad, g_in, g_b, g_out, hyper = pl.pallas_call(
        finish_kernel,
        out_shape=(
            jax.ShapeDtypeStruct((BPD,), F32),
            jax.ShapeDtypeStruct((ROWS, H), F32),
            jax.ShapeDtypeStruct((H, H), F32),
            jax.ShapeDtypeStruct((H,), F32),
            jax.ShapeDtypeStruct((H, H), F32),
            jax.ShapeDtypeStruct((3,), F32),
        ),
        in_specs=[SM, SM, VM, VM, VM],
        out_specs=(SM, VM, VM, VM, VM, SM),
        name="vecchia_finish",
    )(loglik, hyper, grad, weights, bias)
    return loglik, feature_grad, g_in, g_b, g_out, hyper


def solution(mesh):
    placed = (
        P(("region", "dev"), None),
        P(("region", "dev")),
        P(("region", "dev")),
        P(),
        P(("region", "dev"), None),
        P(("region", "dev")),
        P(),
        P(),
        P(),
        P(),
    )
    return jax.shard_map(
        shards,
        mesh=mesh,
        in_specs=placed,
        out_specs=(P(("region", "dev")), P(("region", "dev"), None), P(), P(), P(), P()),
        check_vma=False,
    )
```

```python
import math

import jax
import jax.numpy as jnp
from jax import lax
from jax.experimental import pallas as pl
from jax.experimental.pallas import tpu as pltpu
from jax.sharding import PartitionSpec as P

H = 128
BS = 96
BPD = 2
NMAX = 4
WIN = 3
ROWS = BPD * BS
B = 128
N = 4 * B
STEPS = 8
GROUP = 16
CHUNK = 16
DEPTH = 8

SQRT_THREE = math.sqrt(3.0)
LOG_TWO_PI = math.log(2.0 * math.pi)
MESH = pl.DeviceIdType.MESH
F32 = jnp.float32
BF16 = jnp.bfloat16


def dot(a, b, contract=((1,), (0,))):
    return lax.dot_general(a, b, (contract, ((), ())), preferred_element_type=F32)


NT = ((1,), (1,))
TN = ((0,), (0,))


def split2(a):
    hi = a.astype(BF16)
    return hi, (a - hi.astype(F32)).astype(BF16)


def split3(a):
    hi = a.astype(BF16)
    rest = a - hi.astype(F32)
    mid = rest.astype(BF16)
    return hi, mid, (rest - mid.astype(F32)).astype(BF16)


def lanes(*parts):
    return jnp.concatenate(parts, axis=1)


def rows_of(*parts):
    return jnp.concatenate(parts, axis=0)


def mul2(a, b):
    n = (b[0] if isinstance(b, tuple) else b).shape[1]
    pair = lanes(*(b if isinstance(b, tuple) else split2(b)))
    out = dot(lanes(*split2(a)), rows_of(pair, pair))
    return out[:, :n] + out[:, n:]


def mul3(a, b):
    ah, am, al = a if isinstance(a, tuple) else split3(a)
    bh, bm, bl = b if isinstance(b, tuple) else split3(b)
    n = bh.shape[1]
    pair = lanes(bh, bm)
    out = dot(lanes(ah, am), rows_of(pair, pair))
    low = dot(lanes(ah, al), rows_of(bl, bh))
    return out[:, :n] + (out[:, n:] + low)


def mul3_nt(a, b):
    ah, am, al = a
    bh, bm, bl = b
    n = bh.shape[0]
    pair = rows_of(bh, bm)
    out = dot(lanes(ah, am), lanes(pair, pair), NT)
    low = dot(lanes(ah, al), lanes(bl, bh), NT)
    return out[:, :n] + (out[:, n:] + low)


def eye_of(n):
    return (
        lax.broadcasted_iota(jnp.int32, (n, n), 0) == lax.broadcasted_iota(jnp.int32, (n, n), 1)
    ).astype(F32)


def inverses(mats, eye, scan, fill=()):
    coef, scales = scan
    fill = list(fill)
    share = -(-len(fill) // (STEPS - 2)) if fill else 0
    res = [eye - coef * a for a in mats]
    inv = [(scales[0] * coef) * (eye + r) for r in res]
    res = [(1.0 - scales[0]) * eye + scales[0] * mul3(r, r) for r in res]
    for j in range(1, STEPS - 1):
        s = scales[j]
        mul = mul2 if j == STEPS - 2 else mul3
        both = [mul(rows_of(r, x), r) for x, r in zip(inv, res)]
        for work in fill[:share]:
            work()
        fill = fill[share:]
        inv = [s * (x + b[B:]) for x, b in zip(inv, both)]
        res = [(1.0 - s) * eye + s * b[:B] for b in both]
    s = scales[-1]
    return [s * x for x in inv], res


def device(index):
    per = lax.axis_size("dev")
    return (lax.div(index, per), lax.rem(index, per))


def my_index():
    return lax.axis_index("region") * lax.axis_size("dev") + lax.axis_index("dev")


def network(x, w_in, b_in, w_out):
    pre = dot(x, w_in) + b_in
    sig = 1.0 / (1.0 + jnp.exp(-pre))
    hidden = (pre * sig).astype(BF16)
    return pre, sig, hidden


def one_hot(point_slot, rows, first):
    slot = lax.broadcasted_iota(jnp.int32, (rows, ROWS), 0) + first
    return (slot == point_slot).astype(F32).astype(BF16)


def block(ref, s, a, b):
    return ref[s, a * B : (a + 1) * B, b * B : (b + 1) * B]


def member_windows(me, home_ref, ids_ref, cnt_ref, s):
    places = []
    for k in range(NMAX):
        slot = home_ref[ids_ref[s, k]]
        live = k < cnt_ref[s]
        w = jnp.where(live, (me - slot // BPD) * BPD + slot % BPD, 0)
        places.append((jnp.clip(w, 0, (WIN + 1) * BPD - 1), jnp.where(live, 1.0, 0.0)))
    return places


def kernel_rows(s, count, places, feat_ref, resp_ref, z_ref, e_ref, k_ref, inv_sq, var, nug, eye):
    lane1 = lax.broadcasted_iota(jnp.int32, (1, B), 1)
    y_row = jnp.zeros((1, N), F32)
    for k, (w, flag) in enumerate(places + [(s, None)]):
        member = feat_ref[w]
        resp = jnp.where(lane1 < BS, resp_ref[w][0:1].astype(F32), 0.0)
        if flag is not None:
            member = (member.astype(F32) * flag).astype(BF16)
            resp = resp * flag
        z_ref[s, k * BS : (k + 1) * BS, :] = member
        resp = lanes(resp, jnp.zeros((1, N - B), F32))
        y_row = y_row + (pltpu.roll(resp, k * BS, 1) if k else resp)
    z_ref[s, (NMAX + 1) * BS :, :] = jnp.zeros((N - (NMAX + 1) * BS, H), BF16)
    z = z_ref[s]
    gram = dot(z, z, NT)
    e_ref[s] = gram
    diag = [jnp.where(eye > 0.0, gram[i * B : (i + 1) * B, i * B : (i + 1) * B], 0.0) for i in range(4)]
    sq_row = lanes(*[jnp.sum(d, axis=0, keepdims=True) for d in diag])
    sq_col = [jnp.sum(d, axis=1, keepdims=True) for d in diag]
    col_id = lax.broadcasted_iota(jnp.int32, (1, N), 1)
    own = (col_id >= NMAX * BS) & (col_id < (NMAX + 1) * BS)
    v_row = jnp.where((col_id < count * BS) | own, 1.0, 0.0)

    def piece(i, c):
        part = slice(c, c + 32)
        out = slice(i * B + c, i * B + c + 32)
        row_id = lax.broadcasted_iota(jnp.int32, (32, 1), 0) + (i * B + c)
        own = (row_id >= NMAX * BS) & (row_id < (NMAX + 1) * BS)
        v_col = jnp.where((row_id < count * BS) | own, 1.0, 0.0)
        d2 = jnp.maximum(sq_col[i][part] + sq_row - 2.0 * e_ref[s, out, :], 0.0)
        r2 = d2 * inv_sq + 1e-06
        rad = SQRT_THREE * (r2 * lax.rsqrt(r2))
        e = jnp.exp(-rad) * (v_col * v_row)
        e_ref[s, out, :] = e
        wide = (i + 1) * B
        kern = var * (1.0 + rad[:, :wide]) * e[:, :wide]
        spot = kern[:, i * B :] + eye[part] * (nug * v_col + 1.0 - v_col)
        k_ref[s, out, :wide] = lanes(kern[:, : i * B], spot) if i else spot
        if i == 3 and c == BS:
            k_ref[s, 3 * B + BS : 3 * B + BS + 1, :] = y_row

    return [[lambda i=i, c=c: piece(i, c) for c in range(0, B, 32)] for i in range(4)]


def eliminate(both, k_ref, eye, scan, fill):
    invs = []
    for i in range(3):
        lo = (i + 1) * B
        cols = slice(i * B, lo)
        x, r = inverses([block(k_ref, s, i, i) for s in both], eye, scan, fill)
        fill = []
        below = [split3(k_ref[s, lo:, cols]) for s in both]
        panel = [mul3(below[s], x[s]) for s in both]
        panel = [split3(panel[s] + mul2(panel[s], r[s])) for s in both]
        invs.append([split3(x[s] + mul2(x[s], r[s])) for s in both])
        for b in range(i + 1, 4):
            first = (b - i - 1) * B
            for s in both:
                at = slice(b * B, (b + 1) * B)
                k_ref[s, b * B :, at] = k_ref[s, b * B :, at] - mul3_nt(
                    tuple(p[first:] for p in panel[s]), tuple(p[first : first + B] for p in below[s])
                )
    return invs, [block(k_ref, s, 3, 3) for s in both], []


def joint_gradients(both, invs, schur, resid, scan, fill, z_ref, e_ref, k_ref, var, inv_sq, nug, eye, real):
    sub = lax.broadcasted_iota(jnp.int32, (B, B), 0)
    lane = lax.broadcasted_iota(jnp.int32, (B, B), 1)
    lane1 = lax.broadcasted_iota(jnp.int32, (1, B), 1)
    sign = jnp.where(lax.broadcasted_iota(jnp.int32, (B, 1), 0) < BS, -1.0, 1.0)
    p3, p2, t1, x1, ys, w_pair = {}, {}, {}, {}, {}, {}

    def back(s, step):
        if step == 0:
            p3[s] = split3(mul3(block(k_ref, s, 3, 2), invs[2][s]))
        elif step == 1:
            p2[s] = block(k_ref, s, 3, 1) - mul3(p3[s], block(k_ref, s, 2, 1))
            t1[s] = block(k_ref, s, 3, 0) - mul3(p3[s], block(k_ref, s, 2, 0))
        elif step == 2:
            p2[s] = split3(mul3(p2[s], invs[1][s]))
        elif step == 3:
            t1[s] = t1[s] - mul3(p2[s], block(k_ref, s, 1, 0))
        elif step == 4:
            x1[s] = mul3(t1[s], invs[0][s])
        else:
            x2, x3 = [p[0].astype(F32) + (p[1].astype(F32) + p[2].astype(F32)) for p in (p2[s], p3[s])]
            ys[s] = lanes(x1[s] * sign, x2 * sign, x3 * sign)
            w = rows_of(*[ys[s][:, i * B : (i + 1) * B].T for i in range(3)])
            w_pair[s] = lanes(*split2(w))

    own = jnp.where(real, eye, 0.0)
    steps = [lambda s=s, step=step: back(s, step) for step in range(6) for s in both]
    x, r = inverses(schur, eye, scan, fill + steps)
    beta_m = [mul3(resid[s], x[s]) for s in both]
    beta_m = [beta_m[s] + mul2(beta_m[s], r[s]) for s in both]
    s_inv = [x[s] + mul2(x[s], r[s]) for s in both]
    y_parts = [split2(lanes(ys[s], own)) for s in both]
    beta_row = [m[BS : BS + 1] for m in beta_m]
    beta_col = [jnp.sum(eye * b, axis=1, keepdims=True) for b in beta_row]
    mid = [
        jnp.where(real, beta_col[s] * beta_row[s] - s_inv[s], 0.0)
        + beta_m[s]
        + jnp.where((lane == BS) & (sub < BS), beta_col[s], 0.0)
        for s in both
    ]
    prod = [mul2(mid[s], y_parts[s]) for s in both]
    pairs = [lanes(*split2(p)) for p in prod]
    g = [dot(w_pair[s], rows_of(pairs[s], pairs[s])) for s in both]
    below = lax.broadcasted_iota(jnp.int32, (B, 1), 0) < BS
    low = [jnp.where(below, prod[s], 0.0) for s in both]
    weights = [
        split2(rows_of((g[s][:, :N] + g[s][:, N:]) * e_ref[s, : 3 * B, :], low[s] * e_ref[s, 3 * B :, :]))
        for s in both
    ]
    rhs = [lanes(z_ref[s], jnp.ones((N, H), BF16)) for s in both]
    pz = [dot(weights[s][0], rhs[s]) + dot(weights[s][1], rhs[s]) for s in both]
    out = []
    for s in both:
        quad = jnp.sum(jnp.sum(resid[s] * beta_m[s], axis=0, keepdims=True), axis=1, keepdims=True)
        y = lanes(ys[s], own)
        trace = jnp.sum(jnp.sum(prod[s] * y, axis=0, keepdims=True), axis=1, keepdims=True)
        t2 = 0.5 * nug * trace
        t1 = 0.5 * quad - 0.5 * BS - t2
        zf = z_ref[s].astype(F32)
        grad = (3.0 * var * inv_sq) * (pz[s][:, :H] - pz[s][:, H:] * zf)
        t0 = -jnp.sum(jnp.sum(grad * zf, axis=0, keepdims=True), axis=1, keepdims=True)
        hyper = jnp.where(lane1 == 0, t0, 0.0) + jnp.where(lane1 == 1, t1, 0.0)
        out.append((grad, hyper + jnp.where(lane1 == 2, t2, 0.0), quad))
    return out


def pivot_steps(mat_ref, log_ref, first, last):
    mats = [mat_ref[i, first:BS, :] for i in range(BPD)]
    logdets = [log_ref[i, 0:1, 0:1] for i in range(BPD)]
    for k in range(first, last):
        for i, mat in enumerate(mats):
            at = k - (BS - mat.shape[0])
            row = mat[at : at + 1]
            pivot = row[:, k : k + 1]
            logdets[i] = logdets[i] + jnp.log(pivot)
            if k < BS - 1:
                if (k + 1) % 8 == 0:
                    mat = mat[8:]
                mats[i] = mat - mat[:, k : k + 1] * (row / pivot)
    for i in range(BPD):
        log_ref[i, 0:1, :] = jnp.broadcast_to(logdets[i], (1, B))
        if last < BS:
            mat_ref[i, last:BS, :] = mats[i]


def main_kernel(
    x_in, resp_in, ps_in, w_in_in, b_in, w_out_in, home_in, ids_in, cnt_in, par_in,
    ll_ref, hyp_ref, fg_out, gath, b_out,
    x_ref, resp_ref, ps_ref, w_in_ref, b_ref, w_out_ref, home_ref, ids_ref, cnt_ref, par_ref,
    fg_ref, mine_ref, bsum_ref, in_sem, out_sem,
    win_ref, wresp_ref, feat_ref, hid_ref, dsil_ref, z_ref, e_ref, k_ref, gw_ref,
    out_buf, in_buf, part, part_in, pair, red_in, mat_ref, log_ref,
    f_send, f_recv, g_send, g_recv, s1, r1, s2, r2, s3, r3, c_send, c_recv,
):
    total = lax.axis_size("region") * lax.axis_size("dev")
    region, dev = lax.axis_index("region"), lax.axis_index("dev")
    me = my_index()
    x, core = lax.div(region, 2), lax.rem(region, 2)
    y, z = lax.div(dev, DEPTH), lax.rem(dev, DEPTH)
    ga = x * 4 + y

    xs = [x] + [lax.rem(x + k, 4) for k in range(1, 4)]
    ys = [y] + [lax.rem(y + k, 4) for k in range(1, 4)]
    mates = [
        (xs[k // 4] * 4 + ys[k % 4], (xs[k // 4] * 2 + core, ys[k % 4] * DEPTH + z)) for k in range(GROUP)
    ]
    column = [(region, y * DEPTH + lax.rem(z + k, DEPTH)) for k in range(DEPTH)]

    def send(src, dst, ssem, rsem, place):
        copy = pltpu.make_async_remote_copy(
            src_ref=src, dst_ref=dst, send_sem=ssem, recv_sem=rsem, device_id=place, device_id_type=MESH
        )
        copy.start()
        return copy

    def later(k):
        return device(lax.rem(me + k + total, total))

    ops = (x_in, resp_in, ps_in, w_in_in, b_in, w_out_in, home_in, ids_in, cnt_in, par_in)
    refs = (x_ref, resp_ref, ps_ref, w_in_ref, b_ref, w_out_ref, home_ref, ids_ref, cnt_ref, par_ref)
    loads = [pltpu.make_async_copy(a, b, in_sem.at[i]) for i, (a, b) in enumerate(zip(ops, refs))]
    for c in loads:
        c.start()
    barrier = pltpu.get_barrier_semaphore()
    for k in range(1, WIN + 1):
        pl.semaphore_signal(barrier, inc=1, device_id=later(k), device_id_type=MESH)
        pl.semaphore_signal(barrier, inc=1, device_id=later(-k), device_id_type=MESH)
    for k in range(1, GROUP):
        pl.semaphore_signal(barrier, inc=1, device_id=mates[k][1], device_id_type=MESH)
    for k in range(1, DEPTH):
        pl.semaphore_signal(barrier, inc=1, device_id=column[k], device_id_type=MESH)
    pl.semaphore_signal(barrier, inc=1, device_id=(x * 2 + 1 - core, dev), device_id_type=MESH)

    for c in loads:
        c.wait()
    point_slot = ps_ref[...].reshape(1, ROWS)
    win_ref[0, :ROWS, :] = dot(one_hot(point_slot, ROWS, 0), x_ref[...]).astype(BF16)
    resp = jnp.broadcast_to(resp_ref[...].astype(F32).reshape(1, ROWS), (16, ROWS)).astype(BF16)
    win_ref[0, ROWS : ROWS + 16, :] = dot(resp, one_hot(point_slot, B, 0), NT).astype(BF16)
    win_ref[0, ROWS + 16 :, :] = dot(resp, one_hot(point_slot, B, BS), NT).astype(BF16)
    pl.semaphore_wait(barrier, 2 * WIN + GROUP + DEPTH - 1)

    def shift(src, dst, cut, sem, k):
        at = pl.ds(cut.start, cut.stop - cut.start)
        return send(win_ref.at[src, at], win_ref.at[dst, at], f_send.at[sem], f_recv.at[sem], later(k))

    cuts = [slice(0, 64), slice(64, 128), slice(128, ROWS + 32)]
    two = [shift(0, 2, cut, q, 2) for q, cut in enumerate(cuts)]
    one = shift(0, 1, slice(0, ROWS + 32), 3, 1)

    def forward(d):
        pre, sig, hidden = network(win_ref[d, :ROWS, :], w_in_ref[...], b_ref[...].reshape(1, H), w_out_ref[...])
        hid_ref[d] = hidden
        dsil_ref[d] = sig * (1.0 + pre * (1.0 - sig))
        feats = dot(hidden, w_out_ref[...]).astype(BF16)
        feat_ref[2 * d] = feats[:BS]
        feat_ref[2 * d + 1] = feats[BS:]
        for b in range(BPD):
            wresp_ref[2 * d + b] = win_ref[d, ROWS + 16 * b : ROWS + 16 * (b + 1), :]

    forward(0)

    def const(v):
        return jnp.full((1, 1), v, F32)

    inv_sq = jnp.exp(-2.0 * const(par_ref[0]))
    var = jnp.exp(const(par_ref[1]))
    nug = jnp.exp(const(par_ref[2]))
    eye = eye_of(B)
    lane = lax.broadcasted_iota(jnp.int32, (B, B), 1)
    sub = lax.broadcasted_iota(jnp.int32, (B, B), 0)
    top = B * var + 1.0
    coef = 2.0 / (top + nug)
    delta = (top - nug) / (top + nug)
    scales = []
    for _ in range(STEPS):
        sq = delta * delta
        scales.append(2.0 / (2.0 - sq))
        delta = sq / (2.0 - sq)
    both = range(BPD)
    places = [member_windows(me, home_ref, ids_ref, cnt_ref, s) for s in both]
    three = []
    for q, cut in enumerate(cuts):
        two[q].wait()
        three.append(shift(2, 3, cut, 4 + q, 1))
    forward(2)
    one.wait()
    forward(1)
    for c in three:
        c.wait()
    forward(3)

    rows = [
        kernel_rows(
            s, cnt_ref[s], places[s], feat_ref, wresp_ref, z_ref, e_ref, k_ref, inv_sq, var, nug, eye
        )
        for s in both
    ]
    for s in both:
        for work in rows[s][0]:
            work()
    fill = [work for i in range(1, 4) for s in both for work in rows[s][i]]
    scan = (coef, scales)
    invs, last, fill = eliminate(both, k_ref, eye, scan, fill)
    real = (lane < BS) & (sub < BS)
    resid = [jnp.where((sub == BS) & (lane < BS), m, 0.0) for m in last]
    schur = [jnp.where(real, m, eye) for m in last]
    for s in both:
        mat_ref[s] = schur[s][:BS]
    found = joint_gradients(
        both, invs, schur, resid, scan, fill, z_ref, e_ref, k_ref, var, inv_sq, nug, eye, real
    )
    grads, hypers, quads = [list(part) for part in zip(*found)]
    for w in range((WIN + 1) * BPD):
        acc = grads[w][NMAX * BS : (NMAX + 1) * BS] if w < BPD else jnp.zeros((BS, H), F32)
        for s in both:
            if w == 1 or (w == 0 and s == 0):
                continue
            for k in range(NMAX):
                place, flag = places[s][k]
                acc = acc + jnp.where(place == w, flag, 0.0) * grads[s][k * BS : (k + 1) * BS]
        gw_ref[w] = acc
        if w >= BPD:
            out_buf[w // BPD - 1, (w % BPD) * BS : (w % BPD + 1) * BS, :] = acc.astype(BF16)
    returns = [
        send(out_buf.at[k - 1], in_buf.at[k - 1], g_send.at[k], g_recv.at[k], later(-k))
        for k in range(1, WIN + 1)
    ]

    w_in_part = jnp.zeros((H, 2 * H), F32)
    w_out_part = jnp.zeros((H, 2 * H), F32)
    b_part = jnp.zeros((1, H), F32)
    for d in range(WIN + 1):
        hi, lo = split2(rows_of(gw_ref[2 * d], gw_ref[2 * d + 1]))
        back = dot(hi, w_out_ref[...], NT) + dot(lo, w_out_ref[...], NT)
        dpre = back * dsil_ref[d]
        w_out_part = w_out_part + dot(hid_ref[d], lanes(hi, lo), TN)
        w_in_part = w_in_part + dot(win_ref[d, :ROWS, :], lanes(*split2(dpre)), TN)
        b_part = b_part + jnp.sum(dpre, axis=0, keepdims=True)
    w_in_part = w_in_part[:, :H] + w_in_part[:, H:]
    w_out_part = w_out_part[:, :H] + w_out_part[:, H:]
    row8 = lax.broadcasted_iota(jnp.int32, (8, H), 0)
    row16 = lax.broadcasted_iota(jnp.int32, (CHUNK, H), 0)

    def pack(bias, hyper):
        tile = jnp.zeros((CHUNK, H), F32)
        for i, one_row in enumerate(split2(bias) + split2(hyper)):
            tile = tile + jnp.where(row16 == i, one_row.astype(F32), 0.0)
        return tile.astype(BF16)

    def unpack(tile):
        return tile[0:1] + tile[1:2], tile[2:3] + tile[3:4]

    for s in both:
        log_ref[s] = jnp.where(row8 == 1, quads[s], 0.0)
    small = pack(b_part, hypers[0] + hypers[1])
    w_in_part = w_in_part.astype(BF16)
    w_out_part = w_out_part.astype(BF16)
    for c in range(GROUP):
        src = w_in_part if c < 8 else w_out_part
        part[c, :CHUNK, :] = src[(c % 8) * CHUNK : (c % 8 + 1) * CHUNK]
        part[c, CHUNK:, :] = small
    copies = []
    for k in range(1, GROUP):
        other, place = mates[k]
        copies.append(send(part.at[other], part_in.at[ga], s1.at[k], r1.at[k], place))
    part_in[ga] = part[ga]

    @pl.when(dev >= 0)
    def _():
        pivot_steps(mat_ref, log_ref, 0, 32)

    for c in copies:
        c.wait()
    acc = part_in[0].astype(F32)
    for c in range(1, GROUP):
        acc = acc + part_in[c].astype(F32)
    bias, hyper = unpack(acc[CHUNK:])
    pair[core, :CHUNK, :] = acc[:CHUNK]
    pair[core, CHUNK:, :] = jnp.where(row8 == 0, bias, 0.0) + jnp.where(row8 == 1, hyper, 0.0)
    copy = send(pair.at[core], pair.at[core], c_send, c_recv, (x * 2 + 1 - core, dev))
    copy.wait()
    acc = pair[0] + pair[1]
    red_in[z, :CHUNK, :] = acc[:CHUNK].astype(BF16)
    red_in[z, CHUNK:, :] = pack(acc[CHUNK : CHUNK + 1], acc[CHUNK + 1 : CHUNK + 2])
    copies = []
    for k in range(1, DEPTH):
        copies.append(send(red_in.at[z], red_in.at[z], s2.at[k], r2.at[k], column[k]))

    @pl.when(dev >= 0)
    def _():
        pivot_steps(mat_ref, log_ref, 32, 64)

    for c in copies:
        c.wait()
    acc = red_in[0].astype(F32)
    for c in range(1, DEPTH):
        acc = acc + red_in[c].astype(F32)
    acc = acc * (1.0 / (total * ROWS))
    mine_ref[...] = acc[:CHUNK].astype(BF16)
    bias, hyper = unpack(acc[CHUNK:])
    bsum_ref[...] = bias.reshape(H)
    place = pl.ds(pl.multiple_of(ga * CHUNK, CHUNK), CHUNK)
    copies = []
    for k in range(1, GROUP):
        copies.append(send(mine_ref, gath.at[place], s3.at[k], r3.at[k], mates[k][1]))
    stores = [
        pltpu.make_async_copy(mine_ref, gath.at[place], out_sem.at[0]),
        pltpu.make_async_copy(bsum_ref, b_out, out_sem.at[1]),
        pltpu.make_async_copy(fg_ref, fg_out, out_sem.at[2]),
    ]
    stores[0].start()
    stores[1].start()

    @pl.when(dev >= 0)
    def _():
        pivot_steps(mat_ref, log_ref, 64, BS)
        for s in both:
            ll = -0.5 * (log_ref[s, 0:1, 0:1] + log_ref[s, 1:2, 0:1]) * (1.0 / BS) - 0.5 * LOG_TWO_PI
            ll_ref[s] = jnp.sum(ll)
        for i in range(3):
            hyp_ref[i] = jnp.sum(hyper[:, i : i + 1])

    for c in returns:
        c.wait()
    grad = rows_of(gw_ref[0], gw_ref[1])
    for k in range(WIN):
        grad = grad + in_buf[k].astype(F32)
    perm = one_hot(ps_ref[...].reshape(1, ROWS), ROWS, 0)
    pairs = dot(perm, lanes(*split2(grad)), TN)
    fg_ref[...] = pairs[:, :H] + pairs[:, H:]
    stores[2].start()
    for c in copies + stores:
        c.wait()


def finish_kernel(ll_in, hyp_in, grad_in, weights_in, b_in, ll_out, fg_out, gin_out, b_out, gout_out, hyp_out):
    fg_out[...] = grad_in[...]
    gin_out[...] = weights_in[:H, :].astype(F32)
    gout_out[...] = weights_in[H:, :].astype(F32)
    b_out[...] = b_in[...]
    for s in range(BPD):
        ll_out[s] = ll_in[s]
    for i in range(3):
        hyp_out[i] = hyp_in[i]


VM = pl.BlockSpec(memory_space=pltpu.VMEM)
SM = pl.BlockSpec(memory_space=pltpu.SMEM)
ANY = pl.BlockSpec(memory_space=pl.ANY)
DMA = pltpu.SemaphoreType.DMA


def shards(
    inputs, responses, point_slot, block_home, nbr_ids, nbr_count, w_in, b_in, w_out, kernel_params
):
    loglik, hyper, grad, weights, bias = pl.pallas_call(
        main_kernel,
        out_shape=(
            jax.ShapeDtypeStruct((BPD,), F32),
            jax.ShapeDtypeStruct((3,), F32),
            jax.ShapeDtypeStruct((ROWS, H), F32),
            jax.ShapeDtypeStruct((GROUP * CHUNK, H), BF16),
            jax.ShapeDtypeStruct((H,), F32),
        ),
        in_specs=[ANY] * 10,
        out_specs=(SM, SM, ANY, ANY, ANY),
        scratch_shapes=[
            pltpu.VMEM((ROWS, H), BF16),
            pltpu.VMEM((ROWS,), BF16),
            pltpu.VMEM((ROWS,), jnp.int32),
            pltpu.VMEM((H, H), BF16),
            pltpu.VMEM((H,), F32),
            pltpu.VMEM((H, H), BF16),
            pltpu.SMEM(block_home.shape, jnp.int32),
            pltpu.SMEM((BPD, NMAX), jnp.int32),
            pltpu.SMEM((BPD,), jnp.int32),
            pltpu.SMEM((3,), F32),
            pltpu.VMEM((ROWS, H), F32),
            pltpu.VMEM((CHUNK, H), BF16),
            pltpu.VMEM((H,), F32),
            DMA((10,)),
            DMA((3,)),
            pltpu.VMEM((WIN + 1, ROWS + 32, H), BF16),
            pltpu.VMEM(((WIN + 1) * BPD, 16, H), BF16),
            pltpu.VMEM(((WIN + 1) * BPD, BS, H), BF16),
            pltpu.VMEM((WIN + 1, ROWS, H), BF16),
            pltpu.VMEM((WIN + 1, ROWS, H), F32),
            pltpu.VMEM((BPD, N, H), BF16),
            pltpu.VMEM((BPD, N, N), F32),
            pltpu.VMEM((BPD, N, N), F32),
            pltpu.VMEM(((WIN + 1) * BPD, BS, H), F32),
            pltpu.VMEM((WIN, ROWS, H), BF16),
            pltpu.VMEM((WIN, ROWS, H), BF16),
            pltpu.VMEM((GROUP, 2 * CHUNK, H), BF16),
            pltpu.VMEM((GROUP, 2 * CHUNK, H), BF16),
            pltpu.VMEM((2, CHUNK + 8, H), F32),
            pltpu.VMEM((DEPTH, 2 * CHUNK, H), BF16),
            pltpu.VMEM((BPD, BS, B), F32),
            pltpu.VMEM((BPD, 8, B), F32),
        ]
        + [DMA((8,))] * 2
        + [DMA((WIN + 1,))] * 2
        + [DMA((GROUP,))] * 6
        + [DMA, DMA],
        compiler_params=pltpu.CompilerParams(
            collective_id=0, has_side_effects=True, vmem_limit_bytes=60 * 1024 * 1024
        ),
        name="vecchia_main",
    )(
        inputs, responses, point_slot, w_in, b_in, w_out,
        block_home, nbr_ids, nbr_count, kernel_params,
    )
    loglik, feature_grad, g_in, g_b, g_out, hyper = pl.pallas_call(
        finish_kernel,
        out_shape=(
            jax.ShapeDtypeStruct((BPD,), F32),
            jax.ShapeDtypeStruct((ROWS, H), F32),
            jax.ShapeDtypeStruct((H, H), F32),
            jax.ShapeDtypeStruct((H,), F32),
            jax.ShapeDtypeStruct((H, H), F32),
            jax.ShapeDtypeStruct((3,), F32),
        ),
        in_specs=[SM, SM, VM, VM, VM],
        out_specs=(SM, VM, VM, VM, VM, SM),
        name="vecchia_finish",
    )(loglik, hyper, grad, weights, bias)
    return loglik, feature_grad, g_in, g_b, g_out, hyper


def solution(mesh):
    placed = (
        P(("region", "dev"), None),
        P(("region", "dev")),
        P(("region", "dev")),
        P(),
        P(("region", "dev"), None),
        P(("region", "dev")),
        P(),
        P(),
        P(),
        P(),
    )
    return jax.shard_map(
        shards,
        mesh=mesh,
        in_specs=placed,
        out_specs=(P(("region", "dev")), P(("region", "dev"), None), P(), P(), P(), P()),
        check_vma=False,
    )
```

```python
import math

import jax
import jax.numpy as jnp
from jax import lax
from jax.experimental import pallas as pl
from jax.experimental.pallas import tpu as pltpu
from jax.sharding import PartitionSpec as P

H = 128
BS = 96
BPD = 2
NMAX = 4
WIN = 3
ROWS = BPD * BS
B = 128
N = 4 * B
STEPS = 8
GROUP = 16
CHUNK = 16
DEPTH = 8

SQRT_THREE = math.sqrt(3.0)
LOG_TWO_PI = math.log(2.0 * math.pi)
MESH = pl.DeviceIdType.MESH
F32 = jnp.float32
BF16 = jnp.bfloat16


def dot(a, b, contract=((1,), (0,))):
    return lax.dot_general(a, b, (contract, ((), ())), preferred_element_type=F32)


NT = ((1,), (1,))
TN = ((0,), (0,))


def split2(a):
    hi = a.astype(BF16)
    return hi, (a - hi.astype(F32)).astype(BF16)


def split3(a):
    hi = a.astype(BF16)
    rest = a - hi.astype(F32)
    mid = rest.astype(BF16)
    return hi, mid, (rest - mid.astype(F32)).astype(BF16)


def lanes(*parts):
    return jnp.concatenate(parts, axis=1)


def rows_of(*parts):
    return jnp.concatenate(parts, axis=0)


def mul2(a, b):
    n = (b[0] if isinstance(b, tuple) else b).shape[1]
    pair = lanes(*(b if isinstance(b, tuple) else split2(b)))
    out = dot(lanes(*split2(a)), rows_of(pair, pair))
    return out[:, :n] + out[:, n:]


def mul3(a, b):
    ah, am, al = a if isinstance(a, tuple) else split3(a)
    bh, bm, bl = b if isinstance(b, tuple) else split3(b)
    n = bh.shape[1]
    pair = lanes(bh, bm)
    out = dot(lanes(ah, am), rows_of(pair, pair))
    low = dot(lanes(ah, al), rows_of(bl, bh))
    return out[:, :n] + (out[:, n:] + low)


def mul3_nt(a, b):
    ah, am, al = a
    bh, bm, bl = b
    n = bh.shape[0]
    pair = rows_of(bh, bm)
    out = dot(lanes(ah, am), lanes(pair, pair), NT)
    low = dot(lanes(ah, al), lanes(bl, bh), NT)
    return out[:, :n] + (out[:, n:] + low)


def eye_of(n):
    return (
        lax.broadcasted_iota(jnp.int32, (n, n), 0) == lax.broadcasted_iota(jnp.int32, (n, n), 1)
    ).astype(F32)


def inverses(mats, eye, scan, fill=()):
    coef, scales = scan
    fill = list(fill)
    share = -(-len(fill) // (STEPS - 2)) if fill else 0
    res = [eye - coef * a for a in mats]
    inv = [(scales[0] * coef) * (eye + r) for r in res]
    res = [(1.0 - scales[0]) * eye + scales[0] * mul3(r, r) for r in res]
    for j in range(1, STEPS - 1):
        s = scales[j]
        mul = mul2 if j == STEPS - 2 else mul3
        both = [mul(rows_of(r, x), r) for x, r in zip(inv, res)]
        for work in fill[:share]:
            work()
        fill = fill[share:]
        inv = [s * (x + b[B:]) for x, b in zip(inv, both)]
        res = [(1.0 - s) * eye + s * b[:B] for b in both]
    s = scales[-1]
    return [s * x for x in inv], res


def device(index):
    per = lax.axis_size("dev")
    return (lax.div(index, per), lax.rem(index, per))


def my_index():
    return lax.axis_index("region") * lax.axis_size("dev") + lax.axis_index("dev")


def network(x, w_in, b_in, w_out):
    pre = dot(x, w_in) + b_in
    sig = 1.0 / (1.0 + jnp.exp(-pre))
    hidden = (pre * sig).astype(BF16)
    return pre, sig, hidden


def one_hot(point_slot, rows, first):
    slot = lax.broadcasted_iota(jnp.int32, (rows, ROWS), 0) + first
    return (slot == point_slot).astype(F32).astype(BF16)


def block(ref, s, a, b):
    return ref[s, a * B : (a + 1) * B, b * B : (b + 1) * B]


def member_windows(me, home_ref, ids_ref, cnt_ref, s):
    places = []
    for k in range(NMAX):
        slot = home_ref[ids_ref[s, k]]
        live = k < cnt_ref[s]
        w = jnp.where(live, (me - slot // BPD) * BPD + slot % BPD, 0)
        places.append((jnp.clip(w, 0, (WIN + 1) * BPD - 1), jnp.where(live, 1.0, 0.0)))
    return places


def kernel_rows(s, count, places, feat_ref, resp_ref, z_ref, e_ref, k_ref, inv_sq, var, nug, eye):
    lane1 = lax.broadcasted_iota(jnp.int32, (1, B), 1)
    y_row = jnp.zeros((1, N), F32)
    for k, (w, flag) in enumerate(places + [(s, None)]):
        member = feat_ref[w]
        resp = jnp.where(lane1 < BS, resp_ref[w][0:1].astype(F32), 0.0)
        if flag is not None:
            member = (member.astype(F32) * flag).astype(BF16)
            resp = resp * flag
        z_ref[s, k * BS : (k + 1) * BS, :] = member
        resp = lanes(resp, jnp.zeros((1, N - B), F32))
        y_row = y_row + (pltpu.roll(resp, k * BS, 1) if k else resp)
    z_ref[s, (NMAX + 1) * BS :, :] = jnp.zeros((N - (NMAX + 1) * BS, H), BF16)
    z = z_ref[s]
    gram = dot(z, z, NT)
    e_ref[s] = gram
    diag = [jnp.where(eye > 0.0, gram[i * B : (i + 1) * B, i * B : (i + 1) * B], 0.0) for i in range(4)]
    sq_row = lanes(*[jnp.sum(d, axis=0, keepdims=True) for d in diag])
    sq_col = [jnp.sum(d, axis=1, keepdims=True) for d in diag]
    col_id = lax.broadcasted_iota(jnp.int32, (1, N), 1)
    own = (col_id >= NMAX * BS) & (col_id < (NMAX + 1) * BS)
    v_row = jnp.where((col_id < count * BS) | own, 1.0, 0.0)

    def piece(i, c):
        part = slice(c, c + 32)
        out = slice(i * B + c, i * B + c + 32)
        row_id = lax.broadcasted_iota(jnp.int32, (32, 1), 0) + (i * B + c)
        own = (row_id >= NMAX * BS) & (row_id < (NMAX + 1) * BS)
        v_col = jnp.where((row_id < count * BS) | own, 1.0, 0.0)
        d2 = jnp.maximum(sq_col[i][part] + sq_row - 2.0 * e_ref[s, out, :], 0.0)
        r2 = d2 * inv_sq + 1e-06
        rad = SQRT_THREE * (r2 * lax.rsqrt(r2))
        e = jnp.exp(-rad) * (v_col * v_row)
        e_ref[s, out, :] = e
        wide = (i + 1) * B
        kern = var * (1.0 + rad[:, :wide]) * e[:, :wide]
        spot = kern[:, i * B :] + eye[part] * (nug * v_col + 1.0 - v_col)
        k_ref[s, out, :wide] = lanes(kern[:, : i * B], spot) if i else spot
        if i == 3 and c == BS:
            k_ref[s, 3 * B + BS : 3 * B + BS + 1, :] = y_row

    return [[lambda i=i, c=c: piece(i, c) for c in range(0, B, 32)] for i in range(4)]


def eliminate(both, k_ref, eye, scan, fill):
    invs = []
    for i in range(3):
        lo = (i + 1) * B
        cols = slice(i * B, lo)
        x, r = inverses([block(k_ref, s, i, i) for s in both], eye, scan, fill)
        fill = []
        below = [split3(k_ref[s, lo:, cols]) for s in both]
        panel = [mul3(below[s], x[s]) for s in both]
        panel = [split3(panel[s] + mul2(panel[s], r[s])) for s in both]
        invs.append([split3(x[s] + mul2(x[s], r[s])) for s in both])
        for b in range(i + 1, 4):
            first = (b - i - 1) * B
            for s in both:
                at = slice(b * B, (b + 1) * B)
                k_ref[s, b * B :, at] = k_ref[s, b * B :, at] - mul3_nt(
                    tuple(p[first:] for p in panel[s]), tuple(p[first : first + B] for p in below[s])
                )
    return invs, [block(k_ref, s, 3, 3) for s in both], []


def joint_gradients(both, invs, schur, resid, scan, fill, z_ref, e_ref, k_ref, var, inv_sq, nug, eye, real):
    sub = lax.broadcasted_iota(jnp.int32, (B, B), 0)
    lane = lax.broadcasted_iota(jnp.int32, (B, B), 1)
    lane1 = lax.broadcasted_iota(jnp.int32, (1, B), 1)
    sign = jnp.where(lax.broadcasted_iota(jnp.int32, (B, 1), 0) < BS, -1.0, 1.0)
    p3, p2, t1, x1, ys, w_pair = {}, {}, {}, {}, {}, {}

    def back(s, step):
        if step == 0:
            p3[s] = split3(mul3(block(k_ref, s, 3, 2), invs[2][s]))
        elif step == 1:
            p2[s] = block(k_ref, s, 3, 1) - mul3(p3[s], block(k_ref, s, 2, 1))
            t1[s] = block(k_ref, s, 3, 0) - mul3(p3[s], block(k_ref, s, 2, 0))
        elif step == 2:
            p2[s] = split3(mul3(p2[s], invs[1][s]))
        elif step == 3:
            t1[s] = t1[s] - mul3(p2[s], block(k_ref, s, 1, 0))
        elif step == 4:
            x1[s] = mul3(t1[s], invs[0][s])
        else:
            x2, x3 = [p[0].astype(F32) + (p[1].astype(F32) + p[2].astype(F32)) for p in (p2[s], p3[s])]
            ys[s] = lanes(x1[s] * sign, x2 * sign, x3 * sign)
            w = rows_of(*[ys[s][:, i * B : (i + 1) * B].T for i in range(3)])
            w_pair[s] = lanes(*split2(w))

    own = jnp.where(real, eye, 0.0)
    steps = [lambda s=s, step=step: back(s, step) for step in range(6) for s in both]
    x, r = inverses(schur, eye, scan, fill + steps)
    beta_m = [mul3(resid[s], x[s]) for s in both]
    beta_m = [beta_m[s] + mul2(beta_m[s], r[s]) for s in both]
    s_inv = [x[s] + mul2(x[s], r[s]) for s in both]
    y_parts = [split2(lanes(ys[s], own)) for s in both]
    beta_row = [m[BS : BS + 1] for m in beta_m]
    beta_col = [jnp.sum(eye * b, axis=1, keepdims=True) for b in beta_row]
    mid = [
        jnp.where(real, beta_col[s] * beta_row[s] - s_inv[s], 0.0)
        + beta_m[s]
        + jnp.where((lane == BS) & (sub < BS), beta_col[s], 0.0)
        for s in both
    ]
    prod = [mul2(mid[s], y_parts[s]) for s in both]
    pairs = [lanes(*split2(p)) for p in prod]
    g = [dot(w_pair[s], rows_of(pairs[s], pairs[s])) for s in both]
    below = lax.broadcasted_iota(jnp.int32, (B, 1), 0) < BS
    low = [jnp.where(below, prod[s], 0.0) for s in both]
    weights = [
        split2(rows_of((g[s][:, :N] + g[s][:, N:]) * e_ref[s, : 3 * B, :], low[s] * e_ref[s, 3 * B :, :]))
        for s in both
    ]
    rhs = [lanes(z_ref[s], jnp.ones((N, H), BF16)) for s in both]
    pz = [dot(weights[s][0], rhs[s]) + dot(weights[s][1], rhs[s]) for s in both]
    out = []
    for s in both:
        quad = jnp.sum(jnp.sum(resid[s] * beta_m[s], axis=0, keepdims=True), axis=1, keepdims=True)
        y = lanes(ys[s], own)
        trace = jnp.sum(jnp.sum(prod[s] * y, axis=0, keepdims=True), axis=1, keepdims=True)
        t2 = 0.5 * nug * trace
        t1 = 0.5 * quad - 0.5 * BS - t2
        zf = z_ref[s].astype(F32)
        grad = (3.0 * var * inv_sq) * (pz[s][:, :H] - pz[s][:, H:] * zf)
        t0 = -jnp.sum(jnp.sum(grad * zf, axis=0, keepdims=True), axis=1, keepdims=True)
        hyper = jnp.where(lane1 == 0, t0, 0.0) + jnp.where(lane1 == 1, t1, 0.0)
        out.append((grad, hyper + jnp.where(lane1 == 2, t2, 0.0), quad))
    return out


def pivot_steps(mat_ref, log_ref, first, last):
    mats = [mat_ref[i, first:BS, :] for i in range(BPD)]
    logdets = [log_ref[i, 0:1, 0:1] for i in range(BPD)]
    for k in range(first, last):
        for i, mat in enumerate(mats):
            at = k - (BS - mat.shape[0])
            row = mat[at : at + 1]
            pivot = row[:, k : k + 1]
            logdets[i] = logdets[i] + jnp.log(pivot)
            if k < BS - 1:
                if (k + 1) % 8 == 0:
                    mat = mat[8:]
                mats[i] = mat - mat[:, k : k + 1] * (row / pivot)
    for i in range(BPD):
        log_ref[i, 0:1, :] = jnp.broadcast_to(logdets[i], (1, B))
        if last < BS:
            mat_ref[i, last:BS, :] = mats[i]


def main_kernel(
    x_in, resp_in, ps_in, w_in_in, b_in, w_out_in, home_in, ids_in, cnt_in, par_in,
    ll_ref, hyp_ref, fg_out, gath, b_out,
    x_ref, resp_ref, ps_ref, w_in_ref, b_ref, w_out_ref, home_ref, ids_ref, cnt_ref, par_ref,
    fg_ref, mine_ref, bsum_ref, in_sem, out_sem,
    win_ref, wresp_ref, feat_ref, hid_ref, dsil_ref, z_ref, e_ref, k_ref, gw_ref,
    out_buf, in_buf, part, part_in, pair, red_in, mat_ref, log_ref,
    f_send, f_recv, g_send, g_recv, s1, r1, s2, r2, s3, r3, c_send, c_recv,
):
    total = lax.axis_size("region") * lax.axis_size("dev")
    region, dev = lax.axis_index("region"), lax.axis_index("dev")
    me = my_index()
    x, core = lax.div(region, 2), lax.rem(region, 2)
    y, z = lax.div(dev, DEPTH), lax.rem(dev, DEPTH)
    ga = x * 4 + y

    xs = [x] + [lax.rem(x + k, 4) for k in range(1, 4)]
    ys = [y] + [lax.rem(y + k, 4) for k in range(1, 4)]
    mates = [
        (xs[k // 4] * 4 + ys[k % 4], (xs[k // 4] * 2 + core, ys[k % 4] * DEPTH + z)) for k in range(GROUP)
    ]
    far = sorted(range(1, GROUP), key=lambda k: -(min(k // 4, 4 - k // 4) + min(k % 4, 4 - k % 4)))
    deep = sorted(range(1, DEPTH), key=lambda k: -min(k, DEPTH - k))
    column = [(region, y * DEPTH + lax.rem(z + k, DEPTH)) for k in range(DEPTH)]

    def send(src, dst, ssem, rsem, place):
        copy = pltpu.make_async_remote_copy(
            src_ref=src, dst_ref=dst, send_sem=ssem, recv_sem=rsem, device_id=place, device_id_type=MESH
        )
        copy.start()
        return copy

    def later(k):
        return device(lax.rem(me + k + total, total))

    ops = (x_in, resp_in, ps_in, w_in_in, b_in, w_out_in, home_in, ids_in, cnt_in, par_in)
    refs = (x_ref, resp_ref, ps_ref, w_in_ref, b_ref, w_out_ref, home_ref, ids_ref, cnt_ref, par_ref)
    loads = [pltpu.make_async_copy(a, b, in_sem.at[i]) for i, (a, b) in enumerate(zip(ops, refs))]
    for c in loads:
        c.start()
    barrier = pltpu.get_barrier_semaphore()
    for k in range(1, WIN + 1):
        pl.semaphore_signal(barrier, inc=1, device_id=later(k), device_id_type=MESH)
        pl.semaphore_signal(barrier, inc=1, device_id=later(-k), device_id_type=MESH)
    for k in range(1, GROUP):
        pl.semaphore_signal(barrier, inc=1, device_id=mates[k][1], device_id_type=MESH)
    for k in range(1, DEPTH):
        pl.semaphore_signal(barrier, inc=1, device_id=column[k], device_id_type=MESH)
    pl.semaphore_signal(barrier, inc=1, device_id=(x * 2 + 1 - core, dev), device_id_type=MESH)

    for c in loads:
        c.wait()
    point_slot = ps_ref[...].reshape(1, ROWS)
    win_ref[0, :ROWS, :] = dot(one_hot(point_slot, ROWS, 0), x_ref[...]).astype(BF16)
    resp = jnp.broadcast_to(resp_ref[...].astype(F32).reshape(1, ROWS), (16, ROWS)).astype(BF16)
    win_ref[0, ROWS : ROWS + 16, :] = dot(resp, one_hot(point_slot, B, 0), NT).astype(BF16)
    win_ref[0, ROWS + 16 :, :] = dot(resp, one_hot(point_slot, B, BS), NT).astype(BF16)
    pl.semaphore_wait(barrier, 2 * WIN + GROUP + DEPTH - 1)

    def shift(src, dst, cut, sem, k):
        at = pl.ds(cut.start, cut.stop - cut.start)
        return send(win_ref.at[src, at], win_ref.at[dst, at], f_send.at[sem], f_recv.at[sem], later(k))

    cuts = [slice(0, 96), slice(96, ROWS + 32)]
    two = [shift(0, 2, cut, q, 2) for q, cut in enumerate(cuts)]
    one = shift(0, 1, slice(0, ROWS + 32), 3, 1)

    def forward(d):
        pre, sig, hidden = network(win_ref[d, :ROWS, :], w_in_ref[...], b_ref[...].reshape(1, H), w_out_ref[...])
        hid_ref[d] = hidden
        dsil_ref[d] = sig * (1.0 + pre * (1.0 - sig))
        feats = dot(hidden, w_out_ref[...]).astype(BF16)
        feat_ref[2 * d] = feats[:BS]
        feat_ref[2 * d + 1] = feats[BS:]
        for b in range(BPD):
            wresp_ref[2 * d + b] = win_ref[d, ROWS + 16 * b : ROWS + 16 * (b + 1), :]

    forward(0)

    def const(v):
        return jnp.full((1, 1), v, F32)

    inv_sq = jnp.exp(-2.0 * const(par_ref[0]))
    var = jnp.exp(const(par_ref[1]))
    nug = jnp.exp(const(par_ref[2]))
    eye = eye_of(B)
    lane = lax.broadcasted_iota(jnp.int32, (B, B), 1)
    sub = lax.broadcasted_iota(jnp.int32, (B, B), 0)
    top = B * var + 1.0
    coef = 2.0 / (top + nug)
    delta = (top - nug) / (top + nug)
    scales = []
    for _ in range(STEPS):
        sq = delta * delta
        scales.append(2.0 / (2.0 - sq))
        delta = sq / (2.0 - sq)
    both = range(BPD)
    places = [member_windows(me, home_ref, ids_ref, cnt_ref, s) for s in both]
    three = []
    for q, cut in enumerate(cuts):
        two[q].wait()
        three.append(shift(2, 3, cut, 4 + q, 1))
    forward(2)
    one.wait()
    forward(1)
    for c in three:
        c.wait()
    forward(3)

    rows = [
        kernel_rows(
            s, cnt_ref[s], places[s], feat_ref, wresp_ref, z_ref, e_ref, k_ref, inv_sq, var, nug, eye
        )
        for s in both
    ]
    for s in both:
        for work in rows[s][0]:
            work()
    fill = [work for i in range(1, 4) for s in both for work in rows[s][i]]
    scan = (coef, scales)
    invs, last, fill = eliminate(both, k_ref, eye, scan, fill)
    real = (lane < BS) & (sub < BS)
    resid = [jnp.where((sub == BS) & (lane < BS), m, 0.0) for m in last]
    schur = [jnp.where(real, m, eye) for m in last]
    for s in both:
        mat_ref[s] = schur[s][:BS]
    found = joint_gradients(
        both, invs, schur, resid, scan, fill, z_ref, e_ref, k_ref, var, inv_sq, nug, eye, real
    )
    grads, hypers, quads = [list(part) for part in zip(*found)]
    for w in range((WIN + 1) * BPD):
        acc = grads[w][NMAX * BS : (NMAX + 1) * BS] if w < BPD else jnp.zeros((BS, H), F32)
        for s in both:
            if w == 1 or (w == 0 and s == 0):
                continue
            for k in range(NMAX):
                place, flag = places[s][k]
                acc = acc + jnp.where(place == w, flag, 0.0) * grads[s][k * BS : (k + 1) * BS]
        gw_ref[w] = acc
        if w >= BPD:
            out_buf[w // BPD - 1, (w % BPD) * BS : (w % BPD + 1) * BS, :] = acc.astype(BF16)
    returns = [
        send(out_buf.at[k - 1], in_buf.at[k - 1], g_send.at[k], g_recv.at[k], later(-k))
        for k in range(1, WIN + 1)
    ]

    w_in_part = jnp.zeros((H, 2 * H), F32)
    w_out_part = jnp.zeros((H, 2 * H), F32)
    b_part = jnp.zeros((1, H), F32)
    for d in range(WIN + 1):
        hi, lo = split2(rows_of(gw_ref[2 * d], gw_ref[2 * d + 1]))
        back = dot(hi, w_out_ref[...], NT) + dot(lo, w_out_ref[...], NT)
        dpre = back * dsil_ref[d]
        w_out_part = w_out_part + dot(hid_ref[d], lanes(hi, lo), TN)
        w_in_part = w_in_part + dot(win_ref[d, :ROWS, :], lanes(*split2(dpre)), TN)
        b_part = b_part + jnp.sum(dpre, axis=0, keepdims=True)
    w_in_part = w_in_part[:, :H] + w_in_part[:, H:]
    w_out_part = w_out_part[:, :H] + w_out_part[:, H:]
    row8 = lax.broadcasted_iota(jnp.int32, (8, H), 0)
    row16 = lax.broadcasted_iota(jnp.int32, (CHUNK, H), 0)

    def pack(bias, hyper):
        tile = jnp.zeros((CHUNK, H), F32)
        for i, one_row in enumerate(split2(bias) + split2(hyper)):
            tile = tile + jnp.where(row16 == i, one_row.astype(F32), 0.0)
        return tile.astype(BF16)

    def unpack(tile):
        return tile[0:1] + tile[1:2], tile[2:3] + tile[3:4]

    for s in both:
        log_ref[s] = jnp.where(row8 == 1, quads[s], 0.0)
    small = pack(b_part, hypers[0] + hypers[1])
    w_in_part = w_in_part.astype(BF16)
    w_out_part = w_out_part.astype(BF16)
    for c in range(GROUP):
        src = w_in_part if c < 8 else w_out_part
        part[c, :CHUNK, :] = src[(c % 8) * CHUNK : (c % 8 + 1) * CHUNK]
        part[c, CHUNK:, :] = small
    copies = []
    for k in far:
        other, place = mates[k]
        copies.append(send(part.at[other], part_in.at[ga], s1.at[k], r1.at[k], place))
    part_in[ga] = part[ga]

    @pl.when(dev >= 0)
    def _():
        pivot_steps(mat_ref, log_ref, 0, 32)

    for c in copies:
        c.wait()
    acc = part_in[0].astype(F32)
    for c in range(1, GROUP):
        acc = acc + part_in[c].astype(F32)
    bias, hyper = unpack(acc[CHUNK:])
    pair[core, :CHUNK, :] = acc[:CHUNK]
    pair[core, CHUNK:, :] = jnp.where(row8 == 0, bias, 0.0) + jnp.where(row8 == 1, hyper, 0.0)
    copy = send(pair.at[core], pair.at[core], c_send, c_recv, (x * 2 + 1 - core, dev))
    copy.wait()
    acc = pair[0] + pair[1]
    red_in[z, :CHUNK, :] = acc[:CHUNK].astype(BF16)
    red_in[z, CHUNK:, :] = pack(acc[CHUNK : CHUNK + 1], acc[CHUNK + 1 : CHUNK + 2])
    copies = []
    for k in deep:
        copies.append(send(red_in.at[z], red_in.at[z], s2.at[k], r2.at[k], column[k]))

    @pl.when(dev >= 0)
    def _():
        pivot_steps(mat_ref, log_ref, 32, 64)

    for c in copies:
        c.wait()
    acc = red_in[0].astype(F32)
    for c in range(1, DEPTH):
        acc = acc + red_in[c].astype(F32)
    acc = acc * (1.0 / (total * ROWS))
    mine_ref[...] = acc[:CHUNK].astype(BF16)
    bias, hyper = unpack(acc[CHUNK:])
    bsum_ref[...] = bias.reshape(H)
    place = pl.ds(pl.multiple_of(ga * CHUNK, CHUNK), CHUNK)
    copies = []
    for k in far:
        copies.append(send(mine_ref, gath.at[place], s3.at[k], r3.at[k], mates[k][1]))
    stores = [
        pltpu.make_async_copy(mine_ref, gath.at[place], out_sem.at[0]),
        pltpu.make_async_copy(bsum_ref, b_out, out_sem.at[1]),
        pltpu.make_async_copy(fg_ref, fg_out, out_sem.at[2]),
    ]
    stores[0].start()
    stores[1].start()

    @pl.when(dev >= 0)
    def _():
        pivot_steps(mat_ref, log_ref, 64, BS)
        for s in both:
            ll = -0.5 * (log_ref[s, 0:1, 0:1] + log_ref[s, 1:2, 0:1]) * (1.0 / BS) - 0.5 * LOG_TWO_PI
            ll_ref[s] = jnp.sum(ll)
        for i in range(3):
            hyp_ref[i] = jnp.sum(hyper[:, i : i + 1])

    for c in returns:
        c.wait()
    grad = rows_of(gw_ref[0], gw_ref[1])
    for k in range(WIN):
        grad = grad + in_buf[k].astype(F32)
    perm = one_hot(ps_ref[...].reshape(1, ROWS), ROWS, 0)
    pairs = dot(perm, lanes(*split2(grad)), TN)
    fg_ref[...] = pairs[:, :H] + pairs[:, H:]
    stores[2].start()
    for c in copies + stores:
        c.wait()


def finish_kernel(ll_in, hyp_in, grad_in, weights_in, b_in, ll_out, fg_out, gin_out, b_out, gout_out, hyp_out):
    fg_out[...] = grad_in[...]
    gin_out[...] = weights_in[:H, :].astype(F32)
    gout_out[...] = weights_in[H:, :].astype(F32)
    b_out[...] = b_in[...]
    for s in range(BPD):
        ll_out[s] = ll_in[s]
    for i in range(3):
        hyp_out[i] = hyp_in[i]


VM = pl.BlockSpec(memory_space=pltpu.VMEM)
SM = pl.BlockSpec(memory_space=pltpu.SMEM)
ANY = pl.BlockSpec(memory_space=pl.ANY)
DMA = pltpu.SemaphoreType.DMA


def shards(
    inputs, responses, point_slot, block_home, nbr_ids, nbr_count, w_in, b_in, w_out, kernel_params
):
    loglik, hyper, grad, weights, bias = pl.pallas_call(
        main_kernel,
        out_shape=(
            jax.ShapeDtypeStruct((BPD,), F32),
            jax.ShapeDtypeStruct((3,), F32),
            jax.ShapeDtypeStruct((ROWS, H), F32),
            jax.ShapeDtypeStruct((GROUP * CHUNK, H), BF16),
            jax.ShapeDtypeStruct((H,), F32),
        ),
        in_specs=[ANY] * 10,
        out_specs=(SM, SM, ANY, ANY, ANY),
        scratch_shapes=[
            pltpu.VMEM((ROWS, H), BF16),
            pltpu.VMEM((ROWS,), BF16),
            pltpu.VMEM((ROWS,), jnp.int32),
            pltpu.VMEM((H, H), BF16),
            pltpu.VMEM((H,), F32),
            pltpu.VMEM((H, H), BF16),
            pltpu.SMEM(block_home.shape, jnp.int32),
            pltpu.SMEM((BPD, NMAX), jnp.int32),
            pltpu.SMEM((BPD,), jnp.int32),
            pltpu.SMEM((3,), F32),
            pltpu.VMEM((ROWS, H), F32),
            pltpu.VMEM((CHUNK, H), BF16),
            pltpu.VMEM((H,), F32),
            DMA((10,)),
            DMA((3,)),
            pltpu.VMEM((WIN + 1, ROWS + 32, H), BF16),
            pltpu.VMEM(((WIN + 1) * BPD, 16, H), BF16),
            pltpu.VMEM(((WIN + 1) * BPD, BS, H), BF16),
            pltpu.VMEM((WIN + 1, ROWS, H), BF16),
            pltpu.VMEM((WIN + 1, ROWS, H), F32),
            pltpu.VMEM((BPD, N, H), BF16),
            pltpu.VMEM((BPD, N, N), F32),
            pltpu.VMEM((BPD, N, N), F32),
            pltpu.VMEM(((WIN + 1) * BPD, BS, H), F32),
            pltpu.VMEM((WIN, ROWS, H), BF16),
            pltpu.VMEM((WIN, ROWS, H), BF16),
            pltpu.VMEM((GROUP, 2 * CHUNK, H), BF16),
            pltpu.VMEM((GROUP, 2 * CHUNK, H), BF16),
            pltpu.VMEM((2, CHUNK + 8, H), F32),
            pltpu.VMEM((DEPTH, 2 * CHUNK, H), BF16),
            pltpu.VMEM((BPD, BS, B), F32),
            pltpu.VMEM((BPD, 8, B), F32),
        ]
        + [DMA((8,))] * 2
        + [DMA((WIN + 1,))] * 2
        + [DMA((GROUP,))] * 6
        + [DMA, DMA],
        compiler_params=pltpu.CompilerParams(
            collective_id=0, has_side_effects=True, vmem_limit_bytes=60 * 1024 * 1024
        ),
        name="vecchia_main",
    )(
        inputs, responses, point_slot, w_in, b_in, w_out,
        block_home, nbr_ids, nbr_count, kernel_params,
    )
    loglik, feature_grad, g_in, g_b, g_out, hyper = pl.pallas_call(
        finish_kernel,
        out_shape=(
            jax.ShapeDtypeStruct((BPD,), F32),
            jax.ShapeDtypeStruct((ROWS, H), F32),
            jax.ShapeDtypeStruct((H, H), F32),
            jax.ShapeDtypeStruct((H,), F32),
            jax.ShapeDtypeStruct((H, H), F32),
            jax.ShapeDtypeStruct((3,), F32),
        ),
        in_specs=[SM, SM, VM, VM, VM],
        out_specs=(SM, VM, VM, VM, VM, SM),
        name="vecchia_finish",
    )(loglik, hyper, grad, weights, bias)
    return loglik, feature_grad, g_in, g_b, g_out, hyper


def solution(mesh):
    placed = (
        P(("region", "dev"), None),
        P(("region", "dev")),
        P(("region", "dev")),
        P(),
        P(("region", "dev"), None),
        P(("region", "dev")),
        P(),
        P(),
        P(),
        P(),
    )
    return jax.shard_map(
        shards,
        mesh=mesh,
        in_specs=placed,
        out_specs=(P(("region", "dev")), P(("region", "dev"), None), P(), P(), P(), P()),
        check_vma=False,
    )
```

```python
import math

import jax
import jax.numpy as jnp
from jax import lax
from jax.experimental import pallas as pl
from jax.experimental.pallas import tpu as pltpu
from jax.sharding import PartitionSpec as P

H = 128
BS = 96
BPD = 2
NMAX = 4
WIN = 3
ROWS = BPD * BS
B = 128
N = 4 * B
STEPS = 8
GROUP = 16
CHUNK = 16
DEPTH = 8

SQRT_THREE = math.sqrt(3.0)
LOG_TWO_PI = math.log(2.0 * math.pi)
MESH = pl.DeviceIdType.MESH
F32 = jnp.float32
BF16 = jnp.bfloat16


def dot(a, b, contract=((1,), (0,))):
    return lax.dot_general(a, b, (contract, ((), ())), preferred_element_type=F32)


NT = ((1,), (1,))
TN = ((0,), (0,))


def split2(a):
    hi = a.astype(BF16)
    return hi, (a - hi.astype(F32)).astype(BF16)


def split3(a):
    hi = a.astype(BF16)
    rest = a - hi.astype(F32)
    mid = rest.astype(BF16)
    return hi, mid, (rest - mid.astype(F32)).astype(BF16)


def lanes(*parts):
    return jnp.concatenate(parts, axis=1)


def rows_of(*parts):
    return jnp.concatenate(parts, axis=0)


def mul2(a, b):
    n = (b[0] if isinstance(b, tuple) else b).shape[1]
    pair = lanes(*(b if isinstance(b, tuple) else split2(b)))
    out = dot(lanes(*split2(a)), rows_of(pair, pair))
    return out[:, :n] + out[:, n:]


def mul3(a, b):
    ah, am, al = a if isinstance(a, tuple) else split3(a)
    bh, bm, bl = b if isinstance(b, tuple) else split3(b)
    n = bh.shape[1]
    pair = lanes(bh, bm)
    out = dot(lanes(ah, am), rows_of(pair, pair))
    low = dot(lanes(ah, al), rows_of(bl, bh))
    return out[:, :n] + (out[:, n:] + low)


def mul3_nt(a, b):
    ah, am, al = a
    bh, bm, bl = b
    n = bh.shape[0]
    pair = rows_of(bh, bm)
    out = dot(lanes(ah, am), lanes(pair, pair), NT)
    low = dot(lanes(ah, al), lanes(bl, bh), NT)
    return out[:, :n] + (out[:, n:] + low)


def eye_of(n):
    return (
        lax.broadcasted_iota(jnp.int32, (n, n), 0) == lax.broadcasted_iota(jnp.int32, (n, n), 1)
    ).astype(F32)


def inverses(mats, eye, scan, fill=()):
    coef, scales = scan
    fill = list(fill)
    share = -(-len(fill) // (STEPS - 2)) if fill else 0
    res = [eye - coef * a for a in mats]
    inv = [(scales[0] * coef) * (eye + r) for r in res]
    res = [(1.0 - scales[0]) * eye + scales[0] * mul3(r, r) for r in res]
    for j in range(1, STEPS - 1):
        s = scales[j]
        mul = mul2 if j == STEPS - 2 else mul3
        both = [mul(rows_of(r, x), r) for x, r in zip(inv, res)]
        for work in fill[:share]:
            work()
        fill = fill[share:]
        inv = [s * (x + b[B:]) for x, b in zip(inv, both)]
        res = [(1.0 - s) * eye + s * b[:B] for b in both]
    s = scales[-1]
    return [s * x for x in inv], res


def device(index):
    per = lax.axis_size("dev")
    return (lax.div(index, per), lax.rem(index, per))


def my_index():
    return lax.axis_index("region") * lax.axis_size("dev") + lax.axis_index("dev")


def network(x, w_in, b_in, w_out):
    pre = dot(x, w_in) + b_in
    sig = 1.0 / (1.0 + jnp.exp(-pre))
    hidden = (pre * sig).astype(BF16)
    return pre, sig, hidden


def one_hot(point_slot, rows, first):
    slot = lax.broadcasted_iota(jnp.int32, (rows, ROWS), 0) + first
    return (slot == point_slot).astype(F32).astype(BF16)


def block(ref, s, a, b):
    return ref[s, a * B : (a + 1) * B, b * B : (b + 1) * B]


def member_windows(me, home_ref, ids_ref, cnt_ref, s):
    places = []
    for k in range(NMAX):
        slot = home_ref[ids_ref[s, k]]
        live = k < cnt_ref[s]
        w = jnp.where(live, (me - slot // BPD) * BPD + slot % BPD, 0)
        places.append((jnp.clip(w, 0, (WIN + 1) * BPD - 1), jnp.where(live, 1.0, 0.0)))
    return places


def kernel_rows(s, count, places, feat_ref, resp_ref, z_ref, e_ref, k_ref, inv_sq, var, nug, eye):
    lane1 = lax.broadcasted_iota(jnp.int32, (1, B), 1)
    y_row = jnp.zeros((1, N), F32)
    for k, (w, flag) in enumerate(places + [(s, None)]):
        member = feat_ref[w]
        resp = jnp.where(lane1 < BS, resp_ref[w][0:1].astype(F32), 0.0)
        if flag is not None:
            member = (member.astype(F32) * flag).astype(BF16)
            resp = resp * flag
        z_ref[s, k * BS : (k + 1) * BS, :] = member
        resp = lanes(resp, jnp.zeros((1, N - B), F32))
        y_row = y_row + (pltpu.roll(resp, k * BS, 1) if k else resp)
    z_ref[s, (NMAX + 1) * BS :, :] = jnp.zeros((N - (NMAX + 1) * BS, H), BF16)
    z = z_ref[s]
    gram = dot(z, z, NT)
    e_ref[s] = gram
    diag = [jnp.where(eye > 0.0, gram[i * B : (i + 1) * B, i * B : (i + 1) * B], 0.0) for i in range(4)]
    sq_row = lanes(*[jnp.sum(d, axis=0, keepdims=True) for d in diag])
    sq_col = [jnp.sum(d, axis=1, keepdims=True) for d in diag]
    col_id = lax.broadcasted_iota(jnp.int32, (1, N), 1)
    own = (col_id >= NMAX * BS) & (col_id < (NMAX + 1) * BS)
    v_row = jnp.where((col_id < count * BS) | own, 1.0, 0.0)

    def piece(i, c):
        part = slice(c, c + 32)
        out = slice(i * B + c, i * B + c + 32)
        row_id = lax.broadcasted_iota(jnp.int32, (32, 1), 0) + (i * B + c)
        own = (row_id >= NMAX * BS) & (row_id < (NMAX + 1) * BS)
        v_col = jnp.where((row_id < count * BS) | own, 1.0, 0.0)
        d2 = jnp.maximum(sq_col[i][part] + sq_row - 2.0 * e_ref[s, out, :], 0.0)
        r2 = d2 * inv_sq + 1e-06
        rad = SQRT_THREE * (r2 * lax.rsqrt(r2))
        e = jnp.exp(-rad) * (v_col * v_row)
        e_ref[s, out, :] = e
        wide = (i + 1) * B
        kern = var * (1.0 + rad[:, :wide]) * e[:, :wide]
        spot = kern[:, i * B :] + eye[part] * (nug * v_col + 1.0 - v_col)
        k_ref[s, out, :wide] = lanes(kern[:, : i * B], spot) if i else spot
        if i == 3 and c == BS:
            k_ref[s, 3 * B + BS : 3 * B + BS + 1, :] = y_row

    return [[lambda i=i, c=c: piece(i, c) for c in range(0, B, 32)] for i in range(4)]


def eliminate(both, k_ref, eye, scan, fill):
    invs = []
    for i in range(3):
        lo = (i + 1) * B
        cols = slice(i * B, lo)
        x, r = inverses([block(k_ref, s, i, i) for s in both], eye, scan, fill)
        fill = []
        below = [split3(k_ref[s, lo:, cols]) for s in both]
        panel = [mul3(below[s], x[s]) for s in both]
        panel = [split3(panel[s] + mul2(panel[s], r[s])) for s in both]
        invs.append([split3(x[s] + mul2(x[s], r[s])) for s in both])
        for b in range(i + 1, 4):
            first = (b - i - 1) * B
            for s in both:
                at = slice(b * B, (b + 1) * B)
                k_ref[s, b * B :, at] = k_ref[s, b * B :, at] - mul3_nt(
                    tuple(p[first:] for p in panel[s]), tuple(p[first : first + B] for p in below[s])
                )
    return invs, [block(k_ref, s, 3, 3) for s in both], []


def joint_gradients(both, invs, schur, resid, scan, fill, z_ref, e_ref, k_ref, var, inv_sq, nug, eye, real):
    sub = lax.broadcasted_iota(jnp.int32, (B, B), 0)
    lane = lax.broadcasted_iota(jnp.int32, (B, B), 1)
    lane1 = lax.broadcasted_iota(jnp.int32, (1, B), 1)
    sign = jnp.where(lax.broadcasted_iota(jnp.int32, (B, 1), 0) < BS, -1.0, 1.0)
    p3, p2, t1, x1, ys, w_pair = {}, {}, {}, {}, {}, {}

    def back(s, step):
        if step == 0:
            p3[s] = split3(mul3(block(k_ref, s, 3, 2), invs[2][s]))
        elif step == 1:
            p2[s] = block(k_ref, s, 3, 1) - mul3(p3[s], block(k_ref, s, 2, 1))
            t1[s] = block(k_ref, s, 3, 0) - mul3(p3[s], block(k_ref, s, 2, 0))
        elif step == 2:
            p2[s] = split3(mul3(p2[s], invs[1][s]))
        elif step == 3:
            t1[s] = t1[s] - mul3(p2[s], block(k_ref, s, 1, 0))
        elif step == 4:
            x1[s] = mul3(t1[s], invs[0][s])
        else:
            x2, x3 = [p[0].astype(F32) + (p[1].astype(F32) + p[2].astype(F32)) for p in (p2[s], p3[s])]
            ys[s] = lanes(x1[s] * sign, x2 * sign, x3 * sign)
            w = rows_of(*[ys[s][:, i * B : (i + 1) * B].T for i in range(3)])
            w_pair[s] = lanes(*split2(w))

    own = jnp.where(real, eye, 0.0)
    steps = [lambda s=s, step=step: back(s, step) for step in range(6) for s in both]
    x, r = inverses(schur, eye, scan, fill + steps)
    beta_m = [mul3(resid[s], x[s]) for s in both]
    beta_m = [beta_m[s] + mul2(beta_m[s], r[s]) for s in both]
    s_inv = [x[s] + mul2(x[s], r[s]) for s in both]
    y_parts = [split2(lanes(ys[s], own)) for s in both]
    beta_row = [m[BS : BS + 1] for m in beta_m]
    beta_col = [jnp.sum(eye * b, axis=1, keepdims=True) for b in beta_row]
    mid = [
        jnp.where(real, beta_col[s] * beta_row[s] - s_inv[s], 0.0)
        + beta_m[s]
        + jnp.where((lane == BS) & (sub < BS), beta_col[s], 0.0)
        for s in both
    ]
    prod = [mul2(mid[s], y_parts[s]) for s in both]
    pairs = [lanes(*split2(p)) for p in prod]
    g = [dot(w_pair[s], rows_of(pairs[s], pairs[s])) for s in both]
    below = lax.broadcasted_iota(jnp.int32, (B, 1), 0) < BS
    low = [jnp.where(below, prod[s], 0.0) for s in both]
    weights = [
        split2(rows_of((g[s][:, :N] + g[s][:, N:]) * e_ref[s, : 3 * B, :], low[s] * e_ref[s, 3 * B :, :]))
        for s in both
    ]
    rhs = [lanes(z_ref[s], jnp.ones((N, H), BF16)) for s in both]
    pz = [dot(weights[s][0], rhs[s]) + dot(weights[s][1], rhs[s]) for s in both]
    out = []
    for s in both:
        quad = jnp.sum(jnp.sum(resid[s] * beta_m[s], axis=0, keepdims=True), axis=1, keepdims=True)
        y = lanes(ys[s], own)
        trace = jnp.sum(jnp.sum(prod[s] * y, axis=0, keepdims=True), axis=1, keepdims=True)
        t2 = 0.5 * nug * trace
        t1 = 0.5 * quad - 0.5 * BS - t2
        zf = z_ref[s].astype(F32)
        grad = (3.0 * var * inv_sq) * (pz[s][:, :H] - pz[s][:, H:] * zf)
        t0 = -jnp.sum(jnp.sum(grad * zf, axis=0, keepdims=True), axis=1, keepdims=True)
        hyper = jnp.where(lane1 == 0, t0, 0.0) + jnp.where(lane1 == 1, t1, 0.0)
        out.append((grad, hyper + jnp.where(lane1 == 2, t2, 0.0), quad))
    return out


def pivot_steps(mat_ref, log_ref, first, last):
    mats = [mat_ref[i, first:BS, :] for i in range(BPD)]
    logdets = [log_ref[i, 0:1, 0:1] for i in range(BPD)]
    for k in range(first, last):
        for i, mat in enumerate(mats):
            at = k - (BS - mat.shape[0])
            row = mat[at : at + 1]
            pivot = row[:, k : k + 1]
            logdets[i] = logdets[i] + jnp.log(pivot)
            if k < BS - 1:
                if (k + 1) % 8 == 0:
                    mat = mat[8:]
                mats[i] = mat - mat[:, k : k + 1] * (row / pivot)
    for i in range(BPD):
        log_ref[i, 0:1, :] = jnp.broadcast_to(logdets[i], (1, B))
        if last < BS:
            mat_ref[i, last:BS, :] = mats[i]


def main_kernel(
    x_in, resp_in, ps_in, w_in_in, b_in, w_out_in, home_in, ids_in, cnt_in, par_in,
    ll_out, hyp_out, fg_out, gath, b_out,
    x_ref, resp_ref, ps_ref, w_in_ref, b_ref, w_out_ref, home_ref, ids_ref, cnt_ref, par_ref,
    ll_ref, hyp_ref, fg_ref, mine_ref, bsum_ref, in_sem, out_sem,
    win_ref, wresp_ref, feat_ref, hid_ref, dsil_ref, z_ref, e_ref, k_ref, gw_ref,
    out_buf, in_buf, part, part_in, pair, red_in, mat_ref, log_ref,
    f_send, f_recv, g_send, g_recv, s1, r1, s2, r2, s3, r3, c_send, c_recv,
):
    total = lax.axis_size("region") * lax.axis_size("dev")
    region, dev = lax.axis_index("region"), lax.axis_index("dev")
    me = my_index()
    x, core = lax.div(region, 2), lax.rem(region, 2)
    y, z = lax.div(dev, DEPTH), lax.rem(dev, DEPTH)
    ga = x * 4 + y

    xs = [x] + [lax.rem(x + k, 4) for k in range(1, 4)]
    ys = [y] + [lax.rem(y + k, 4) for k in range(1, 4)]
    mates = [
        (xs[k // 4] * 4 + ys[k % 4], (xs[k // 4] * 2 + core, ys[k % 4] * DEPTH + z)) for k in range(GROUP)
    ]
    far = sorted(range(1, GROUP), key=lambda k: -(min(k // 4, 4 - k // 4) + min(k % 4, 4 - k % 4)))
    deep = sorted(range(1, DEPTH), key=lambda k: -min(k, DEPTH - k))
    column = [(region, y * DEPTH + lax.rem(z + k, DEPTH)) for k in range(DEPTH)]

    def send(src, dst, ssem, rsem, place):
        copy = pltpu.make_async_remote_copy(
            src_ref=src, dst_ref=dst, send_sem=ssem, recv_sem=rsem, device_id=place, device_id_type=MESH
        )
        copy.start()
        return copy

    def later(k):
        return device(lax.rem(me + k + total, total))

    ops = (x_in, resp_in, ps_in, w_in_in, b_in, w_out_in, home_in, ids_in, cnt_in, par_in)
    refs = (x_ref, resp_ref, ps_ref, w_in_ref, b_ref, w_out_ref, home_ref, ids_ref, cnt_ref, par_ref)
    loads = [pltpu.make_async_copy(a, b, in_sem.at[i]) for i, (a, b) in enumerate(zip(ops, refs))]
    for c in loads:
        c.start()
    barrier = pltpu.get_barrier_semaphore()
    for k in range(1, WIN + 1):
        pl.semaphore_signal(barrier, inc=1, device_id=later(k), device_id_type=MESH)
        pl.semaphore_signal(barrier, inc=1, device_id=later(-k), device_id_type=MESH)
    for k in range(1, GROUP):
        pl.semaphore_signal(barrier, inc=1, device_id=mates[k][1], device_id_type=MESH)
    for k in range(1, DEPTH):
        pl.semaphore_signal(barrier, inc=1, device_id=column[k], device_id_type=MESH)
    pl.semaphore_signal(barrier, inc=1, device_id=(x * 2 + 1 - core, dev), device_id_type=MESH)

    for c in loads:
        c.wait()
    point_slot = ps_ref[...].reshape(1, ROWS)
    win_ref[0, :ROWS, :] = dot(one_hot(point_slot, ROWS, 0), x_ref[...]).astype(BF16)
    resp = jnp.broadcast_to(resp_ref[...].astype(F32).reshape(1, ROWS), (16, ROWS)).astype(BF16)
    win_ref[0, ROWS : ROWS + 16, :] = dot(resp, one_hot(point_slot, B, 0), NT).astype(BF16)
    win_ref[0, ROWS + 16 :, :] = dot(resp, one_hot(point_slot, B, BS), NT).astype(BF16)
    pl.semaphore_wait(barrier, 2 * WIN + GROUP + DEPTH - 1)

    def shift(src, dst, cut, sem, k):
        at = pl.ds(cut.start, cut.stop - cut.start)
        return send(win_ref.at[src, at], win_ref.at[dst, at], f_send.at[sem], f_recv.at[sem], later(k))

    cuts = [slice(0, 96), slice(96, ROWS + 32)]
    two = [shift(0, 2, cut, q, 2) for q, cut in enumerate(cuts)]
    one = shift(0, 1, slice(0, ROWS + 32), 3, 1)

    def forward(d):
        pre, sig, hidden = network(win_ref[d, :ROWS, :], w_in_ref[...], b_ref[...].reshape(1, H), w_out_ref[...])
        hid_ref[d] = hidden
        dsil_ref[d] = sig * (1.0 + pre * (1.0 - sig))
        feats = dot(hidden, w_out_ref[...]).astype(BF16)
        feat_ref[2 * d] = feats[:BS]
        feat_ref[2 * d + 1] = feats[BS:]
        for b in range(BPD):
            wresp_ref[2 * d + b] = win_ref[d, ROWS + 16 * b : ROWS + 16 * (b + 1), :]

    forward(0)

    def const(v):
        return jnp.full((1, 1), v, F32)

    inv_sq = jnp.exp(-2.0 * const(par_ref[0]))
    var = jnp.exp(const(par_ref[1]))
    nug = jnp.exp(const(par_ref[2]))
    eye = eye_of(B)
    lane = lax.broadcasted_iota(jnp.int32, (B, B), 1)
    sub = lax.broadcasted_iota(jnp.int32, (B, B), 0)
    top = B * var + 1.0
    coef = 2.0 / (top + nug)
    delta = (top - nug) / (top + nug)
    scales = []
    for _ in range(STEPS):
        sq = delta * delta
        scales.append(2.0 / (2.0 - sq))
        delta = sq / (2.0 - sq)
    both = range(BPD)
    places = [member_windows(me, home_ref, ids_ref, cnt_ref, s) for s in both]
    three = []
    for q, cut in enumerate(cuts):
        two[q].wait()
        three.append(shift(2, 3, cut, 4 + q, 1))
    forward(2)
    one.wait()
    forward(1)
    for c in three:
        c.wait()
    forward(3)

    rows = [
        kernel_rows(
            s, cnt_ref[s], places[s], feat_ref, wresp_ref, z_ref, e_ref, k_ref, inv_sq, var, nug, eye
        )
        for s in both
    ]
    for s in both:
        for work in rows[s][0]:
            work()
    fill = [work for i in range(1, 4) for s in both for work in rows[s][i]]
    scan = (coef, scales)
    invs, last, fill = eliminate(both, k_ref, eye, scan, fill)
    real = (lane < BS) & (sub < BS)
    resid = [jnp.where((sub == BS) & (lane < BS), m, 0.0) for m in last]
    schur = [jnp.where(real, m, eye) for m in last]
    for s in both:
        mat_ref[s] = schur[s][:BS]
    found = joint_gradients(
        both, invs, schur, resid, scan, fill, z_ref, e_ref, k_ref, var, inv_sq, nug, eye, real
    )
    grads, hypers, quads = [list(part) for part in zip(*found)]
    for w in range((WIN + 1) * BPD):
        acc = grads[w][NMAX * BS : (NMAX + 1) * BS] if w < BPD else jnp.zeros((BS, H), F32)
        for s in both:
            if w == 1 or (w == 0 and s == 0):
                continue
            for k in range(NMAX):
                place, flag = places[s][k]
                acc = acc + jnp.where(place == w, flag, 0.0) * grads[s][k * BS : (k + 1) * BS]
        gw_ref[w] = acc
        if w >= BPD:
            out_buf[w // BPD - 1, (w % BPD) * BS : (w % BPD + 1) * BS, :] = acc.astype(BF16)
    returns = [
        send(out_buf.at[k - 1], in_buf.at[k - 1], g_send.at[k], g_recv.at[k], later(-k))
        for k in range(1, WIN + 1)
    ]

    w_in_part = jnp.zeros((H, 2 * H), F32)
    w_out_part = jnp.zeros((H, 2 * H), F32)
    b_part = jnp.zeros((1, H), F32)
    for d in range(WIN + 1):
        hi, lo = split2(rows_of(gw_ref[2 * d], gw_ref[2 * d + 1]))
        back = dot(hi, w_out_ref[...], NT) + dot(lo, w_out_ref[...], NT)
        dpre = back * dsil_ref[d]
        w_out_part = w_out_part + dot(hid_ref[d], lanes(hi, lo), TN)
        w_in_part = w_in_part + dot(win_ref[d, :ROWS, :], lanes(*split2(dpre)), TN)
        b_part = b_part + jnp.sum(dpre, axis=0, keepdims=True)
    w_in_part = w_in_part[:, :H] + w_in_part[:, H:]
    w_out_part = w_out_part[:, :H] + w_out_part[:, H:]
    row8 = lax.broadcasted_iota(jnp.int32, (8, H), 0)
    row16 = lax.broadcasted_iota(jnp.int32, (CHUNK, H), 0)

    def pack(bias, hyper):
        tile = jnp.zeros((CHUNK, H), F32)
        for i, one_row in enumerate(split2(bias) + split2(hyper)):
            tile = tile + jnp.where(row16 == i, one_row.astype(F32), 0.0)
        return tile.astype(BF16)

    def unpack(tile):
        return tile[0:1] + tile[1:2], tile[2:3] + tile[3:4]

    for s in both:
        log_ref[s] = jnp.where(row8 == 1, quads[s], 0.0)
    small = pack(b_part, hypers[0] + hypers[1])
    w_in_part = w_in_part.astype(BF16)
    w_out_part = w_out_part.astype(BF16)
    for c in range(GROUP):
        src = w_in_part if c < 8 else w_out_part
        part[c, :CHUNK, :] = src[(c % 8) * CHUNK : (c % 8 + 1) * CHUNK]
        part[c, CHUNK:, :] = small
    copies = []
    for k in far:
        other, place = mates[k]
        copies.append(send(part.at[other], part_in.at[ga], s1.at[k], r1.at[k], place))
    part_in[ga] = part[ga]

    @pl.when(dev >= 0)
    def _():
        pivot_steps(mat_ref, log_ref, 0, 32)

    for c in copies:
        c.wait()
    acc = part_in[0].astype(F32)
    for c in range(1, GROUP):
        acc = acc + part_in[c].astype(F32)
    bias, hyper = unpack(acc[CHUNK:])
    pair[core, :CHUNK, :] = acc[:CHUNK]
    pair[core, CHUNK:, :] = jnp.where(row8 == 0, bias, 0.0) + jnp.where(row8 == 1, hyper, 0.0)
    copy = send(pair.at[core], pair.at[core], c_send, c_recv, (x * 2 + 1 - core, dev))
    copy.wait()
    acc = pair[0] + pair[1]
    red_in[z, :CHUNK, :] = acc[:CHUNK].astype(BF16)
    red_in[z, CHUNK:, :] = pack(acc[CHUNK : CHUNK + 1], acc[CHUNK + 1 : CHUNK + 2])
    copies = []
    for k in deep:
        copies.append(send(red_in.at[z], red_in.at[z], s2.at[k], r2.at[k], column[k]))

    @pl.when(dev >= 0)
    def _():
        pivot_steps(mat_ref, log_ref, 32, 64)

    for c in copies:
        c.wait()
    acc = red_in[0].astype(F32)
    for c in range(1, DEPTH):
        acc = acc + red_in[c].astype(F32)
    acc = acc * (1.0 / (total * ROWS))
    mine_ref[...] = acc[:CHUNK].astype(BF16)
    bias, hyper = unpack(acc[CHUNK:])
    bsum_ref[...] = bias.reshape(H)
    place = pl.ds(pl.multiple_of(ga * CHUNK, CHUNK), CHUNK)
    copies = []
    for k in far:
        copies.append(send(mine_ref, gath.at[place], s3.at[k], r3.at[k], mates[k][1]))
    stores = [
        pltpu.make_async_copy(mine_ref, gath.at[place], out_sem.at[0]),
        pltpu.make_async_copy(bsum_ref, b_out, out_sem.at[1]),
        pltpu.make_async_copy(fg_ref, fg_out, out_sem.at[2]),
        pltpu.make_async_copy(ll_ref, ll_out, out_sem.at[3]),
        pltpu.make_async_copy(hyp_ref, hyp_out, out_sem.at[4]),
    ]
    stores[0].start()
    stores[1].start()

    @pl.when(dev >= 0)
    def _():
        pivot_steps(mat_ref, log_ref, 64, BS)
        for s in both:
            ll = -0.5 * (log_ref[s, 0:1, 0:1] + log_ref[s, 1:2, 0:1]) * (1.0 / BS) - 0.5 * LOG_TWO_PI
            ll_ref[s] = jnp.sum(ll)
        for i in range(3):
            hyp_ref[i] = jnp.sum(hyper[:, i : i + 1])

    for c in returns:
        c.wait()
    grad = rows_of(gw_ref[0], gw_ref[1])
    for k in range(WIN):
        grad = grad + in_buf[k].astype(F32)
    perm = one_hot(ps_ref[...].reshape(1, ROWS), ROWS, 0)
    pairs = dot(perm, lanes(*split2(grad)), TN)
    fg_ref[...] = pairs[:, :H] + pairs[:, H:]
    for c in stores[2:]:
        c.start()
    for c in copies + stores:
        c.wait()


def finish_kernel(ll_in, hyp_in, grad_in, weights_in, b_in, ll_out, fg_out, gin_out, b_out, gout_out, hyp_out):
    fg_out[...] = grad_in[...]
    gin_out[...] = weights_in[:H, :].astype(F32)
    gout_out[...] = weights_in[H:, :].astype(F32)
    b_out[...] = b_in[...]
    for s in range(BPD):
        ll_out[s] = ll_in[s]
    for i in range(3):
        hyp_out[i] = hyp_in[i]


VM = pl.BlockSpec(memory_space=pltpu.VMEM)
SM = pl.BlockSpec(memory_space=pltpu.SMEM)
ANY = pl.BlockSpec(memory_space=pl.ANY)
DMA = pltpu.SemaphoreType.DMA


def shards(
    inputs, responses, point_slot, block_home, nbr_ids, nbr_count, w_in, b_in, w_out, kernel_params
):
    loglik, hyper, grad, weights, bias = pl.pallas_call(
        main_kernel,
        out_shape=(
            jax.ShapeDtypeStruct((BPD,), F32),
            jax.ShapeDtypeStruct((3,), F32),
            jax.ShapeDtypeStruct((ROWS, H), F32),
            jax.ShapeDtypeStruct((GROUP * CHUNK, H), BF16),
            jax.ShapeDtypeStruct((H,), F32),
        ),
        in_specs=[ANY] * 10,
        out_specs=(ANY,) * 5,
        scratch_shapes=[
            pltpu.VMEM((ROWS, H), BF16),
            pltpu.VMEM((ROWS,), BF16),
            pltpu.VMEM((ROWS,), jnp.int32),
            pltpu.VMEM((H, H), BF16),
            pltpu.VMEM((H,), F32),
            pltpu.VMEM((H, H), BF16),
            pltpu.SMEM(block_home.shape, jnp.int32),
            pltpu.SMEM((BPD, NMAX), jnp.int32),
            pltpu.SMEM((BPD,), jnp.int32),
            pltpu.SMEM((3,), F32),
            pltpu.SMEM((BPD,), F32),
            pltpu.SMEM((3,), F32),
            pltpu.VMEM((ROWS, H), F32),
            pltpu.VMEM((CHUNK, H), BF16),
            pltpu.VMEM((H,), F32),
            DMA((10,)),
            DMA((5,)),
            pltpu.VMEM((WIN + 1, ROWS + 32, H), BF16),
            pltpu.VMEM(((WIN + 1) * BPD, 16, H), BF16),
            pltpu.VMEM(((WIN + 1) * BPD, BS, H), BF16),
            pltpu.VMEM((WIN + 1, ROWS, H), BF16),
            pltpu.VMEM((WIN + 1, ROWS, H), F32),
            pltpu.VMEM((BPD, N, H), BF16),
            pltpu.VMEM((BPD, N, N), F32),
            pltpu.VMEM((BPD, N, N), F32),
            pltpu.VMEM(((WIN + 1) * BPD, BS, H), F32),
            pltpu.VMEM((WIN, ROWS, H), BF16),
            pltpu.VMEM((WIN, ROWS, H), BF16),
            pltpu.VMEM((GROUP, 2 * CHUNK, H), BF16),
            pltpu.VMEM((GROUP, 2 * CHUNK, H), BF16),
            pltpu.VMEM((2, CHUNK + 8, H), F32),
            pltpu.VMEM((DEPTH, 2 * CHUNK, H), BF16),
            pltpu.VMEM((BPD, BS, B), F32),
            pltpu.VMEM((BPD, 8, B), F32),
        ]
        + [DMA((8,))] * 2
        + [DMA((WIN + 1,))] * 2
        + [DMA((GROUP,))] * 6
        + [DMA, DMA],
        compiler_params=pltpu.CompilerParams(
            collective_id=0, has_side_effects=True, vmem_limit_bytes=60 * 1024 * 1024
        ),
        name="vecchia_main",
    )(
        inputs, responses, point_slot, w_in, b_in, w_out,
        block_home, nbr_ids, nbr_count, kernel_params,
    )
    loglik, feature_grad, g_in, g_b, g_out, hyper = pl.pallas_call(
        finish_kernel,
        out_shape=(
            jax.ShapeDtypeStruct((BPD,), F32),
            jax.ShapeDtypeStruct((ROWS, H), F32),
            jax.ShapeDtypeStruct((H, H), F32),
            jax.ShapeDtypeStruct((H,), F32),
            jax.ShapeDtypeStruct((H, H), F32),
            jax.ShapeDtypeStruct((3,), F32),
        ),
        in_specs=[SM, SM, VM, VM, VM],
        out_specs=(SM, VM, VM, VM, VM, SM),
        name="vecchia_finish",
    )(loglik, hyper, grad, weights, bias)
    return loglik, feature_grad, g_in, g_b, g_out, hyper


def solution(mesh):
    placed = (
        P(("region", "dev"), None),
        P(("region", "dev")),
        P(("region", "dev")),
        P(),
        P(("region", "dev"), None),
        P(("region", "dev")),
        P(),
        P(),
        P(),
        P(),
    )
    return jax.shard_map(
        shards,
        mesh=mesh,
        in_specs=placed,
        out_specs=(P(("region", "dev")), P(("region", "dev"), None), P(), P(), P(), P()),
        check_vma=False,
    )
```
